128 devices in a mesh: win: 4 (over y_lo, core), blk: 32 (over y_hi, z, x).
Axes of the slice: x: 4, y: 4 (y_hi: 2, y_lo: 2; y = y_hi * 2 + y_lo), z: 4, core: 2. Of those that a mesh axis runs over, the one named last changes fastest.
Arguments:
- hidden_in: bfloat16 [4, 8192, 1920], P('win', 'blk'), may hold values from -6 to 6
- cond_codes: int32 [4, 2048], P('win', 'blk'), may hold values from 0 to 2047
- level_ids: int32 [4], P('win'), may hold values from 0 to 1, as said below
- qkv_weight: bfloat16 [1920, 1440], P(('win', 'blk')), may hold values from -0.125 to 0.125
- attn_out_weight: bfloat16 [480, 1920], P(None, ('win', 'blk')), may hold values from -1 to 1
- mlp_in_weight: bfloat16 [1920, 1920], P(('win', 'blk')), may hold values from -0.125 to 0.125
- mlp_out_weight: bfloat16 [1920, 1920], P(('win', 'blk')), may hold values from -0.125 to 0.125
- code_table: bfloat16 [2048, 1920], P(('win', 'blk')), may hold values from -6 to 6
- level_table: bfloat16 [2, 1920], P(None, ('win', 'blk')), may hold values from -6 to 6
- norm_gain: bfloat16 [2, 1920], P(None, ('win', 'blk')), may hold values from 0.5 to 2
- norm_bias: bfloat16 [2, 1920], P(None, ('win', 'blk')), may hold values from -0.5 to 0.5
- grad_out: bfloat16 [4, 8192, 1920], P('win', 'blk'), may hold values from -6 to 6
Outputs:
- block_out: bfloat16 [4, 8192, 1920], P('win', 'blk')
- grad_in: float32 [4, 8192, 1920], P('win', 'blk')
- grad_qkv: float32 [1920, 1440], P(('win', 'blk'))
- grad_attn_out: float32 [480, 1920], P(None, ('win', 'blk'))
- grad_mlp_in: float32 [1920, 1920], P(('win', 'blk'))
- grad_mlp_out: float32 [1920, 1920], P(('win', 'blk'))
- grad_codes: float32 [2048, 1920], P(('win', 'blk'))
- grad_levels: float32 [2, 1920], P(None, ('win', 'blk'))
- grad_gain: float32 [2, 1920], P(None, ('win', 'blk'))
- grad_bias: float32 [2, 1920], P(None, ('win', 'blk'))
The draws below stay inside these ranges and needn't reach their ends.
Inputs may be any that keep to these rules, and one draw needn't show every extreme that they name: `level_ids`: each level is the level of 2 windows.
All inputs are finite; a program needn't handle non-finite values.
Results may differ from the reference program's by a relative error of at most 0.0092.
Values may be sent and summed in bfloat16 or wider, within the bound.
No kernel may reach another device: no remote copies, remote signals or barrier semaphores. Data moves between devices by JAX's collectives and lax.ppermute only.
A program may use at most 192 MiB of HBM per device.

```python
import math
import jax
import jax.numpy as jnp
from jax import lax

D = 1920
HEADS = 1
HEAD = 480
FF = 1920
VOCAB = 2048
BLOCK = 128
RATIO = 4
LEVELS = 2
ATT = 480
BLOCKS = 64
WIN_LEN = 8192
CODES = 2048
WINDOWS = 4


def draw_level_ids(key, part):
    key = jax.random.fold_in(key, 7)
    ordering = jax.random.permutation(key, WINDOWS)
    return (ordering % LEVELS).astype(jnp.int32)


def place_ends(array, stream_key, smallest, top_value):
    longest = array.shape.index(max(array.shape))
    spots = []
    for shift in (0, 1):
        where = [jax.random.randint(jax.random.fold_in(stream_key, axis), (), 0, length) for axis, length in enumerate(array.shape)]
        where[longest] = (where[longest] + shift) % array.shape[longest]
        spots.append(tuple(where))
    return array.at[spots[0]].set(smallest).at[spots[1]].set(top_value)


def block_levels(key, dims, pieces, low, largest):
    def one(dim, shards_of):
        heights = jax.random.uniform(jax.random.fold_in(jax.random.fold_in(key, 6), dim), (shards_of,), jnp.float32, low / len(pieces), largest / len(pieces))
        return jnp.repeat(jnp.exp(heights), dims[dim] // shards_of).reshape((-1,) + (1,) * (len(dims) - dim - 1))

    level = one(*pieces[0])
    for cut in pieces[1:]:
        level = level * one(*cut)
    return level


def scatter_about(key, dims, spread, most, shards=(), dtype=jnp.bfloat16):
    loudness = block_levels(key, dims, shards, -0.22, 0.18) if shards else 1.0
    values = jax.random.normal(key, dims, jnp.float32) * spread * loudness
    return jnp.minimum(jnp.maximum(values, -most), most).astype(dtype)


def setup_inputs(seed: int = 0) -> dict:
    seeds = jax.random.split(jax.random.key(seed), 13)
    hidden_in = scatter_about(seeds[0], (WINDOWS, WIN_LEN, D), 1.0, 6.0, ((0, 4), (1, 32)))
    cond_codes = place_ends(jax.random.randint(seeds[1], (WINDOWS, CODES), 0, VOCAB), jax.random.fold_in(seeds[1], 1), 0, VOCAB - 1).astype(jnp.int32)
    level_ids = draw_level_ids(jax.random.fold_in(seeds[12], 71), 0)
    qkv_weight = scatter_about(seeds[3], (D, 3 * ATT), D ** -0.5, 0.125, ((0, 128),))
    attn_out_weight = scatter_about(seeds[4], (ATT, D), (ATT // 16) ** -0.5, 1.0, ((1, 128),))
    mlp_in_weight = scatter_about(seeds[5], (D, FF), D ** -0.5, 0.125, ((0, 128),))
    mlp_out_weight = scatter_about(seeds[6], (FF, D), FF ** -0.5, 0.125, ((0, 128),))
    code_table = scatter_about(seeds[7], (VOCAB, D), 1.0, 6.0, ((0, 128),))
    level_table = scatter_about(seeds[8], (LEVELS, D), 1.0, 6.0, ((1, 128),))
    norm_gain = jnp.clip(jnp.exp(math.log(2.0) - 1.3862944 * jax.random.uniform(seeds[9], (2, D), jnp.float32) ** block_levels(seeds[9], (2, D), ((1, 128),), -0.2, 0.2)), 0.5, 2.0).astype(jnp.bfloat16)
    norm_bias = jnp.clip(jax.random.uniform(seeds[10], (2, D), jnp.float32, -0.5, 0.5) * block_levels(seeds[10], (2, D), ((1, 128),), -0.4, 0.0), -0.5, 0.5).astype(jnp.bfloat16)
    grad_out = scatter_about(seeds[11], (WINDOWS, WIN_LEN, D), 1.0, 6.0, ((0, 4), (1, 32)))
    return {"hidden_in": hidden_in, "cond_codes": cond_codes, "level_ids": level_ids, "qkv_weight": qkv_weight, "attn_out_weight": attn_out_weight, "mlp_in_weight": mlp_in_weight, "mlp_out_weight": mlp_out_weight, "code_table": code_table, "level_table": level_table, "norm_gain": norm_gain, "norm_bias": norm_bias, "grad_out": grad_out}


highest = lax.Precision.HIGHEST
epsilon = 1e-05

@jax.custom_vjp
def low(v):
    return lax.optimization_barrier(v.astype(jnp.bfloat16)).astype(jnp.float32)

@jax.custom_vjp
def low_back(v):
    return v

def low_keep(v):
    return (low(v), None)

def low_pass(kept, grad):
    return (grad,)

def back_keep(v):
    return (v, None)

def back_low(kept, grad):
    return (low(grad),)
low.defvjp(low_keep, low_pass)
low_back.defvjp(back_keep, back_low)

def layer_norm(stream, gain, shift):
    average = lax.optimization_barrier(jnp.mean(stream, axis=-1, keepdims=True))
    centered = stream - average
    variance = lax.optimization_barrier(jnp.mean(centered * centered, axis=-1, keepdims=True))
    return centered * lax.rsqrt(variance + epsilon) * gain + shift

def window_forward(params, hidden, codes_here, level_here):
    qkv_weight, attn_out_weight, mlp_in_weight, mlp_out_weight, code_table, level_table, norm_gain, norm_bias = params
    embedded = jnp.repeat(code_table[codes_here], RATIO, axis=0)
    stream = hidden + embedded + level_table[level_here][None, :]
    normed_first = low(layer_norm(stream, norm_gain[0], norm_bias[0]))
    packed = low(low_back(jnp.dot(normed_first, qkv_weight, precision=highest)))
    head_parts = packed.reshape(BLOCKS, BLOCK, 3, HEADS, HEAD)
    query_part = head_parts[:, :, 0]
    key_part = head_parts[:, :, 1]
    value_part = head_parts[:, :, 2]
    scores = low_back(jnp.einsum('ichd,jchd->chij', query_part, key_part, precision=highest) * HEAD ** (-0.5))
    causal = jnp.arange(BLOCKS)[:, None] >= jnp.arange(BLOCKS)[None, :]
    scores = jnp.where(causal, scores, -1e+30)
    probs = jax.nn.softmax(scores, axis=-1)
    mixed = low(low_back(jnp.einsum('chij,jchd->ichd', low(probs), value_part, precision=highest)))
    mixed = mixed.reshape(WIN_LEN, HEADS * HEAD)
    stream_mid = stream + low_back(jnp.dot(mixed, attn_out_weight, precision=highest))
    normed_second = low(layer_norm(stream_mid, norm_gain[1], norm_bias[1]))
    upward = low_back(jnp.dot(normed_second, mlp_in_weight, precision=highest))
    active = low(jax.nn.gelu(upward, approximate=True))
    return stream_mid + low_back(jnp.dot(active, mlp_out_weight, precision=highest))

def reference(hidden_in, cond_codes, level_ids, qkv_weight, attn_out_weight, mlp_in_weight, mlp_out_weight, code_table, level_table, norm_gain, norm_bias, grad_out):
    params = tuple((weight_in.astype(jnp.float32) for weight_in in (qkv_weight, attn_out_weight, mlp_in_weight, mlp_out_weight, code_table, level_table, norm_gain, norm_bias)))

    def window_step(totals, window_items):
        hidden, codes_here, level_here, cotangent = window_items

        def forward(params_in, hidden_here):
            return window_forward(params_in, hidden_here, codes_here, level_here)
        produced, pullback = jax.vjp(forward, params, hidden.astype(jnp.float32))
        grad_params, grad_hidden = pullback(cotangent.astype(jnp.float32))
        totals = jax.tree.map(jnp.add, totals, grad_params)
        return (totals, (produced.astype(jnp.bfloat16), grad_hidden))
    initial = jax.tree.map(jnp.zeros_like, params)
    totals, (block_out, grad_in) = lax.scan(window_step, initial, (hidden_in, cond_codes, level_ids, grad_out))
    return (block_out, grad_in, totals[0], totals[1], totals[2], totals[3], totals[4], totals[5], totals[6], totals[7])
```

```python
import jax
import jax.numpy as jnp
from jax import lax
from jax.sharding import Mesh, PartitionSpec as P

HEAD = 480
BLOCK = 128
RATIO = 4
D = 1920
SHARDS = 128
ROWS = 16
PART = 640
epsilon = 1e-05
bf16 = jnp.bfloat16
f32 = jnp.float32
AXES = ("yl", "co", "yh", "z", "x")
WIN = ("yl", "co")
BLK = ("yh", "z", "x")
STEP_BITS = {"x": (1, 3), "z": (4, 12), "y": (64, 80)}
CORE_BIT = 32
ORDERS = (("x", "z", "y"), ("z", "y", "x"), ("y", "x", "z"))
RANK = {"y": 0, "z": 1, "x": 2}


def exchange(value, axis, step):
    pairs = []
    for device in range(SHARDS):
        core = (device >> 5) & 1
        pairs.append((device, device ^ STEP_BITS[axis][step ^ core]))
    return lax.ppermute(value, AXES, pairs)


def swap_cores(value):
    return lax.ppermute(value, AXES, [(i, i ^ CORE_BIT) for i in range(SHARDS)])


def bit_place(done, axis, step):
    return sum(1 for other in done if (RANK[other[0]], -other[1]) < (RANK[axis], -step))


def gather_steps(buf, order, done, steps):
    for axis, step in steps:
        place = bit_place(done, axis, step)
        buf = jnp.stack((buf, exchange(buf, axis, step)), axis=place)
        done = done + ((axis, step),)
    return buf, done


def all_steps(order):
    return [(axis, step) for axis in order for step in (0, 1)]


def scatter_steps(buf, done, steps):
    for axis, step in steps:
        done = tuple(d for d in done if d != (axis, step))
        place = bit_place(done, axis, step)
        kept = lax.index_in_dim(buf, 0, place, keepdims=False)
        sent = lax.index_in_dim(buf, 1, place, keepdims=False)
        got = exchange(sent, axis, step)
        buf = (kept.astype(f32) + got.astype(f32)).astype(bf16)
    return buf, done


def layer_norm(stream, gain, shift):
    average = jnp.mean(stream, axis=-1, keepdims=True)
    centered = stream - average
    variance = jnp.mean(centered * centered, axis=-1, keepdims=True)
    return centered * lax.rsqrt(variance + epsilon) * gain + shift


def rows_dot(left, right):
    return lax.dot_general(left, right, (((0,), (0,)), ((), ())), preferred_element_type=f32)


def cols_dot(left, right):
    return lax.dot_general(left, right, (((1,), (1,)), ((), ())), preferred_element_type=f32)


def dot(left, right):
    return jnp.dot(left, right, preferred_element_type=f32)


def attention_mask():
    row = jnp.arange(256)
    block = (row // 8) * 2 + (row // 4) % 2
    column = row % 4
    return (column[:, None] == column[None, :]) & (block[:, None] >= block[None, :])


def rel_shards(yl, co, yh, z, x, core):
    place = jnp.arange(64)
    first = jnp.where(core == 0, 1, 3)
    second = jnp.where(core == 0, 3, 1)

    def offset(high, low):
        return ((place >> low) & 1) * first ^ ((place >> high) & 1) * second

    along_y = offset(5, 4) ^ (yh * 2 + yl)
    along_z = offset(3, 2) ^ z
    along_x = offset(1, 0) ^ x
    return (along_y & 1) * 64 + core * 32 + (along_y >> 1) * 16 + along_z * 4 + along_x


def body(
    hidden_in,
    cond_codes,
    level_ids,
    qkv_weight,
    attn_out_weight,
    mlp_in_weight,
    mlp_out_weight,
    code_table,
    level_table,
    norm_gain,
    norm_bias,
    grad_out,
):
    yl, co, yh, z, x = (lax.axis_index(name) for name in AXES)
    vectors = jnp.concatenate((norm_gain, norm_bias, level_table), axis=0).reshape(1, 90)
    shard0 = jnp.concatenate(
        (
            jnp.concatenate((qkv_weight, attn_out_weight.T), axis=1),
            jnp.pad(vectors, ((0, 0), (0, D - 90))),
        ),
        axis=0,
    )
    shard1 = jnp.pad(mlp_in_weight, ((0, 1), (0, 0)))
    shard2 = jnp.pad(mlp_out_weight, ((0, 1), (0, 0)))
    shards = (shard0, code_table, shard1, shard2)
    early, late = [], []
    for part, order in enumerate(ORDERS):
        cut = slice(part * PART, (part + 1) * PART)
        buf = jnp.concatenate([s[:, cut] for s in shards], axis=1)
        steps = all_steps(order)
        buf, done = gather_steps(buf, order, (), steps[:4])
        first, _ = gather_steps(buf[..., : 2 * PART], order, done, steps[4:])
        second, _ = gather_steps(buf[..., 2 * PART :], order, done, steps[4:])
        early.append(first)
        late.append(second)

    def assemble(bufs, index):
        cut = slice(index * PART, (index + 1) * PART)
        own = jnp.concatenate([b[0][..., cut].reshape(1024, PART) for b in bufs], axis=1)
        other = jnp.concatenate([b[1][..., cut].reshape(1024, PART) for b in bufs], axis=1)
        return jnp.concatenate((own, other), axis=0)

    early = [(b, swap_cores(b)) for b in early]
    late = [(b, swap_cores(b)) for b in late]
    full0, table = assemble(early, 0), assemble(early, 1)
    expand, reduce = assemble(late, 0), assemble(late, 1)

    shard_of = jnp.concatenate(
        (rel_shards(yl, co, yh, z, x, co), rel_shards(yl, co, yh, z, x, 1 - co))
    )
    feature = jnp.arange(D)
    place_feature = (shard_of[:, None] * 15 + jnp.arange(ROWS)[None, :]).reshape(-1)
    place_feature = jnp.where(jnp.arange(SHARDS * ROWS) % ROWS < 15, place_feature, -1)
    shuffle = (feature[:, None] == place_feature[None, :]).astype(bf16)
    shard_hot = (shard_of[:, None] == feature[None, :] // 15).astype(bf16)
    vector_mask = (jnp.arange(90)[:, None] % 15) == (feature[None, :] % 15)
    place_code = (shard_of[:, None] * 16 + jnp.arange(ROWS)[None, :]).reshape(-1)
    codes = jnp.repeat(cond_codes[0], RATIO)
    code_hot = (codes[:, None] == place_code[None, :]).astype(bf16)

    small = full0.reshape(SHARDS, ROWS, D)[:, 15, :90]
    spread = jnp.where(vector_mask, rows_dot(small, shard_hot), 0.0)
    spread = jnp.sum(spread.reshape(6, 15, D), axis=1)
    gains, shifts, levels = spread[0:2], spread[2:4], spread[4:6]
    chosen = jnp.arange(2) == level_ids[0]
    level_row = jnp.sum(jnp.where(chosen[:, None], levels, 0.0), axis=0)

    hidden = hidden_in[0].astype(f32)
    stream = hidden + dot(code_hot, table) + level_row[None, :]
    normed_first = layer_norm(stream, gains[0], shifts[0]).astype(bf16)
    first_shuffled = dot(normed_first, shuffle).astype(bf16)
    packed = dot(first_shuffled, full0[:, :1440]).astype(bf16)

    token = jnp.arange(256)
    moved = (token // 4 % 2) * 128 + (token // 8) * 4 + token % 4
    row_move = (moved[:, None] == token[None, :]).astype(bf16)

    def to_columns(value):
        value = dot(row_move, value).astype(bf16)
        return lax.all_to_all(value, BLK, split_axis=0, concat_axis=0, tiled=True)

    def to_tokens(value):
        value = lax.all_to_all(value, BLK, split_axis=0, concat_axis=0, tiled=True)
        return rows_dot(row_move, value).astype(bf16)

    columns = to_columns(packed)
    query, key, value = columns[:, :480], columns[:, 480:960], columns[:, 960:]
    mask = attention_mask()

    scores = jnp.where(mask, cols_dot(query, key) * HEAD ** (-0.5), -1e30)
    row_top = jnp.max(scores, axis=-1, keepdims=True)
    log_total = row_top + jnp.log(jnp.sum(jnp.exp(scores - row_top), axis=-1, keepdims=True))
    probs = jnp.exp(scores - log_total)
    probs_low = probs.astype(bf16)
    mixed = to_tokens(dot(probs_low, value).astype(bf16))

    attn_rows = dot(shuffle, full0[:, 1440:]).astype(bf16)
    stream_mid = stream + cols_dot(mixed, attn_rows)
    normed_second = layer_norm(stream_mid, gains[1], shifts[1]).astype(bf16)
    second_shuffled = dot(normed_second, shuffle).astype(bf16)
    upward = dot(second_shuffled, expand)
    active, gelu_pull = jax.vjp(lambda pre: jax.nn.gelu(pre, approximate=True), upward)
    active = active.astype(bf16)
    active_shuffled = dot(active, shuffle).astype(bf16)
    block_out = (stream_mid + dot(active_shuffled, reduce)).astype(bf16)

    upstream = grad_out[0]
    grad_reduce = rows_dot(active_shuffled, upstream).astype(bf16)
    d_active = cols_dot(cols_dot(upstream, reduce).astype(bf16), shuffle)
    d_upward = gelu_pull(d_active)[0].astype(bf16)
    grad_expand = rows_dot(second_shuffled, d_upward).astype(bf16)
    d_second = cols_dot(cols_dot(d_upward, expand).astype(bf16), shuffle)
    _, second_pull = jax.vjp(layer_norm, stream_mid, gains[1], shifts[1])
    d_mid_part, d_gain_second, d_shift_second = second_pull(d_second)
    d_stream_mid = upstream.astype(f32) + d_mid_part
    d_attn = d_stream_mid.astype(bf16)
    attn_shuffled = dot(d_attn, shuffle).astype(bf16)
    grad_attn = rows_dot(attn_shuffled, mixed).astype(bf16)
    d_mixed = to_columns(dot(d_attn, attn_rows).astype(bf16))

    def scatter_parts(arrays, count):
        bufs = []
        for part, order in enumerate(ORDERS):
            cut = slice(part * PART, (part + 1) * PART)
            kept = jnp.concatenate([a[:1024, cut] for a in arrays], axis=1)
            sent = jnp.concatenate([a[1024:, cut] for a in arrays], axis=1)
            buf = (kept.astype(f32) + swap_cores(sent).astype(f32)).astype(bf16)
            buf = buf.reshape(2, 2, 2, 2, 2, 2, ROWS, len(arrays) * PART)
            steps = all_steps(order)
            buf, done = scatter_steps(buf, tuple(steps), steps[::-1][:count])
            bufs.append((buf, done, steps[::-1][count:]))
        return bufs

    sums_early = scatter_parts((grad_expand, grad_reduce), 2)

    d_values = rows_dot(probs_low, d_mixed)
    d_probs = cols_dot(d_mixed, value)
    d_scores = (
        probs * (d_probs - jnp.sum(probs * d_probs, axis=-1, keepdims=True))
    ).astype(bf16)
    d_queries = dot(d_scores, key) * HEAD ** (-0.5)
    d_keys = rows_dot(d_scores, query) * HEAD ** (-0.5)
    d_packed = to_tokens(jnp.concatenate((d_queries, d_keys, d_values), axis=1).astype(bf16))

    grad_qkv = rows_dot(first_shuffled, d_packed).astype(bf16)
    d_first = cols_dot(cols_dot(d_packed, full0[:, :1440]).astype(bf16), shuffle)
    _, first_pull = jax.vjp(layer_norm, stream, gains[0], shifts[0])
    d_stream_part, d_gain_first, d_shift_first = first_pull(d_first)
    d_stream = d_stream_mid + d_stream_part
    grad_table = rows_dot(code_hot, d_stream.astype(bf16)).astype(bf16)

    d_level = jnp.where(chosen[:, None], jnp.sum(d_stream, axis=0)[None, :], 0.0)
    totals = jnp.concatenate(
        (
            jnp.stack((d_gain_first, d_gain_second, d_shift_first, d_shift_second)),
            d_level,
        ),
        axis=0,
    )
    totals = jnp.where(vector_mask, jnp.repeat(totals, 15, axis=0), 0.0).astype(bf16)
    small = cols_dot(shard_hot, totals).astype(bf16)
    small = jnp.pad(small[:, None, :], ((0, 0), (15, 0), (0, D - 90)))
    grad0 = jnp.concatenate((grad_qkv, grad_attn), axis=1) + small.reshape(SHARDS * ROWS, D)

    sums_late = scatter_parts((grad0, grad_table), 2)
    ends = []
    for (a, done, steps), (b, _, _) in zip(sums_late, sums_early):
        buf, _ = scatter_steps(jnp.concatenate((a, b), axis=-1), done, steps)
        ends.append(buf.astype(f32))
    out0, out3, out1, out2 = (
        jnp.concatenate([e[:, i * PART : (i + 1) * PART] for e in ends], axis=1) for i in range(4)
    )
    small = out0[15, :90].reshape(6, 15)
    return (
        block_out[None],
        d_stream[None],
        out0[:15, :1440],
        out0[:15, 1440:].T,
        out1[:15],
        out2[:15],
        out3,
        small[4:6],
        small[0:2],
        small[2:4],
    )


def solution(mesh):
    fine = Mesh(mesh.devices.reshape(2, 2, 2, 4, 4), AXES)
    return jax.shard_map(
        body,
        mesh=fine,
        in_specs=(
            P(WIN, BLK, None),
            P(WIN, BLK),
            P(WIN),
            P(AXES, None),
            P(None, AXES),
            P(AXES, None),
            P(AXES, None),
            P(AXES, None),
            P(None, AXES),
            P(None, AXES),
            P(None, AXES),
            P(WIN, BLK, None),
        ),
        out_specs=(
            P(WIN, BLK, None),
            P(WIN, BLK, None),
            P(AXES, None),
            P(None, AXES),
            P(AXES, None),
            P(AXES, None),
            P(AXES, None),
            P(None, AXES),
            P(None, AXES),
            P(None, AXES),
        ),
        check_vma=False,
    )
```

```python
import jax
import jax.numpy as jnp
from jax import lax
from jax.sharding import Mesh, PartitionSpec as P

HEAD = 480
BLOCK = 128
RATIO = 4
D = 1920
SHARDS = 128
ROWS = 16
HALVES = (slice(0, 1024), slice(1024, 2048))
epsilon = 1e-05
bf16 = jnp.bfloat16
f32 = jnp.float32
AXES = ("yl", "co", "yh", "z", "x")
WIN = ("yl", "co")
BLK = ("yh", "z", "x")
STEP_BITS = {"x": (1, 3), "z": (4, 12), "y": (64, 80)}
CORE_BIT = 32
ORDERS = (("x", "z", "y"), ("z", "y", "x"), ("y", "x", "z"))


def exchange(value, order, step):
    masks = STEP_BITS[order[step // 2]]
    pairs = [(i, i ^ masks[(step % 2) ^ ((i >> 5) & 1)]) for i in range(SHARDS)]
    return lax.ppermute(value, AXES, pairs)


def swap_cores(value):
    return lax.ppermute(value, AXES, [(i, i ^ CORE_BIT) for i in range(SHARDS)])


def gather_small(buf, order):
    for step in range(4):
        buf = jnp.concatenate((buf, exchange(buf, order, step)), axis=0)
    return buf


def gather_large(buf, order):
    half = jnp.concatenate((buf, exchange(buf, order, 4)), axis=0)
    rest = exchange(half, order, 5)
    return half, rest, swap_cores(half), swap_cores(rest)


def add_halves(kept, got):
    rows = kept.shape[0] // 2
    return tuple(
        (kept[cut].astype(f32) + got[cut].astype(f32)).astype(bf16)
        for cut in (slice(0, rows), slice(rows, 2 * rows))
    )


def scatter_large(own, other, order):
    kept, sent = add_halves(own, swap_cores(other))
    kept, sent = add_halves(kept, exchange(sent, order, 5))
    return add_halves(kept, exchange(sent, order, 4))


def scatter_small(kept, sent, order):
    for step in (3, 2, 1):
        kept, sent = add_halves(kept, exchange(sent, order, step))
    return kept.astype(f32) + exchange(sent, order, 0).astype(f32)


def shards_of(me, order):
    place = jnp.arange(64)

    def held(device):
        core = (device >> 5) & 1
        shard = device
        for step in range(6):
            masks = STEP_BITS[order[step // 2]]
            mask = jnp.where(core == step % 2, masks[0], masks[1])
            shard = shard ^ (((place >> step) & 1) * mask)
        return shard

    return jnp.concatenate((held(me), held(me ^ CORE_BIT)))


def layer_norm(stream, gain, shift):
    average = jnp.mean(stream, axis=-1, keepdims=True)
    centered = stream - average
    variance = jnp.mean(centered * centered, axis=-1, keepdims=True)
    return centered * lax.rsqrt(variance + epsilon) * gain + shift


def rows_dot(left, right):
    return lax.dot_general(left, right, (((0,), (0,)), ((), ())), preferred_element_type=f32)


def cols_dot(left, right):
    return lax.dot_general(left, right, (((1,), (1,)), ((), ())), preferred_element_type=f32)


def dot(left, right):
    return jnp.dot(left, right, preferred_element_type=f32)


def attention_mask():
    row = jnp.arange(256)
    block = (row // 8) * 2 + (row // 4) % 2
    column = row % 4
    return (column[:, None] == column[None, :]) & (block[:, None] >= block[None, :])


def k_dot(left, pieces):
    return sum(dot(left[:, 512 * k : 512 * k + 512], piece) for k, piece in enumerate(pieces))


def n_dot(left, pieces):
    return jnp.concatenate([cols_dot(left, piece).astype(bf16) for piece in pieces], axis=1)


def body(
    hidden_in,
    cond_codes,
    level_ids,
    qkv_weight,
    attn_out_weight,
    mlp_in_weight,
    mlp_out_weight,
    code_table,
    level_table,
    norm_gain,
    norm_bias,
    grad_out,
):
    yl, co, yh, z, x = (lax.axis_index(name) for name in AXES)
    vectors = jnp.concatenate((norm_gain, norm_bias, level_table), axis=0).reshape(1, 90)
    shard0 = jnp.concatenate(
        (
            jnp.concatenate((qkv_weight, attn_out_weight.T), axis=1),
            jnp.pad(vectors, ((0, 0), (0, D - 90))),
        ),
        axis=0,
    )
    shard1 = jnp.pad(mlp_in_weight, ((0, 1), (0, 0)))
    shard2 = jnp.pad(mlp_out_weight, ((0, 1), (0, 0)))
    shards = (shard0, code_table, shard1, shard2)
    me = yl * 64 + co * 32 + yh * 16 + z * 4 + x
    own = (
        gather_small(shard0, ORDERS[0]),
        gather_small(jnp.concatenate((code_table[:, :1024], shard1), axis=1), ORDERS[1]),
        gather_small(jnp.concatenate((code_table[:, 1024:], shard2), axis=1), ORDERS[2]),
    )
    qkv, table_a, table_b = (
        gather_large(buf[:, :cut], order) for buf, cut, order in zip(own, (1440, 1024, 896), ORDERS)
    )
    attn, expand, reduce = (
        gather_large(buf[:, cut:], order) for buf, cut, order in zip(own, (1440, 1024, 896), ORDERS)
    )

    shard_sets = [shards_of(me, order) for order in ORDERS]
    feature = jnp.arange(D)
    in_chunk = jnp.arange(ROWS)

    def shuffle_of(shards):
        target = jnp.where(in_chunk[None, :] < 15, shards[:, None] * 15 + in_chunk[None, :], -1)
        return (feature[:, None] == target.reshape(1, -1)).astype(bf16)

    shuffle0, shuffle1, shuffle2 = (shuffle_of(s) for s in shard_sets)
    shard_hot = (shard_sets[0][:, None] == feature[None, :] // 15).astype(bf16)
    vector_mask = (jnp.arange(90)[:, None] % 15) == (feature[None, :] % 15)
    codes = jnp.repeat(cond_codes[0], RATIO)

    def code_hot_of(shards):
        target = (shards[:, None] * 16 + in_chunk[None, :]).reshape(1, -1)
        return (codes[:, None] == target).astype(bf16)

    hot_a, hot_b = code_hot_of(shard_sets[1]), code_hot_of(shard_sets[2])

    small = jnp.concatenate([q.reshape(32, ROWS, 1440)[:, 15, :90] for q in qkv], axis=0)
    spread = jnp.where(vector_mask, rows_dot(small, shard_hot), 0.0)
    spread = jnp.sum(spread.reshape(6, 15, D), axis=1)
    gains, shifts, levels = spread[0:2], spread[2:4], spread[4:6]
    chosen = jnp.arange(2) == level_ids[0]
    level_row = jnp.sum(jnp.where(chosen[:, None], levels, 0.0), axis=0)

    hidden = hidden_in[0].astype(f32)
    stream = hidden + jnp.concatenate((k_dot(hot_a, table_a), k_dot(hot_b, table_b)), axis=1) + level_row[None, :]
    normed_first = layer_norm(stream, gains[0], shifts[0]).astype(bf16)
    first_shuffled = dot(normed_first, shuffle0).astype(bf16)
    packed = k_dot(first_shuffled, qkv).astype(bf16)

    token = jnp.arange(256)
    moved = (token // 4 % 2) * 128 + (token // 8) * 4 + token % 4
    row_move = (moved[:, None] == token[None, :]).astype(bf16)

    def to_columns(value):
        value = dot(row_move, value).astype(bf16)
        return lax.all_to_all(value, BLK, split_axis=0, concat_axis=0, tiled=True)

    def to_tokens(value):
        value = lax.all_to_all(value, BLK, split_axis=0, concat_axis=0, tiled=True)
        return rows_dot(row_move, value).astype(bf16)

    columns = to_columns(packed)
    query, key, value = columns[:, :480], columns[:, 480:960], columns[:, 960:]
    mask = attention_mask()

    scores = jnp.where(mask, cols_dot(query, key) * HEAD ** (-0.5), -1e30)
    row_top = jnp.max(scores, axis=-1, keepdims=True)
    log_total = row_top + jnp.log(jnp.sum(jnp.exp(scores - row_top), axis=-1, keepdims=True))
    probs = jnp.exp(scores - log_total)
    probs_low = probs.astype(bf16)
    mixed = to_tokens(dot(probs_low, value).astype(bf16))

    attn_rows = dot(shuffle0, jnp.concatenate(attn, axis=0)).astype(bf16)
    stream_mid = stream + cols_dot(mixed, attn_rows)
    normed_second = layer_norm(stream_mid, gains[1], shifts[1]).astype(bf16)
    second_shuffled = dot(normed_second, shuffle1).astype(bf16)
    upward = k_dot(second_shuffled, expand)
    active, gelu_pull = jax.vjp(lambda pre: jax.nn.gelu(pre, approximate=True), upward)
    active = active.astype(bf16)
    active_shuffled = dot(active, shuffle2).astype(bf16)
    block_out = (stream_mid + k_dot(active_shuffled, reduce)).astype(bf16)

    upstream = grad_out[0]
    grad_reduce = tuple(rows_dot(active_shuffled[:, cut], upstream).astype(bf16) for cut in HALVES)
    d_active = cols_dot(n_dot(upstream, reduce), shuffle2)
    d_upward = gelu_pull(d_active)[0].astype(bf16)
    grad_expand = tuple(rows_dot(second_shuffled[:, cut], d_upward).astype(bf16) for cut in HALVES)
    d_second = cols_dot(n_dot(d_upward, expand), shuffle1)
    _, second_pull = jax.vjp(layer_norm, stream_mid, gains[1], shifts[1])
    d_mid_part, d_gain_second, d_shift_second = second_pull(d_second)
    d_stream_mid = upstream.astype(f32) + d_mid_part
    d_attn = d_stream_mid.astype(bf16)
    attn_shuffled = dot(d_attn, shuffle0).astype(bf16)
    grad_attn = tuple(rows_dot(attn_shuffled[:, cut], mixed).astype(bf16) for cut in HALVES)
    d_mixed = to_columns(dot(d_attn, attn_rows).astype(bf16))

    sums_early = [
        scatter_large(own, other, order)
        for (own, other), order in zip((grad_attn, grad_expand, grad_reduce), ORDERS)
    ]

    d_values = rows_dot(probs_low, d_mixed)
    d_probs = cols_dot(d_mixed, value)
    d_scores = (
        probs * (d_probs - jnp.sum(probs * d_probs, axis=-1, keepdims=True))
    ).astype(bf16)
    d_queries = dot(d_scores, key) * HEAD ** (-0.5)
    d_keys = rows_dot(d_scores, query) * HEAD ** (-0.5)
    d_packed = to_tokens(jnp.concatenate((d_queries, d_keys, d_values), axis=1).astype(bf16))

    grad_qkv = tuple(rows_dot(first_shuffled[:, cut], d_packed).astype(bf16) for cut in HALVES)
    d_first = cols_dot(n_dot(d_packed, qkv), shuffle0)
    _, first_pull = jax.vjp(layer_norm, stream, gains[0], shifts[0])
    d_stream_part, d_gain_first, d_shift_first = first_pull(d_first)
    d_stream = d_stream_mid + d_stream_part
    d_low = d_stream.astype(bf16)
    grad_table_a = tuple(rows_dot(hot_a[:, cut], d_low[:, :1024]).astype(bf16) for cut in HALVES)
    grad_table_b = tuple(rows_dot(hot_b[:, cut], d_low[:, 1024:]).astype(bf16) for cut in HALVES)

    d_level = jnp.where(chosen[:, None], jnp.sum(d_stream, axis=0)[None, :], 0.0)
    totals = jnp.concatenate(
        (
            jnp.stack((d_gain_first, d_gain_second, d_shift_first, d_shift_second)),
            d_level,
        ),
        axis=0,
    )
    totals = jnp.where(vector_mask, jnp.repeat(totals, 15, axis=0), 0.0).astype(bf16)
    small = cols_dot(shard_hot, totals).astype(bf16)
    small = jnp.pad(small[:, None, :], ((0, 0), (15, 0), (0, 1440 - 90))).reshape(2048, 1440)
    grad_qkv = tuple(g + small[cut] for g, cut in zip(grad_qkv, HALVES))
    sums_late = [
        scatter_large(own, other, order)
        for (own, other), order in zip((grad_qkv, grad_table_a, grad_table_b), ORDERS)
    ]
    ends = []
    for late, early, order in zip(sums_late, sums_early, ORDERS):
        kept, sent = (jnp.concatenate(pair, axis=1) for pair in zip(late, early))
        ends.append(scatter_small(kept, sent, order))
    out0, out1, out2 = ends[0], ends[1][:, 1024:], ends[2][:, 896:]
    out3 = jnp.concatenate((ends[1][:, :1024], ends[2][:, :896]), axis=1)
    small = out0[15, :90].reshape(6, 15)
    return (
        block_out[None],
        d_stream[None],
        out0[:15, :1440],
        out0[:15, 1440:].T,
        out1[:15],
        out2[:15],
        out3,
        small[4:6],
        small[0:2],
        small[2:4],
    )


def solution(mesh):
    fine = Mesh(mesh.devices.reshape(2, 2, 2, 4, 4), AXES)
    return jax.shard_map(
        body,
        mesh=fine,
        in_specs=(
            P(WIN, BLK, None),
            P(WIN, BLK),
            P(WIN),
            P(AXES, None),
            P(None, AXES),
            P(AXES, None),
            P(AXES, None),
            P(AXES, None),
            P(None, AXES),
            P(None, AXES),
            P(None, AXES),
            P(WIN, BLK, None),
        ),
        out_specs=(
            P(WIN, BLK, None),
            P(WIN, BLK, None),
            P(AXES, None),
            P(None, AXES),
            P(AXES, None),
            P(AXES, None),
            P(AXES, None),
            P(None, AXES),
            P(None, AXES),
            P(None, AXES),
        ),
        check_vma=False,
    )
```

```python
import functools

import jax
import jax.numpy as jnp
import numpy as np
from jax import lax
from jax.experimental import pallas as pl
from jax.experimental.pallas import tpu as pltpu
from jax.sharding import Mesh, PartitionSpec as P

HEAD = 480
BLOCK = 128
RATIO = 4
D = 1920
SHARDS = 128
ROWS = 16
HALF = 1024
HALVES = (slice(0, HALF), slice(HALF, 2 * HALF))
SPLITS = (512, 1024, 896)
epsilon = 1e-05
bf16 = jnp.bfloat16
f32 = jnp.float32
AXES = ("yl", "co", "yh", "z", "x")
WIN = ("yl", "co")
BLK = ("yh", "z", "x")
STEP_BITS = {"x": (1, 3), "z": (4, 12), "y": (64, 80)}
CORE_BIT = 32
ORDERS = (("x", "z", "y"), ("z", "y", "x"), ("y", "x", "z"))


def exchange(value, order, step):
    masks = STEP_BITS[order[step // 2]]
    pairs = [(i, i ^ masks[(step % 2) ^ ((i >> 5) & 1)]) for i in range(SHARDS)]
    return lax.ppermute(value, AXES, pairs)


def swap_cores(value):
    return lax.ppermute(value, AXES, [(i, i ^ CORE_BIT) for i in range(SHARDS)])


def call(kernel, out_shape, **options):
    params = pltpu.CompilerParams(vmem_limit_bytes=options.pop("vmem", 32 * 2**20))
    return pl.pallas_call(kernel, out_shape=out_shape, compiler_params=params, **options)


def join_kernel(cuts, *refs):
    sources, targets, sem = refs[:2], refs[2:-1], refs[-1]
    rows = sources[0].shape[0]
    copies = []
    for i, source in enumerate(sources):
        for j, (target, (start, stop)) in enumerate(zip(targets, cuts)):
            copies.append(
                pltpu.make_async_copy(
                    source.at[:, start:stop],
                    target.at[i * rows : (i + 1) * rows],
                    sem.at[i * len(cuts) + j],
                )
            )
    for copy in copies:
        copy.start()
    for copy in copies:
        copy.wait()


def join(first, second, cuts=None):
    rows, columns = first.shape
    cuts = cuts or ((0, columns),)
    out = call(
        functools.partial(join_kernel, cuts),
        tuple(jax.ShapeDtypeStruct((2 * rows, stop - start), bf16) for start, stop in cuts),
        in_specs=[pl.BlockSpec(memory_space=pl.ANY)] * 2,
        out_specs=tuple(pl.BlockSpec(memory_space=pl.ANY) for _ in cuts),
        scratch_shapes=[pltpu.SemaphoreType.DMA((2 * len(cuts),))],
    )(first, second)
    return out if len(cuts) > 1 else out[0]


def gather_small(buf, order, split):
    for step in range(3):
        buf = join(buf, exchange(buf, order, step))
    return join(buf, exchange(buf, order, 3), ((0, split), (split, buf.shape[1])))


def gather_large(buf, order):
    half = join(buf, exchange(buf, order, 4))
    rest = exchange(half, order, 5)
    return half, rest, swap_cores(half), swap_cores(rest)


def add_kernel(kept_low, kept_high, got_low, got_high, kept, sent):
    kept[...] = (kept_low[...].astype(f32) + got_low[...].astype(f32)).astype(bf16)
    sent[...] = (kept_high[...].astype(f32) + got_high[...].astype(f32)).astype(bf16)


def add_halves(kept, got):
    rows, columns = kept.shape[0] // 2, kept.shape[1]
    tiles = max(rows // 64, 1)
    tile = rows // tiles
    low = pl.BlockSpec((tile, columns), lambda i: (i, 0))
    high = pl.BlockSpec((tile, columns), lambda i: (i + tiles, 0))
    half = jax.ShapeDtypeStruct((rows, columns), bf16)
    return call(
        add_kernel, (half, half), grid=(tiles,), in_specs=[low, high, low, high], out_specs=(low, low)
    )(kept, kept, got, got)


def scatter_small(kept, sent, order):
    for step in (3, 2, 1):
        kept, sent = add_halves(kept, exchange(sent, order, step))
    return kept.astype(f32) + exchange(sent, order, 0).astype(f32)


def outer_kernel(tiles, left, left_got, right, right_got, kept, sent):
    rows = HALF // 2 // tiles
    columns = right.shape[1]
    step = pl.program_id(0)
    for target, base in ((kept, 0), (sent, HALF // 2)):
        start = pl.multiple_of(base + step * rows, rows)
        one, two = left[:, pl.ds(start, rows)], left_got[:, pl.ds(start, rows)]
        for cut in range(0, columns, 512):
            span = slice(cut, min(cut + 512, columns))
            total = rows_dot(one, right[:, span]) + rows_dot(two, right_got[:, span])
            target[:, span] = total.astype(bf16)


def outer(left, left_got, right, right_got):
    tiles = 4
    columns = right.shape[1]
    whole = lambda v: pl.BlockSpec(v.shape, lambda i: (0, 0))
    half = jax.ShapeDtypeStruct((HALF // 2, columns), bf16)
    tile = pl.BlockSpec((HALF // 2 // tiles, columns), lambda i: (i, 0))
    return call(
        functools.partial(outer_kernel, tiles),
        (half, half),
        grid=(tiles,),
        in_specs=[whole(v) for v in (left, left_got, right, right_got)],
        out_specs=(tile, tile),
    )(left, left_got, right, right_got)


def shard_tables():
    table = np.zeros((2, 3, SHARDS), np.int32)
    for core in range(2):
        for number, order in enumerate(ORDERS):
            for place in range(SHARDS):
                here = core ^ (place >> 6)
                mask = (place >> 6) * CORE_BIT
                for step in range(6):
                    if (place >> step) & 1:
                        mask ^= STEP_BITS[order[step // 2]][(step % 2) ^ here]
                table[core, number, place] = mask
    return np.repeat(table, ROWS, axis=2)


def layer_norm(stream, gain, shift):
    average = jnp.mean(stream, axis=-1, keepdims=True)
    centered = stream - average
    variance = jnp.mean(centered * centered, axis=-1, keepdims=True)
    return centered * lax.rsqrt(variance + epsilon) * gain + shift


def rows_dot(left, right):
    return lax.dot_general(left, right, (((0,), (0,)), ((), ())), preferred_element_type=f32)


def cols_dot(left, right):
    return lax.dot_general(left, right, (((1,), (1,)), ((), ())), preferred_element_type=f32)


def dot(left, right):
    return jnp.dot(left, right, preferred_element_type=f32)


def attention_mask():
    row = jnp.arange(256)
    block = (row // 8) * 2 + (row // 4) % 2
    column = row % 4
    return (column[:, None] == column[None, :]) & (block[:, None] >= block[None, :])


def k_dot(left, pieces):
    halves = [half[:, cut] for half in left for cut in (slice(0, 512), slice(512, 1024))]
    return sum(dot(half, piece) for half, piece in zip(halves, pieces))


def n_dot(left, pieces):
    return jnp.concatenate([cols_dot(left, piece).astype(bf16) for piece in pieces], axis=1)


def body(
    hidden_in,
    cond_codes,
    level_ids,
    qkv_weight,
    attn_out_weight,
    mlp_in_weight,
    mlp_out_weight,
    code_table,
    level_table,
    norm_gain,
    norm_bias,
    grad_out,
):
    yl, co, yh, z, x = (lax.axis_index(name) for name in AXES)
    vectors = jnp.concatenate((norm_gain, norm_bias, level_table), axis=0).reshape(1, 90)
    shard0 = jnp.pad(
        jnp.concatenate(
            (
                jnp.pad(attn_out_weight.T, ((0, 0), (0, 32))),
                qkv_weight,
            ),
            axis=1,
        ),
        ((0, 1), (0, 0)),
    ) + jnp.pad(vectors, ((15, 0), (512, 1440 - 90)))
    shard1 = jnp.concatenate((code_table[:, :1024], jnp.pad(mlp_in_weight, ((0, 1), (0, 0)))), axis=1)
    shard2 = jnp.concatenate((code_table[:, 1024:], jnp.pad(mlp_out_weight, ((0, 1), (0, 0)))), axis=1)
    me = yl * 64 + co * 32 + yh * 16 + z * 4 + x
    (attn, qkv), (table_a, expand), (table_b, reduce) = (
        gather_small(shard, order, split)
        for shard, order, split in zip((shard0, shard1, shard2), ORDERS, SPLITS)
    )
    qkv, table_a, table_b = (
        gather_large(buf, order) for buf, order in zip((qkv, table_a, table_b), ORDERS)
    )
    attn, expand, reduce, _ = lax.optimization_barrier((attn, expand, reduce, (qkv[1], table_a[1], table_b[1])))
    attn, expand, reduce = (
        gather_large(buf, order) for buf, order in zip((attn, expand, reduce), ORDERS)
    )

    masks = jnp.asarray(shard_tables())
    place_shard = jnp.where(co == 0, masks[0], masks[1]) ^ me
    row_here = jnp.arange(SHARDS * ROWS) % ROWS
    place_feature = jnp.where(row_here < 15, place_shard * 15 + row_here, -1)
    place_code = place_shard * 16 + row_here
    feature = jnp.arange(D)
    shuffles = [
        [(feature[:, None] == place_feature[k : k + 1, cut]).astype(bf16) for cut in HALVES]
        for k in range(3)
    ]
    shuffle0, shuffle1, shuffle2 = shuffles
    shard_hot = (place_shard[0, ::ROWS][:, None] == feature[None, :] // 15).astype(bf16)
    vector_mask = (jnp.arange(90)[:, None] % 15) == (feature[None, :] % 15)
    codes = jnp.repeat(cond_codes[0], RATIO)

    def hot_of(codes, k):
        return [(codes[:, None] == place_code[k : k + 1, cut]).astype(bf16) for cut in HALVES]

    hot_a, hot_b = hot_of(codes, 1), hot_of(codes, 2)

    def shuffled(value, halves):
        return [dot(value, half).astype(bf16) for half in halves]

    def unshuffled(value, halves):
        return sum(cols_dot(value[:, cut], half) for cut, half in zip(HALVES, halves))

    small = jnp.concatenate([q.reshape(32, ROWS, 1440)[:, 15, :90] for q in qkv], axis=0)
    spread = jnp.where(vector_mask, rows_dot(small, shard_hot), 0.0)
    spread = jnp.sum(spread.reshape(6, 15, D), axis=1)
    gains, shifts, levels = spread[0:2], spread[2:4], spread[4:6]
    chosen = jnp.arange(2) == level_ids[0]
    level_row = jnp.sum(jnp.where(chosen[:, None], levels, 0.0), axis=0)

    hidden = hidden_in[0].astype(f32)
    stream = hidden + jnp.concatenate((k_dot(hot_a, table_a), k_dot(hot_b, table_b)), axis=1) + level_row[None, :]
    normed_first = layer_norm(stream, gains[0], shifts[0]).astype(bf16)
    first_shuffled = shuffled(normed_first, shuffle0)
    packed = k_dot(first_shuffled, qkv).astype(bf16)

    token = jnp.arange(256)
    moved = (token // 4 % 2) * 128 + (token // 8) * 4 + token % 4
    row_move = (moved[:, None] == token[None, :]).astype(bf16)

    def to_columns(value):
        value = dot(row_move, value).astype(bf16)
        return lax.all_to_all(value, BLK, split_axis=0, concat_axis=0, tiled=True)

    def to_tokens(value):
        value = lax.all_to_all(value, BLK, split_axis=0, concat_axis=0, tiled=True)
        return rows_dot(row_move, value).astype(bf16)

    columns = to_columns(packed)
    query, key, value = columns[:, :480], columns[:, 480:960], columns[:, 960:]
    mask = attention_mask()

    scores = jnp.where(mask, cols_dot(query, key) * HEAD ** (-0.5), -1e30)
    row_top = jnp.max(scores, axis=-1, keepdims=True)
    log_total = row_top + jnp.log(jnp.sum(jnp.exp(scores - row_top), axis=-1, keepdims=True))
    probs = jnp.exp(scores - log_total)
    probs_low = probs.astype(bf16)
    mixed = to_tokens(dot(probs_low, value).astype(bf16))

    attn_rows = sum(dot(shuffle0[k // 2][:, 512 * (k % 2) : 512 * (k % 2) + 512], attn[k][:, :480]) for k in range(4)).astype(bf16)
    stream_mid = stream + cols_dot(mixed, attn_rows)
    normed_second = layer_norm(stream_mid, gains[1], shifts[1]).astype(bf16)
    second_shuffled = shuffled(normed_second, shuffle1)
    upward = k_dot(second_shuffled, expand)
    active, gelu_pull = jax.vjp(lambda pre: jax.nn.gelu(pre, approximate=True), upward)
    active = active.astype(bf16)
    active_shuffled = shuffled(active, shuffle2)
    block_out = (stream_mid + k_dot(active_shuffled, reduce)).astype(bf16)

    upstream = grad_out[0]
    d_active = unshuffled(n_dot(upstream, reduce), shuffle2)
    d_upward = gelu_pull(d_active)[0].astype(bf16)
    d_second = unshuffled(n_dot(d_upward, expand), shuffle1)
    _, second_pull = jax.vjp(layer_norm, stream_mid, gains[1], shifts[1])
    d_mid_part, d_gain_second, d_shift_second = second_pull(d_second)
    d_stream_mid = upstream.astype(f32) + d_mid_part
    d_attn = d_stream_mid.astype(bf16)
    attn_shuffled = shuffled(d_attn, shuffle0)
    d_mixed = to_columns(dot(d_attn, attn_rows).astype(bf16))

    early = []
    for left, right in (
        (attn_shuffled, jnp.pad(mixed, ((0, 0), (0, 32)))),
        (second_shuffled, d_upward),
        (active_shuffled, upstream),
    ):
        early.append(outer(left[0], swap_cores(left[1]), right, swap_cores(right)))
    early_got = [exchange(sent, order, 5) for (_, sent), order in zip(early, ORDERS)]

    d_values = rows_dot(probs_low, d_mixed)
    d_probs = cols_dot(d_mixed, value)
    d_scores = (
        probs * (d_probs - jnp.sum(probs * d_probs, axis=-1, keepdims=True))
    ).astype(bf16)
    d_queries = dot(d_scores, key) * HEAD ** (-0.5)
    d_keys = rows_dot(d_scores, query) * HEAD ** (-0.5)
    d_packed = jnp.concatenate((d_queries, d_keys, d_values), axis=1).astype(bf16)
    d_packed, early_got = lax.optimization_barrier((d_packed, early_got))
    d_packed = to_tokens(d_packed)
    early = [add_halves(kept, got) for (kept, _), got in zip(early, early_got)]
    early_got = [exchange(sent, order, 4) for (_, sent), order in zip(early, ORDERS)]
    d_packed_got = swap_cores(d_packed)
    first_got = swap_cores(first_shuffled[1])
    codes_got = swap_cores(codes)
    d_first = unshuffled(n_dot(d_packed, qkv), shuffle0)
    _, first_pull = jax.vjp(layer_norm, stream, gains[0], shifts[0])
    d_stream_part, d_gain_first, d_shift_first = first_pull(d_first)
    d_stream = d_stream_mid + d_stream_part
    d_low = d_stream.astype(bf16)
    d_low_got = swap_cores(d_low)
    table_grad_a = outer(
        hot_a[0], hot_of(codes_got, 1)[0], d_low[:, :1024], d_low_got[:, :1024]
    )
    table_grad_b = outer(
        hot_b[0], hot_of(codes_got, 2)[0], d_low[:, 1024:], d_low_got[:, 1024:]
    )
    d_level = jnp.where(chosen[:, None], jnp.sum(d_stream, axis=0)[None, :], 0.0)
    totals = jnp.concatenate(
        (
            jnp.stack((d_gain_first, d_gain_second, d_shift_first, d_shift_second)),
            d_level,
        ),
        axis=0,
    )
    totals = jnp.where(vector_mask, jnp.repeat(totals, 15, axis=0), 0.0).astype(bf16)
    small = cols_dot(shard_hot, totals).astype(bf16)
    small = small[:64] + swap_cores(small[64:])
    small = jnp.pad(small[:, None, :], ((0, 0), (15, 0), (0, 1440 - 90))).reshape(HALF, 1440)
    qkv_grad = outer(first_shuffled[0], first_got, d_packed, d_packed_got)
    qkv_grad = tuple(g + small[cut] for g, cut in zip(qkv_grad, (slice(0, 512), slice(512, 1024))))
    early = [add_halves(kept, got) for (kept, _), got in zip(early, early_got)]
    ends = []
    for (kept, sent), sums, order in zip((qkv_grad, table_grad_a, table_grad_b), early, ORDERS):
        kept, sent = add_halves(kept, exchange(sent, order, 5))
        late = add_halves(kept, exchange(sent, order, 4))
        kept, sent = (jnp.concatenate(pair, axis=1) for pair in zip(sums, late))
        ends.append(scatter_small(kept, sent, order))
    out0 = jnp.concatenate((ends[0][:, 512:], ends[0][:, :480]), axis=1)
    out1, out2 = ends[1][:, :1920], ends[2][:, :1920]
    out3 = jnp.concatenate((ends[1][:, 1920:], ends[2][:, 1920:]), axis=1)
    small = out0[15, :90].reshape(6, 15)
    return (
        block_out[None],
        d_stream[None],
        out0[:15, :1440],
        out0[:15, 1440:].T,
        out1[:15],
        out2[:15],
        out3,
        small[4:6],
        small[0:2],
        small[2:4],
    )


def solution(mesh):
    fine = Mesh(mesh.devices.reshape(2, 2, 2, 4, 4), AXES)
    return jax.shard_map(
        body,
        mesh=fine,
        in_specs=(
            P(WIN, BLK, None),
            P(WIN, BLK),
            P(WIN),
            P(AXES, None),
            P(None, AXES),
            P(AXES, None),
            P(AXES, None),
            P(AXES, None),
            P(None, AXES),
            P(None, AXES),
            P(None, AXES),
            P(WIN, BLK, None),
        ),
        out_specs=(
            P(WIN, BLK, None),
            P(WIN, BLK, None),
            P(AXES, None),
            P(None, AXES),
            P(AXES, None),
            P(AXES, None),
            P(AXES, None),
            P(None, AXES),
            P(None, AXES),
            P(None, AXES),
        ),
        check_vma=False,
    )
```

```python
import functools

import jax
import jax.numpy as jnp
import numpy as np
from jax import lax
from jax.experimental import pallas as pl
from jax.experimental.pallas import tpu as pltpu
from jax.sharding import Mesh, PartitionSpec as P

HEAD = 480
BLOCK = 128
RATIO = 4
D = 1920
SHARDS = 128
ROWS = 16
HALF = 1024
HALVES = (slice(0, HALF), slice(HALF, 2 * HALF))
SPLITS = (512, 1024, 896)
TOKENS = 256
CHUNK = 640
MIB = 2**20
ROW_STEP = 32
epsilon = 1e-05
bf16 = jnp.bfloat16
f32 = jnp.float32
AXES = ("yl", "co", "yh", "z", "x")
WIN = ("yl", "co")
BLK = ("yh", "z", "x")
STEP_BITS = {"x": (1, 3), "z": (4, 12), "y": (64, 80)}
CORE_BIT = 32
ORDERS = (("x", "z", "y"), ("z", "y", "x"), ("y", "x", "z"))


def exchange(value, order, step):
    masks = STEP_BITS[order[step // 2]]
    pairs = [(i, i ^ masks[(step % 2) ^ ((i >> 5) & 1)]) for i in range(SHARDS)]
    return lax.ppermute(value, AXES, pairs)


def swap_cores(value):
    return lax.ppermute(value, AXES, [(i, i ^ CORE_BIT) for i in range(SHARDS)])


def call(kernel, out_shape, vmem=32, **options):
    params = pltpu.CompilerParams(vmem_limit_bytes=vmem * MIB)
    return pl.pallas_call(kernel, out_shape=out_shape, compiler_params=params, **options)


def shape(rows, columns, dtype=bf16):
    return jax.ShapeDtypeStruct((rows, columns), dtype)


def dot(left, right):
    return jnp.dot(left, right, preferred_element_type=f32)


def rows_dot(left, right):
    return lax.dot_general(left, right, (((0,), (0,)), ((), ())), preferred_element_type=f32)


def cols_dot(left, right):
    return lax.dot_general(left, right, (((1,), (1,)), ((), ())), preferred_element_type=f32)


def hot(left, right):
    return jnp.where(left == right, 1.0, 0.0).astype(bf16)


def join_kernel(tiles, cuts, first, second, *targets):
    @pl.when(pl.program_id(0) < tiles)
    def _():
        for target, (start, stop) in zip(targets, cuts):
            target[...] = first[:, start:stop]

    @pl.when(pl.program_id(0) >= tiles)
    def _():
        for target, (start, stop) in zip(targets, cuts):
            target[...] = second[:, start:stop]


def join(first, second, cuts=None):
    rows, columns = first.shape
    cuts = cuts or ((0, columns),)
    tiles = max(rows // 64, 1)
    tile = rows // tiles
    out = call(
        functools.partial(join_kernel, tiles, cuts),
        tuple(shape(2 * rows, stop - start) for start, stop in cuts),
        grid=(2 * tiles,),
        in_specs=[
            pl.BlockSpec((tile, columns), lambda i: (jnp.minimum(i, tiles - 1), 0)),
            pl.BlockSpec((tile, columns), lambda i: (jnp.maximum(i - tiles, 0), 0)),
        ],
        out_specs=tuple(pl.BlockSpec((tile, stop - start), lambda i: (i, 0)) for start, stop in cuts),
    )(first, second)
    return out if len(cuts) > 1 else out[0]


def gather_small(buf, order, split):
    for step in range(3):
        buf = join(buf, exchange(buf, order, step))
    return join(buf, exchange(buf, order, 3), ((0, split), (split, buf.shape[1])))


def gather_large(buf, order):
    half = join(buf, exchange(buf, order, 4))
    rest = exchange(half, order, 5)
    return half, rest, swap_cores(half), swap_cores(rest)


def add_kernel(kept_low, kept_high, got_low, got_high, kept, sent):
    kept[...] = (kept_low[...].astype(f32) + got_low[...].astype(f32)).astype(bf16)
    sent[...] = (kept_high[...].astype(f32) + got_high[...].astype(f32)).astype(bf16)


def add_halves(kept, got):
    rows, columns = kept.shape[0] // 2, kept.shape[1]
    tiles = max(rows // 64, 1)
    tile = rows // tiles
    low = pl.BlockSpec((tile, columns), lambda i: (i, 0))
    high = pl.BlockSpec((tile, columns), lambda i: (i + tiles, 0))
    half = shape(rows, columns)
    return call(
        add_kernel, (half, half), grid=(tiles,), in_specs=[low, high, low, high], out_specs=(low, low)
    )(kept, kept, got, got)


def merge_kernel(*refs):
    sources, kept, sent = refs[:8], refs[8], refs[9]
    start = 0
    for one in (0, 4):
        columns = sources[one].shape[1]
        for target, low in ((kept, one), (sent, one + 1)):
            total = sources[low][...].astype(f32) + sources[low + 2][...].astype(f32)
            target[:, start : start + columns] = total.astype(bf16)
        start += columns


def merge_halves(early, early_got, late, late_got):
    rows = early.shape[0] // 2
    tiles = rows // 64
    columns = early.shape[1] + late.shape[1]
    low = lambda v: pl.BlockSpec((64, v.shape[1]), lambda i: (i, 0))
    high = lambda v: pl.BlockSpec((64, v.shape[1]), lambda i: (i + tiles, 0))
    specs = [spec(v) for v in (early, late) for spec in (low, high, low, high)]
    out = pl.BlockSpec((64, columns), lambda i: (i, 0))
    half = shape(rows, columns)
    return call(merge_kernel, (half, half), grid=(tiles,), in_specs=specs, out_specs=(out, out))(
        early, early, early_got, early_got, late, late, late_got, late_got
    )


def outer_kernel(tiles, extra, left, left_got, right, right_got, *refs):
    small, kept, sent = refs if extra else (None,) + refs
    rows = HALF // 2 // tiles
    columns = right.shape[1]
    step = pl.program_id(0)
    for target, base in ((kept, 0), (sent, HALF // 2)):
        start = pl.multiple_of(base + step * rows, rows)
        one, two = left[:, pl.ds(start, rows)], left_got[:, pl.ds(start, rows)]
        for cut in range(0, columns, 512):
            span = slice(cut, min(cut + 512, columns))
            total = rows_dot(one, right[:, span]) + rows_dot(two, right_got[:, span])
            target[:, span] = total.astype(bf16)
        if extra:
            row = lax.broadcasted_iota(jnp.int32, (rows, 64), 0) + start
            chunk = lax.broadcasted_iota(jnp.int32, (rows, 64), 1)
            target[:, columns:] = dot(hot(row, chunk * ROWS), small[...]).astype(bf16)


def outer(left, left_got, right, right_got, small=None):
    tiles = 4
    extra = small is not None
    columns = right.shape[1] + (128 if extra else 0)
    whole = lambda v: pl.BlockSpec(v.shape, lambda i: (0, 0))
    half = shape(HALF // 2, columns)
    tile = pl.BlockSpec((HALF // 2 // tiles, columns), lambda i: (i, 0))
    args = (left, left_got, right, right_got) + ((small,) if extra else ())
    return call(
        functools.partial(outer_kernel, tiles, extra),
        (half, half),
        grid=(tiles,),
        in_specs=[whole(v) for v in args],
        out_specs=(tile, tile),
    )(*args)


def shard_tables():
    table = np.zeros((2, 3, SHARDS), np.int32)
    for core in range(2):
        for number, order in enumerate(ORDERS):
            for place in range(SHARDS):
                here = core ^ (place >> 6)
                mask = (place >> 6) * CORE_BIT
                for step in range(6):
                    if (place >> step) & 1:
                        mask ^= STEP_BITS[order[step // 2]][(step % 2) ^ here]
                table[core, number, place] = mask
    return table


class Fetch:
    def __init__(self, sources, targets, sem):
        self.copies = [
            pltpu.make_async_copy(source, target, sem.at[i])
            for i, (source, target) in enumerate(zip(sources, targets))
        ]
        self.targets = targets
        for copy in self.copies:
            copy.start()

    def __call__(self, *numbers):
        for number in numbers:
            self.copies[number].wait()
        return [self.targets[number] for number in numbers]


def fetched(arrays):
    return [pltpu.VMEM(v.shape, v.dtype) for v in arrays] + [pltpu.SemaphoreType.DMA((len(arrays),))]


def split_refs(refs, *counts):
    out, start = [], 0
    for count in counts:
        out.append(refs[start : start + count])
        start += count
    return out


def each_chunk(columns, body, width=CHUNK):
    @pl.loop(0, columns // width)
    def _(i):
        body(pl.ds(pl.multiple_of(i * width, 128), width))


def each_rows(body):
    @pl.loop(0, TOKENS // ROW_STEP)
    def _(i):
        body(pl.ds(pl.multiple_of(i * ROW_STEP, ROW_STEP), ROW_STEP))


def shuffle(value, targets, line, own, other):
    for half, target in enumerate((own, other)):

        def part(span, half=half, target=target):
            place = targets[line : line + 1, pl.ds(pl.multiple_of(span.start + half * HALF, 128), 256)]
            feature = lax.broadcasted_iota(jnp.int32, (D, 256), 0)
            target[:, span] = dot(value[...], hot(feature, place)).astype(bf16)

        each_chunk(HALF, part, 256)


def unshuffle(value, target_columns, line, out):
    def part(span):
        feature = lax.broadcasted_iota(jnp.int32, (512, CHUNK), 1) + span.start
        total = None
        for k in range(4):
            cut = slice(512 * k, 512 * k + 512)
            place = target_columns[cut, line : line + 1]
            term = dot(value[:, cut], hot(place, feature))
            total = term if total is None else total + term
        out[:, span] = total

    each_chunk(D, part)


def pieces_of(own, other):
    return [ref[:, cut] for ref in (own, other) for cut in (slice(0, 512), slice(512, 1024))]


def row_move(transposed=False):
    row = lax.broadcasted_iota(jnp.int32, (TOKENS, TOKENS), 1 if transposed else 0)
    token = lax.broadcasted_iota(jnp.int32, (TOKENS, TOKENS), 0 if transposed else 1)
    moved = jnp.right_shift(row, 3) * 4 + (row & 3) + (jnp.right_shift(row, 2) & 1) * 128
    return hot(token, moved)


def moments(value):
    average = jnp.mean(value, axis=-1, keepdims=True)
    centered = value - average
    variance = jnp.mean(centered * centered, axis=-1, keepdims=True)
    return centered, lax.rsqrt(variance + epsilon)


def norm_back(value, grad, gain, base):
    centered, scale = moments(value)
    normed = centered * scale
    scaled = grad * gain
    inner = scaled - jnp.mean(scaled, axis=-1, keepdims=True)
    inner = inner - normed * jnp.mean(scaled * normed, axis=-1, keepdims=True)
    return base + scale * inner, grad * normed


def embed_kernel(*refs):
    small, big, outs, scratch = split_refs(refs, 6, 12, 5, len(refs) - 23)
    hidden, codes, level, targets, shard_column, marks = small
    stream, own, other, packed, vectors = outs
    normed = scratch[-1]
    fetch = Fetch(big, scratch[:12], scratch[12])
    tables_a, tables_b, weights = range(0, 4), range(4, 8), range(8, 12)
    for line, numbers, start in ((3, tables_a, 0), (4, tables_b, 1024)):
        table = fetch(*numbers)
        total = None
        for k in range(4):
            term = dot(hot(codes[...], targets[line : line + 1, 512 * k : 512 * k + 512]), table[k][...])
            total = term if total is None else total + term
        stream[:, start : start + table[0].shape[1]] = total
    weight = fetch(*weights)
    chunk = lax.broadcasted_iota(jnp.int32, (SHARDS, 512), 0)
    row = lax.broadcasted_iota(jnp.int32, (SHARDS, 512), 1)
    lines = None
    for k in range(4):
        term = dot(hot(row + 512 * k, chunk * ROWS + 15), weight[k][:, :128])
        lines = term if lines is None else lines + term
    spread = rows_dot(lines.astype(bf16), hot(shard_column[:, 0:1], marks[0:1, :]))
    within = lax.broadcasted_iota(jnp.int32, (SHARDS, 1), 0)
    group = sum((within >= 15 * r).astype(jnp.int32) for r in range(1, 7))
    spread = jnp.where(within - group * 15 == marks[1:2, :], spread, 0.0).astype(bf16)
    number = lax.broadcasted_iota(jnp.int32, (8, SHARDS), 1)
    first = lax.broadcasted_iota(jnp.int32, (8, SHARDS), 0) * 15
    chosen = jnp.where((number >= first) & (number < first + 15), 1.0, 0.0).astype(bf16)
    vectors[...] = dot(chosen, spread)
    level_row = jnp.where(level[0] == 0, vectors[4:5, :], vectors[5:6, :])

    def rows(span):
        value = stream[span, :] + hidden[span, :].astype(f32) + level_row
        stream[span, :] = value
        centered, scale = moments(value)
        normed[span, :] = (centered * scale * vectors[0:1, :] + vectors[2:3, :]).astype(bf16)

    each_rows(rows)
    normed[...] = dot(row_move(), normed[...]).astype(bf16)
    shuffle(normed, targets, 0, own, other)
    packed[...] = sum(dot(p, w[...]) for p, w in zip(pieces_of(own, other), weight)).astype(bf16)


def embed(hidden, codes, level, targets, shard_column, marks, tables_a, tables_b, qkv):
    big = (*tables_a, *tables_b, *qkv)
    vmem = pl.BlockSpec(memory_space=pltpu.VMEM)
    return call(
        embed_kernel,
        (
            shape(TOKENS, D, f32),
            shape(TOKENS, HALF),
            shape(TOKENS, HALF),
            shape(TOKENS, 1440),
            shape(8, D, f32),
        ),
        vmem=48,
        in_specs=[vmem, vmem, pl.BlockSpec(memory_space=pltpu.SMEM), vmem, vmem, vmem]
        + [pl.BlockSpec(memory_space=pl.ANY)] * 12,
        out_specs=[vmem] * 5,
        scratch_shapes=fetched(big) + [pltpu.VMEM((TOKENS, D), bf16)],
    )(hidden, codes, level, targets, shard_column, marks, *big)


def probabilities(columns):
    query, key = columns[:, 0:480], columns[:, 480:960]
    row = lax.broadcasted_iota(jnp.int32, (TOKENS, TOKENS), 0)
    other = lax.broadcasted_iota(jnp.int32, (TOKENS, TOKENS), 1)
    mask = ((row & 3) == (other & 3)) & (jnp.right_shift(row, 2) >= jnp.right_shift(other, 2))
    scores = jnp.where(mask, cols_dot(query, key) * HEAD ** (-0.5), -1e30)
    top = jnp.max(scores, axis=-1, keepdims=True)
    total = top + jnp.log(jnp.sum(jnp.exp(scores - top), axis=-1, keepdims=True))
    return jnp.exp(scores - total)


def attend_kernel(columns, mixed):
    mixed[...] = dot(probabilities(columns).astype(bf16), columns[:, 960:1440]).astype(bf16)


def attend(columns):
    return call(attend_kernel, shape(TOKENS, 480))(columns)


def attend_back_kernel(columns, d_mixed, d_packed):
    probs = probabilities(columns)
    low = probs.astype(bf16)
    d_probs = cols_dot(d_mixed[...], columns[:, 960:1440])
    d_scores = (probs * (d_probs - jnp.sum(probs * d_probs, axis=-1, keepdims=True))).astype(bf16)
    scale = HEAD ** (-0.5)
    d_packed[:, 0:480] = (dot(d_scores, columns[:, 480:960]) * scale).astype(bf16)
    d_packed[:, 480:960] = (rows_dot(d_scores, columns[:, 0:480]) * scale).astype(bf16)
    d_packed[:, 960:1440] = rows_dot(low, d_mixed[...]).astype(bf16)


def attend_back(columns, d_mixed):
    return call(attend_back_kernel, shape(TOKENS, 1440))(columns, d_mixed)


def middle_kernel(*refs):
    small, big, outs, scratch = split_refs(refs, 6, 12, 12, len(refs) - 30)
    mixed_columns, stream, vectors, upstream, targets, target_columns = small
    block_out, d_mid, second_own, second_other, active_own, active_other = outs[:6]
    attn_own, attn_other, d_upward, mixed, d_mixed, sums = outs[6:]
    fetch = Fetch(big, scratch[:12], scratch[12])
    mid, work, slope, wide, low = scratch[13:]
    attn = fetch(*range(0, 4))
    mixed[...] = jnp.zeros(mixed.shape, bf16)
    mixed[:, 0:480] = dot(row_move(True), mixed_columns[...]).astype(bf16)
    for k in range(4):
        wide[:, 512 * k : 512 * k + 512] = cols_dot(mixed[...], attn[k][...]).astype(bf16)
    unshuffle(wide, target_columns, 0, work)

    def rows_first(span):
        value = stream[span, :] + work[span, :]
        mid[span, :] = value
        centered, scale = moments(value)
        low[span, :] = (centered * scale * vectors[1:2, :] + vectors[3:4, :]).astype(bf16)

    each_rows(rows_first)
    shuffle(low, targets, 1, second_own, second_other)
    expand = fetch(*range(4, 8))

    def up(span):
        parts = zip(pieces_of(second_own, second_other), expand)
        work[:, span] = sum(dot(p, w[:, span]) for p, w in parts)

    each_chunk(D, up)

    def rows_active(span):
        value = work[span, :]
        root = np.float32(np.sqrt(2 / np.pi))
        square = value * value
        bend = jnp.tanh(root * value * (1.0 + 0.044715 * square))
        low[span, :] = (0.5 * value * (1.0 + bend)).astype(bf16)
        inner = root * (1.0 + 3 * 0.044715 * square)
        slope[span, :] = 0.5 * (1.0 + bend) + 0.5 * value * (1.0 - bend * bend) * inner

    each_rows(rows_active)
    shuffle(low, targets, 2, active_own, active_other)
    reduce = fetch(*range(8, 12))

    def down(span):
        parts = zip(pieces_of(active_own, active_other), reduce)
        total = sum(dot(p, w[:, span]) for p, w in parts)
        block_out[:, span] = (mid[:, span] + total).astype(bf16)

    each_chunk(D, down)
    for k in range(4):
        wide[:, 512 * k : 512 * k + 512] = cols_dot(upstream[...], reduce[k][...]).astype(bf16)
    unshuffle(wide, target_columns, 2, work)

    def rows_upward(span):
        d_upward[span, :] = (slope[span, :] * work[span, :]).astype(bf16)

    each_rows(rows_upward)
    for k in range(4):
        wide[:, 512 * k : 512 * k + 512] = cols_dot(d_upward[...], expand[k][...]).astype(bf16)
    unshuffle(wide, target_columns, 1, work)
    sums[...] = jnp.zeros(sums.shape, f32)

    def rows_back(span):
        base = upstream[span, :].astype(f32)
        grad = work[span, :]
        value, gain_part = norm_back(mid[span, :], grad, vectors[1:2, :], base)
        d_mid[span, :] = value
        low[span, :] = value.astype(bf16)
        sums[0:1, :] += jnp.sum(gain_part, axis=0, keepdims=True)
        sums[1:2, :] += jnp.sum(grad, axis=0, keepdims=True)

    each_rows(rows_back)
    shuffle(low, targets, 0, attn_own, attn_other)
    back = sum(dot(p, w[:, 0:480]) for p, w in zip(pieces_of(attn_own, attn_other), attn))
    d_mixed[...] = dot(row_move(), back.astype(bf16)).astype(bf16)


def middle(mixed_columns, stream, vectors, upstream, targets, target_columns, attn, expand, reduce):
    big = (*attn, *expand, *reduce)
    vmem = pl.BlockSpec(memory_space=pltpu.VMEM)
    half = shape(TOKENS, HALF)
    return call(
        middle_kernel,
        (shape(TOKENS, D), shape(TOKENS, D, f32))
        + (half,) * 6
        + (shape(TOKENS, D), shape(TOKENS, 512), shape(TOKENS, 480), shape(8, D, f32)),
        vmem=60,
        in_specs=[vmem] * 6 + [pl.BlockSpec(memory_space=pl.ANY)] * 12,
        out_specs=[vmem] * 12,
        scratch_shapes=fetched(big)
        + [pltpu.VMEM((TOKENS, D), f32)] * 3
        + [pltpu.VMEM((TOKENS, 2 * HALF), bf16), pltpu.VMEM((TOKENS, D), bf16)],
    )(mixed_columns, stream, vectors, upstream, targets, target_columns, *big)


def last_kernel(*refs):
    small, big, outs, scratch = split_refs(refs, 9, 4, 3, len(refs) - 16)
    d_packed, stream, d_mid, vectors, sums, level, target_columns, shard_column, marks = small
    d_stream, d_low, spread = outs
    fetch = Fetch(big, scratch[:4], scratch[4])
    work, wide, totals = scratch[5:]
    weight = fetch(*range(4))
    for k in range(4):
        wide[:, 512 * k : 512 * k + 512] = cols_dot(d_packed[...], weight[k][...]).astype(bf16)
    wide[...] = dot(row_move(True), wide[...]).astype(bf16)
    unshuffle(wide, target_columns, 0, work)
    totals[...] = jnp.zeros(totals.shape, f32)

    def rows(span):
        grad = work[span, :]
        value, gain_part = norm_back(stream[span, :], grad, vectors[0:1, :], d_mid[span, :])
        d_stream[span, :] = value
        d_low[span, :] = value.astype(bf16)
        totals[0:1, :] += jnp.sum(gain_part, axis=0, keepdims=True)
        totals[2:3, :] += jnp.sum(grad, axis=0, keepdims=True)
        totals[6:7, :] += jnp.sum(value, axis=0, keepdims=True)

    each_rows(rows)
    totals[1:2, :] = sums[0:1, :]
    totals[3:4, :] = sums[1:2, :]
    totals[4:5, :] = jnp.where(level[0] == 0, totals[6:7, :], 0.0)
    totals[5:6, :] = jnp.where(level[0] == 1, totals[6:7, :], 0.0)
    number = lax.broadcasted_iota(jnp.int32, (SHARDS, 8), 0)
    first = lax.broadcasted_iota(jnp.int32, (SHARDS, 8), 1) * 15
    chosen = jnp.where((number >= first) & (number < first + 15) & (number < 90), 1.0, 0.0)
    repeated = dot(chosen.astype(bf16), totals[...].astype(bf16))
    within = lax.broadcasted_iota(jnp.int32, (SHARDS, 1), 0)
    group = sum((within >= 15 * r).astype(jnp.int32) for r in range(1, 7))
    repeated = jnp.where(within - group * 15 == marks[1:2, :], repeated, 0.0).astype(bf16)
    spread[...] = cols_dot(hot(shard_column[:, 2:3], marks[0:1, :]), repeated).astype(bf16)


def last(d_packed, stream, d_mid, vectors, sums, level, target_columns, shard_column, marks, qkv):
    vmem = pl.BlockSpec(memory_space=pltpu.VMEM)
    return call(
        last_kernel,
        (shape(TOKENS, D, f32), shape(TOKENS, D), shape(SHARDS, 128)),
        vmem=40,
        in_specs=[vmem] * 5
        + [pl.BlockSpec(memory_space=pltpu.SMEM)]
        + [vmem] * 3
        + [pl.BlockSpec(memory_space=pl.ANY)] * 4,
        out_specs=[vmem] * 3,
        scratch_shapes=fetched(qkv)
        + [
            pltpu.VMEM((TOKENS, D), f32),
            pltpu.VMEM((TOKENS, 2 * HALF), bf16),
            pltpu.VMEM((8, D), f32),
        ],
    )(d_packed, stream, d_mid, vectors, sums, level, target_columns, shard_column, marks, *qkv)


def finish_kernel(kept0, got0, kept1, got1, kept2, got2, *outs):
    grad_qkv, grad_attn, grad_expand, grad_reduce, table, levels, gains, shifts = outs

    def total(kept, got, start, stop):
        return kept[:, start:stop].astype(f32) + got[:, start:stop].astype(f32)

    grad_attn[...] = total(kept0, got0, 0, 480)[:15]
    grad_qkv[...] = total(kept0, got0, 512, 1952)[:15]
    grad_expand[...] = total(kept1, got1, 0, 1920)[:15]
    table[:, 0:1024] = total(kept1, got1, 1920, 2944)
    grad_reduce[...] = total(kept2, got2, 0, 1920)[:15]
    table[:, 1024:1920] = total(kept2, got2, 1920, 2816)
    line = total(kept2, got2, 2816, 2944)[0:1]
    for target, first in ((gains, 0), (shifts, 2), (levels, 4)):
        for row in range(2):
            start = (first + row) * 15
            target[row : row + 1, :] = line[:, start : start + 15]


def finish(*pairs):
    vmem = pl.BlockSpec(memory_space=pltpu.VMEM)
    return call(
        finish_kernel,
        tuple(
            shape(*s, f32)
            for s in ((15, 1440), (15, 480), (15, D), (15, D), (16, D), (2, 15), (2, 15), (2, 15))
        ),
        in_specs=[vmem] * 6,
        out_specs=[vmem] * 8,
    )(*pairs)


def body(
    hidden_in,
    cond_codes,
    level_ids,
    qkv_weight,
    attn_out_weight,
    mlp_in_weight,
    mlp_out_weight,
    code_table,
    level_table,
    norm_gain,
    norm_bias,
    grad_out,
):
    yl, co, yh, z, x = (lax.axis_index(name) for name in AXES)
    me = yl * 64 + co * 32 + yh * 16 + z * 4 + x
    vectors = jnp.concatenate((norm_gain, norm_bias, level_table), axis=0).reshape(1, 90)
    shard0 = jnp.pad(
        jnp.concatenate((jnp.pad(attn_out_weight.T, ((0, 0), (0, 32))), qkv_weight), axis=1),
        ((0, 1), (0, 0)),
    ) + jnp.pad(vectors, ((15, 0), (512, 1440 - 90)))
    shard1 = jnp.concatenate((code_table[:, :1024], jnp.pad(mlp_in_weight, ((0, 1), (0, 0)))), axis=1)
    shard2 = jnp.concatenate((code_table[:, 1024:], jnp.pad(mlp_out_weight, ((0, 1), (0, 0)))), axis=1)
    (attn, qkv), (table_a, expand), (table_b, reduce) = (
        gather_small(shard, order, split)
        for shard, order, split in zip((shard0, shard1, shard2), ORDERS, SPLITS)
    )
    qkv, table_a, table_b = (
        gather_large(buf, order) for buf, order in zip((qkv, table_a, table_b), ORDERS)
    )
    attn, expand, reduce, _ = lax.optimization_barrier(
        (attn, expand, reduce, (qkv[1], table_a[1], table_b[1]))
    )
    attn, expand, reduce = (
        gather_large(buf, order) for buf, order in zip((attn, expand, reduce), ORDERS)
    )

    masks = jnp.asarray(shard_tables())
    here = jnp.where(co == 0, masks[0], masks[1]) ^ me
    place = jnp.repeat(here, ROWS, axis=1)
    row_here = jnp.arange(SHARDS * ROWS)[None, :] % ROWS
    place_feature = jnp.where(row_here < 15, place * 15 + row_here, -1)
    targets = jnp.concatenate((place_feature, (place * 16 + row_here)[1:]), axis=0)
    target_columns = place_feature.T
    shard_column = here.T
    feature = np.arange(D, dtype=np.int32)
    marks = jnp.asarray(np.stack((feature // 15, feature % 15)))
    codes = jnp.repeat(cond_codes[0], RATIO)[:, None]

    stream, first_own, first_other, packed, vectors = embed(
        hidden_in[0], codes, level_ids, targets, shard_column, marks, table_a, table_b, qkv
    )

    def over_blocks(value):
        return lax.all_to_all(value, BLK, split_axis=0, concat_axis=0, tiled=True)

    columns = over_blocks(packed)
    mixed = over_blocks(attend(columns))
    upstream = grad_out[0]
    (
        block_out,
        d_mid,
        second_own,
        second_other,
        active_own,
        active_other,
        attn_own,
        attn_other,
        d_upward,
        mixed,
        d_mixed,
        sums,
    ) = middle(mixed, stream, vectors, upstream, targets, target_columns, attn, expand, reduce)
    d_mixed = over_blocks(d_mixed)
    early = [
        outer(own, swap_cores(other), right, swap_cores(right))
        for own, other, right in (
            (attn_own, attn_other, mixed),
            (second_own, second_other, d_upward),
            (active_own, active_other, upstream),
        )
    ]
    early_got = [exchange(sent, order, 5) for (_, sent), order in zip(early, ORDERS)]
    first_got = swap_cores(first_other)
    codes_got = swap_cores(codes)

    d_packed = attend_back(columns, d_mixed)
    d_packed, early_got = lax.optimization_barrier((d_packed, early_got))
    d_packed = over_blocks(d_packed)
    early = [add_halves(kept, got) for (kept, _), got in zip(early, early_got)]
    early_got = [exchange(sent, order, 4) for (_, sent), order in zip(early, ORDERS)]
    qkv_grad = outer(first_own, first_got, d_packed, swap_cores(d_packed))

    d_stream, d_low, small = last(
        d_packed, stream, d_mid, vectors, sums, level_ids, target_columns, shard_column, marks, qkv
    )
    small = small[:64] + swap_cores(small[64:])
    d_low_got = swap_cores(d_low)

    def hot_of(codes, line):
        return (codes == targets[line : line + 1, :HALF]).astype(bf16)

    grad_a = outer(hot_of(codes, 3), hot_of(codes_got, 3), d_low[:, :1024], d_low_got[:, :1024])
    grad_b = outer(hot_of(codes, 4), hot_of(codes_got, 4), d_low[:, 1024:], d_low_got[:, 1024:], small)
    pairs = []
    for (kept, sent), (before, _), before_got, order in zip(
        (qkv_grad, grad_a, grad_b), early, early_got, ORDERS
    ):
        kept, sent = add_halves(kept, exchange(sent, order, 5))
        kept, sent = merge_halves(before, before_got, kept, exchange(sent, order, 4))
        for step in (3, 2, 1):
            kept, sent = add_halves(kept, exchange(sent, order, step))
        pairs += [kept, exchange(sent, order, 0)]
    grad_qkv, grad_attn, grad_expand, grad_reduce, grad_table, levels, gains, shifts = finish(*pairs)
    return (
        block_out[None],
        d_stream[None],
        grad_qkv,
        grad_attn.T,
        grad_expand,
        grad_reduce,
        grad_table,
        levels,
        gains,
        shifts,
    )


def solution(mesh):
    fine = Mesh(mesh.devices.reshape(2, 2, 2, 4, 4), AXES)
    return jax.shard_map(
        body,
        mesh=fine,
        in_specs=(
            P(WIN, BLK, None),
            P(WIN, BLK),
            P(WIN),
            P(AXES, None),
            P(None, AXES),
            P(AXES, None),
            P(AXES, None),
            P(AXES, None),
            P(None, AXES),
            P(None, AXES),
            P(None, AXES),
            P(WIN, BLK, None),
        ),
        out_specs=(
            P(WIN, BLK, None),
            P(WIN, BLK, None),
            P(AXES, None),
            P(None, AXES),
            P(AXES, None),
            P(AXES, None),
            P(AXES, None),
            P(None, AXES),
            P(None, AXES),
            P(None, AXES),
        ),
        check_vma=False,
    )
```

```python
import functools

import jax
import jax.numpy as jnp
import numpy as np
from jax import lax
from jax.experimental import pallas as pl
from jax.experimental.pallas import tpu as pltpu
from jax.sharding import Mesh, PartitionSpec as P

HEAD = 480
BLOCK = 128
RATIO = 4
D = 1920
SHARDS = 128
ROWS = 16
HALF = 1024
HALVES = (slice(0, HALF), slice(HALF, 2 * HALF))
SPLITS = (1536, 1024, 896)
TOKENS = 256
CHUNK = 640
MIB = 2**20
ROW_STEP = 32
epsilon = 1e-05
bf16 = jnp.bfloat16
f32 = jnp.float32
AXES = ("yl", "co", "yh", "z", "x")
WIN = ("yl", "co")
BLK = ("yh", "z", "x")
STEP_BITS = {"x": (1, 3), "z": (4, 12), "y": (64, 80)}
CORE_BIT = 32
ORDERS = (("x", "z", "y"), ("z", "y", "x"), ("y", "x", "z"))


def exchange(value, order, step):
    masks = STEP_BITS[order[step // 2]]
    pairs = [(i, i ^ masks[(step % 2) ^ ((i >> 5) & 1)]) for i in range(SHARDS)]
    return lax.ppermute(value, AXES, pairs)


def swap_cores(value):
    return lax.ppermute(value, AXES, [(i, i ^ CORE_BIT) for i in range(SHARDS)])


def call(kernel, out_shape, vmem=32, **options):
    params = pltpu.CompilerParams(vmem_limit_bytes=vmem * MIB)
    return pl.pallas_call(kernel, out_shape=out_shape, compiler_params=params, **options)


def shape(rows, columns, dtype=bf16):
    return jax.ShapeDtypeStruct((rows, columns), dtype)


def dot(left, right):
    return jnp.dot(left, right, preferred_element_type=f32)


def rows_dot(left, right):
    return lax.dot_general(left, right, (((0,), (0,)), ((), ())), preferred_element_type=f32)


def cols_dot(left, right):
    return lax.dot_general(left, right, (((1,), (1,)), ((), ())), preferred_element_type=f32)


def hot(left, right):
    return jnp.where(left == right, 1.0, 0.0).astype(bf16)


def join_kernel(tiles, cuts, first, second, *targets):
    @pl.when(pl.program_id(0) < tiles)
    def _():
        for target, (start, stop) in zip(targets, cuts):
            target[...] = first[:, start:stop]

    @pl.when(pl.program_id(0) >= tiles)
    def _():
        for target, (start, stop) in zip(targets, cuts):
            target[...] = second[:, start:stop]


def join(first, second, cuts=None):
    rows, columns = first.shape
    cuts = cuts or ((0, columns),)
    tiles = max(rows // 128, 1)
    tile = rows // tiles
    out = call(
        functools.partial(join_kernel, tiles, cuts),
        tuple(shape(2 * rows, stop - start) for start, stop in cuts),
        grid=(2 * tiles,),
        in_specs=[
            pl.BlockSpec((tile, columns), lambda i: (jnp.minimum(i, tiles - 1), 0)),
            pl.BlockSpec((tile, columns), lambda i: (jnp.maximum(i - tiles, 0), 0)),
        ],
        out_specs=tuple(pl.BlockSpec((tile, stop - start), lambda i: (i, 0)) for start, stop in cuts),
    )(first, second)
    return out if len(cuts) > 1 else out[0]


def add_kernel(kept_low, kept_high, got_low, got_high, kept, sent):
    kept[...] = (kept_low[...].astype(f32) + got_low[...].astype(f32)).astype(bf16)
    sent[...] = (kept_high[...].astype(f32) + got_high[...].astype(f32)).astype(bf16)


def add_halves(kept, got):
    rows, columns = kept.shape[0] // 2, kept.shape[1]
    tiles = max(rows // 128, 1)
    tile = rows // tiles
    low = pl.BlockSpec((tile, columns), lambda i: (i, 0))
    high = pl.BlockSpec((tile, columns), lambda i: (i + tiles, 0))
    half = shape(rows, columns)
    return call(
        add_kernel, (half, half), grid=(tiles,), in_specs=[low, high, low, high], out_specs=(low, low)
    )(kept, kept, got, got)


def merge_kernel(*refs):
    sources, kept, sent = refs[:8], refs[8], refs[9]
    start = 0
    for one in (0, 4):
        columns = sources[one].shape[1]
        for target, low in ((kept, one), (sent, one + 1)):
            total = sources[low][...].astype(f32) + sources[low + 2][...].astype(f32)
            target[:, start : start + columns] = total.astype(bf16)
        start += columns


def merge_halves(early, early_got, late, late_got):
    rows = early.shape[0] // 2
    tiles = rows // 64
    columns = early.shape[1] + late.shape[1]
    low = lambda v: pl.BlockSpec((64, v.shape[1]), lambda i: (i, 0))
    high = lambda v: pl.BlockSpec((64, v.shape[1]), lambda i: (i + tiles, 0))
    specs = [spec(v) for v in (early, late) for spec in (low, high, low, high)]
    out = pl.BlockSpec((64, columns), lambda i: (i, 0))
    half = shape(rows, columns)
    return call(merge_kernel, (half, half), grid=(tiles,), in_specs=specs, out_specs=(out, out))(
        early, early, early_got, early_got, late, late, late_got, late_got
    )


def outer_kernel(tiles, line, extra, left, left_got, right, right_got, *refs):
    kept, sent = refs[-2:]
    rows = HALF // 2 // tiles
    columns = right.shape[1]
    step = pl.program_id(0)
    for target, base in ((kept, 0), (sent, HALF // 2)):
        start = pl.multiple_of(base + step * rows, rows)
        if line is None:
            one, two = left[:, pl.ds(start, rows)], left_got[:, pl.ds(start, rows)]
        else:
            places_here = refs[0][line : line + 1, pl.ds(start, rows)]
            one, two = hot(left[...], places_here), hot(left_got[...], places_here)
        for cut in range(0, columns, 512):
            span = slice(cut, min(cut + 512, columns))
            total = rows_dot(one, right[:, span]) + rows_dot(two, right_got[:, span])
            target[:, span] = total.astype(bf16)
        if extra == "small":
            row = lax.broadcasted_iota(jnp.int32, (rows, 64), 0) + start
            chunk = lax.broadcasted_iota(jnp.int32, (rows, 64), 1)
            target[:, columns:] = dot(hot(row, chunk * ROWS), refs[1][...]).astype(bf16)
        elif extra == "zero":
            target[:, columns:] = jnp.zeros((rows, target.shape[1] - columns), bf16)


def outer(left, left_got, right, right_got, line=None, targets=None, small=None):
    tiles = 4
    args = (left, left_got, right, right_got)
    columns = right.shape[1]
    extra = None
    if line is not None:
        args += (targets,)
    if small is not None:
        args += (small,)
        extra = "small"
        columns += 128
    elif columns % 128:
        extra = "zero"
        columns += 128 - columns % 128
    whole = lambda v: pl.BlockSpec(v.shape, lambda i: (0, 0))
    half = shape(HALF // 2, columns)
    tile = pl.BlockSpec((HALF // 2 // tiles, columns), lambda i: (i, 0))
    return call(
        functools.partial(outer_kernel, tiles, line, extra),
        (half, half),
        grid=(tiles,),
        in_specs=[whole(v) for v in args],
        out_specs=(tile, tile),
    )(*args)


def shard_tables():
    table = np.zeros((2, 8, SHARDS), np.int32)
    for core in range(2):
        for number, order in enumerate(ORDERS):
            for place in range(SHARDS):
                here = core ^ (place >> 6)
                mask = (place >> 6) * CORE_BIT
                for step in range(6):
                    if (place >> step) & 1:
                        mask ^= STEP_BITS[order[step // 2]][(step % 2) ^ here]
                table[core, number, place] = mask
    table[:, 3:5] = table[:, 1:3]
    lines = np.repeat(table, ROWS, axis=2)
    return lines, lines.transpose(0, 2, 1).copy(), table.transpose(0, 2, 1).copy()


def prepare_kernel(qkv, attn, expand, reduce, table, gain, shift, level, *outs):
    for target in outs:
        target[...] = jnp.zeros(target.shape, bf16)
    first, second, third = outs
    first[0:15, 0:1440] = qkv[...]
    first[0:15, 1440:1536] = attn[:, 384:480]
    first[0:15, 1536:1920] = attn[:, 0:384]
    second[:, 0:1024] = table[:, 0:1024]
    second[0:15, 1024:2944] = expand[...]
    third[:, 0:896] = table[:, 1024:1920]
    third[0:15, 896:2816] = reduce[...]
    for number, ref in enumerate((gain, shift, level)):
        for row in range(2):
            start = (2 * number + row) * 15
            first[15:16, start : start + 15] = ref[row : row + 1, :]


def prepare(*args):
    vmem = pl.BlockSpec(memory_space=pltpu.VMEM)
    return call(
        prepare_kernel,
        (shape(16, 1920), shape(16, 2944), shape(16, 2816)),
        in_specs=[vmem] * 8,
        out_specs=[vmem] * 3,
    )(*args)


def places_kernel(here, codes_line, lines, columns, shards, targets, target_columns, shard_column, codes):
    me, core = here[0], here[1]

    def feature_of(place, inside):
        return jnp.where(inside < 15, place * 15 + inside, -1)

    place = jnp.where(core == 0, lines[0], lines[1]) ^ me
    inside = lax.broadcasted_iota(jnp.int32, place.shape, 1) & 15
    line = lax.broadcasted_iota(jnp.int32, place.shape, 0)
    targets[...] = jnp.where(line < 3, feature_of(place, inside), place * 16 + inside)
    place = jnp.where(core == 0, columns[0], columns[1]) ^ me
    inside = lax.broadcasted_iota(jnp.int32, place.shape, 0) & 15
    target_columns[...] = feature_of(place, inside)
    shard_column[...] = jnp.where(core == 0, shards[0], shards[1]) ^ me
    row = jnp.right_shift(lax.broadcasted_iota(jnp.int32, (TOKENS, 64), 0), 2)
    column = lax.broadcasted_iota(jnp.int32, (TOKENS, 64), 1)
    spread = jnp.where(row == column, codes_line[...], 0)
    codes[...] = jnp.sum(spread, axis=1, keepdims=True)


def places(here, codes_line):
    vmem = pl.BlockSpec(memory_space=pltpu.VMEM)
    i32 = jnp.int32
    return call(
        places_kernel,
        (shape(8, 2048, i32), shape(2048, 8, i32), shape(SHARDS, 8, i32), shape(TOKENS, 1, i32)),
        in_specs=[pl.BlockSpec(memory_space=pltpu.SMEM)] + [vmem] * 4,
        out_specs=[vmem] * 4,
    )(here, codes_line, *(jnp.asarray(t) for t in shard_tables()))


class Fetch:
    def __init__(self, sources, targets, sem):
        self.copies = [
            pltpu.make_async_copy(source, target, sem.at[i])
            for i, (source, target) in enumerate(zip(sources, targets))
        ]
        self.targets = targets
        for copy in self.copies:
            copy.start()

    def __call__(self, *numbers):
        for number in numbers:
            self.copies[number].wait()
        return [self.targets[number] for number in numbers]


def fetched(arrays):
    return [pltpu.VMEM(v.shape, v.dtype) for v in arrays] + [pltpu.SemaphoreType.DMA((len(arrays),))]


def tail_lanes(value):
    source = lax.broadcasted_iota(jnp.int32, (480, 256), 0)
    target = lax.broadcasted_iota(jnp.int32, (480, 256), 1)
    return dot(value, hot(source, jnp.where(target >= 160, target + 224, -1))).astype(bf16)


def split_refs(refs, *counts):
    out, start = [], 0
    for count in counts:
        out.append(refs[start : start + count])
        start += count
    return out


def each_chunk(columns, body, width=CHUNK):
    @pl.loop(0, columns // width)
    def _(i):
        body(pl.ds(pl.multiple_of(i * width, 128), width))


def each_rows(body):
    @pl.loop(0, TOKENS // ROW_STEP)
    def _(i):
        body(pl.ds(pl.multiple_of(i * ROW_STEP, ROW_STEP), ROW_STEP))


def shuffle(value, targets, line, own, other):
    for half, target in enumerate((own, other)):

        def part(span, half=half, target=target):
            place = targets[line : line + 1, pl.ds(pl.multiple_of(span.start + half * HALF, 128), 256)]
            feature = lax.broadcasted_iota(jnp.int32, (D, 256), 0)
            target[:, span] = dot(value[...], hot(feature, place)).astype(bf16)

        each_chunk(HALF, part, 256)


def unshuffle(value, target_columns, line, out):
    def part(span):
        feature = lax.broadcasted_iota(jnp.int32, (512, CHUNK), 1) + span.start
        total = None
        for k in range(4):
            cut = slice(512 * k, 512 * k + 512)
            place = target_columns[cut, line : line + 1]
            term = dot(value[:, cut], hot(place, feature))
            total = term if total is None else total + term
        out[:, span] = total

    each_chunk(D, part)


def pieces_of(own, other):
    return [ref[:, cut] for ref in (own, other) for cut in (slice(0, 512), slice(512, 1024))]


def row_move(transposed=False):
    row = lax.broadcasted_iota(jnp.int32, (TOKENS, TOKENS), 1 if transposed else 0)
    token = lax.broadcasted_iota(jnp.int32, (TOKENS, TOKENS), 0 if transposed else 1)
    moved = jnp.right_shift(row, 3) * 4 + (row & 3) + (jnp.right_shift(row, 2) & 1) * 128
    return hot(token, moved)


def moments(value):
    average = jnp.mean(value, axis=-1, keepdims=True)
    centered = value - average
    variance = jnp.mean(centered * centered, axis=-1, keepdims=True)
    return centered, lax.rsqrt(variance + epsilon)


def norm_back(value, grad, gain, base):
    centered, scale = moments(value)
    normed = centered * scale
    scaled = grad * gain
    inner = scaled - jnp.mean(scaled, axis=-1, keepdims=True)
    inner = inner - normed * jnp.mean(scaled * normed, axis=-1, keepdims=True)
    return base + scale * inner, grad * normed


def embed_kernel(*refs):
    small, big, outs, scratch = split_refs(refs, 6, 12, 5, len(refs) - 23)
    hidden, codes, level, targets, shard_column, marks = small
    stream, own, other, packed, vectors = outs
    normed = scratch[-1]
    fetch = Fetch(big, scratch[:12], scratch[12])
    tables_a, tables_b, weights = range(0, 4), range(4, 8), range(8, 12)
    for line, numbers, start in ((3, tables_a, 0), (4, tables_b, 1024)):
        table = fetch(*numbers)
        total = None
        for k in range(4):
            term = dot(hot(codes[...], targets[line : line + 1, 512 * k : 512 * k + 512]), table[k][...])
            total = term if total is None else total + term
        stream[:, start : start + table[0].shape[1]] = total
    weight = fetch(*weights)
    chunk = lax.broadcasted_iota(jnp.int32, (SHARDS, 512), 0)
    row = lax.broadcasted_iota(jnp.int32, (SHARDS, 512), 1)
    lines = None
    for k in range(4):
        term = dot(hot(row + 512 * k, chunk * ROWS + 15), weight[k][:, :128])
        lines = term if lines is None else lines + term
    spread = rows_dot(lines.astype(bf16), hot(shard_column[:, 0:1], marks[0:1, :]))
    within = lax.broadcasted_iota(jnp.int32, (SHARDS, 1), 0)
    group = sum((within >= 15 * r).astype(jnp.int32) for r in range(1, 7))
    spread = jnp.where(within - group * 15 == marks[1:2, :], spread, 0.0).astype(bf16)
    number = lax.broadcasted_iota(jnp.int32, (8, SHARDS), 1)
    first = lax.broadcasted_iota(jnp.int32, (8, SHARDS), 0) * 15
    chosen = jnp.where((number >= first) & (number < first + 15), 1.0, 0.0).astype(bf16)
    vectors[...] = dot(chosen, spread)
    level_row = jnp.where(level[0] == 0, vectors[4:5, :], vectors[5:6, :])

    def rows(span):
        value = stream[span, :] + hidden[span, :].astype(f32) + level_row
        stream[span, :] = value
        centered, scale = moments(value)
        normed[span, :] = (centered * scale * vectors[0:1, :] + vectors[2:3, :]).astype(bf16)

    each_rows(rows)
    normed[...] = dot(row_move(), normed[...]).astype(bf16)
    shuffle(normed, targets, 0, own, other)
    packed[...] = sum(dot(p, w[:, 0:1440]) for p, w in zip(pieces_of(own, other), weight)).astype(bf16)


def embed(hidden, codes, level, targets, shard_column, marks, tables_a, tables_b, qkv):
    big = (*tables_a, *tables_b, *qkv)
    vmem = pl.BlockSpec(memory_space=pltpu.VMEM)
    return call(
        embed_kernel,
        (
            shape(TOKENS, D, f32),
            shape(TOKENS, HALF),
            shape(TOKENS, HALF),
            shape(TOKENS, 1440),
            shape(8, D, f32),
        ),
        vmem=48,
        in_specs=[vmem, vmem, pl.BlockSpec(memory_space=pltpu.SMEM), vmem, vmem, vmem]
        + [pl.BlockSpec(memory_space=pl.ANY)] * 12,
        out_specs=[vmem] * 5,
        scratch_shapes=fetched(big) + [pltpu.VMEM((TOKENS, D), bf16)],
    )(hidden, codes, level, targets, shard_column, marks, *big)


def probabilities(columns):
    query, key = columns[:, 0:480], columns[:, 480:960]
    row = lax.broadcasted_iota(jnp.int32, (TOKENS, TOKENS), 0)
    other = lax.broadcasted_iota(jnp.int32, (TOKENS, TOKENS), 1)
    mask = ((row & 3) == (other & 3)) & (jnp.right_shift(row, 2) >= jnp.right_shift(other, 2))
    scores = jnp.where(mask, cols_dot(query, key) * HEAD ** (-0.5), -1e30)
    top = jnp.max(scores, axis=-1, keepdims=True)
    total = top + jnp.log(jnp.sum(jnp.exp(scores - top), axis=-1, keepdims=True))
    return jnp.exp(scores - total)


def attend_kernel(columns, mixed):
    mixed[...] = dot(probabilities(columns).astype(bf16), columns[:, 960:1440]).astype(bf16)


def attend(columns):
    return call(attend_kernel, shape(TOKENS, 480))(columns)


def attend_back_kernel(columns, d_mixed, d_packed):
    probs = probabilities(columns)
    low = probs.astype(bf16)
    d_probs = cols_dot(d_mixed[...], columns[:, 960:1440])
    d_scores = (probs * (d_probs - jnp.sum(probs * d_probs, axis=-1, keepdims=True))).astype(bf16)
    scale = HEAD ** (-0.5)
    d_packed[:, 0:480] = (dot(d_scores, columns[:, 480:960]) * scale).astype(bf16)
    d_packed[:, 480:960] = (rows_dot(d_scores, columns[:, 0:480]) * scale).astype(bf16)
    d_packed[:, 960:1440] = rows_dot(low, d_mixed[...]).astype(bf16)


def attend_back(columns, d_mixed):
    return call(attend_back_kernel, shape(TOKENS, 1440))(columns, d_mixed)


def middle_kernel(*refs):
    small, big, outs, scratch = split_refs(refs, 6, 16, 12, len(refs) - 34)
    mixed_columns, stream, vectors, upstream, targets, target_columns = small
    block_out, d_mid, second_own, second_other, active_own, active_other = outs[:6]
    attn_own, attn_other, d_upward, mixed, d_mixed, sums = outs[6:]
    fetch = Fetch([ref.at[:, 1280:1536] for ref in big[:4]] + list(big[4:]), scratch[:16], scratch[16])
    mid, work, slope, wide, low = scratch[17:]
    rest, attn = fetch(*range(0, 4)), fetch(*range(4, 8))
    mixed[...] = dot(row_move(True), mixed_columns[...]).astype(bf16)
    end = tail_lanes(mixed[...])
    for k in range(4):
        total = cols_dot(mixed[:, 0:384], attn[k][...]) + cols_dot(end, rest[k][...])
        wide[:, 512 * k : 512 * k + 512] = total.astype(bf16)
    unshuffle(wide, target_columns, 0, work)

    def rows_first(span):
        value = stream[span, :] + work[span, :]
        mid[span, :] = value
        centered, scale = moments(value)
        low[span, :] = (centered * scale * vectors[1:2, :] + vectors[3:4, :]).astype(bf16)

    each_rows(rows_first)
    shuffle(low, targets, 1, second_own, second_other)
    expand = fetch(*range(8, 12))

    def up(span):
        parts = zip(pieces_of(second_own, second_other), expand)
        work[:, span] = sum(dot(p, w[:, span]) for p, w in parts)

    each_chunk(D, up)

    def rows_active(span):
        value = work[span, :]
        root = np.float32(np.sqrt(2 / np.pi))
        square = value * value
        bend = jnp.tanh(root * value * (1.0 + 0.044715 * square))
        low[span, :] = (0.5 * value * (1.0 + bend)).astype(bf16)
        inner = root * (1.0 + 3 * 0.044715 * square)
        slope[span, :] = 0.5 * (1.0 + bend) + 0.5 * value * (1.0 - bend * bend) * inner

    each_rows(rows_active)
    shuffle(low, targets, 2, active_own, active_other)
    reduce = fetch(*range(12, 16))

    def down(span):
        parts = zip(pieces_of(active_own, active_other), reduce)
        total = sum(dot(p, w[:, span]) for p, w in parts)
        block_out[:, span] = (mid[:, span] + total).astype(bf16)

    each_chunk(D, down)
    for k in range(4):
        wide[:, 512 * k : 512 * k + 512] = cols_dot(upstream[...], reduce[k][...]).astype(bf16)
    unshuffle(wide, target_columns, 2, work)

    def rows_upward(span):
        d_upward[span, :] = (slope[span, :] * work[span, :]).astype(bf16)

    each_rows(rows_upward)
    for k in range(4):
        wide[:, 512 * k : 512 * k + 512] = cols_dot(d_upward[...], expand[k][...]).astype(bf16)
    unshuffle(wide, target_columns, 1, work)
    sums[...] = jnp.zeros(sums.shape, f32)

    def rows_back(span):
        base = upstream[span, :].astype(f32)
        grad = work[span, :]
        value, gain_part = norm_back(mid[span, :], grad, vectors[1:2, :], base)
        d_mid[span, :] = value
        low[span, :] = value.astype(bf16)
        sums[0:1, :] += jnp.sum(gain_part, axis=0, keepdims=True)
        sums[1:2, :] += jnp.sum(grad, axis=0, keepdims=True)

    each_rows(rows_back)
    shuffle(low, targets, 0, attn_own, attn_other)
    parts = pieces_of(attn_own, attn_other)
    back = sum(dot(p, w[...]) for p, w in zip(parts, attn)).astype(bf16)
    d_mixed[:, 0:384] = dot(row_move(), back).astype(bf16)
    back = sum(dot(p, w[...]) for p, w in zip(parts, rest)).astype(bf16)
    back = dot(row_move(), back).astype(bf16)
    source = lax.broadcasted_iota(jnp.int32, (256, 128), 0)
    target = lax.broadcasted_iota(jnp.int32, (256, 128), 1)
    d_mixed[:, 384:480] = dot(back, hot(source - 160, target))[:, 0:96].astype(bf16)


def middle(mixed_columns, stream, vectors, upstream, targets, target_columns, qkv, attn, expand, reduce):
    big = (*qkv, *attn, *expand, *reduce)
    scratch = [jax.ShapeDtypeStruct((512, 256), bf16)] * 4 + list(big[4:])
    vmem = pl.BlockSpec(memory_space=pltpu.VMEM)
    half = shape(TOKENS, HALF)
    return call(
        middle_kernel,
        (shape(TOKENS, D), shape(TOKENS, D, f32))
        + (half,) * 6
        + (shape(TOKENS, D), shape(TOKENS, 480), shape(TOKENS, 480), shape(8, D, f32)),
        vmem=60,
        in_specs=[vmem] * 6 + [pl.BlockSpec(memory_space=pl.ANY)] * 16,
        out_specs=[vmem] * 12,
        scratch_shapes=fetched(scratch)
        + [pltpu.VMEM((TOKENS, D), f32)] * 3
        + [pltpu.VMEM((TOKENS, 2 * HALF), bf16), pltpu.VMEM((TOKENS, D), bf16)],
    )(mixed_columns, stream, vectors, upstream, targets, target_columns, *big)


def last_kernel(*refs):
    small, big, outs, scratch = split_refs(refs, 9, 4, 4, len(refs) - 17)
    d_packed, stream, d_mid, vectors, sums, level, target_columns, shard_column, marks = small
    d_stream, low_a, low_b, spread = outs
    fetch = Fetch(big, scratch[:4], scratch[4])
    work, wide, totals = scratch[5:]
    weight = fetch(*range(4))
    for k in range(4):
        wide[:, 512 * k : 512 * k + 512] = cols_dot(d_packed[...], weight[k][:, 0:1440]).astype(bf16)
    wide[...] = dot(row_move(True), wide[...]).astype(bf16)
    unshuffle(wide, target_columns, 0, work)
    totals[...] = jnp.zeros(totals.shape, f32)

    def rows(span):
        grad = work[span, :]
        value, gain_part = norm_back(stream[span, :], grad, vectors[0:1, :], d_mid[span, :])
        d_stream[span, :] = value
        low_a[span, :] = value[:, 0:1024].astype(bf16)
        low_b[span, :] = value[:, 1024:1920].astype(bf16)
        totals[0:1, :] += jnp.sum(gain_part, axis=0, keepdims=True)
        totals[2:3, :] += jnp.sum(grad, axis=0, keepdims=True)
        totals[6:7, :] += jnp.sum(value, axis=0, keepdims=True)

    each_rows(rows)
    totals[1:2, :] = sums[0:1, :]
    totals[3:4, :] = sums[1:2, :]
    totals[4:5, :] = jnp.where(level[0] == 0, totals[6:7, :], 0.0)
    totals[5:6, :] = jnp.where(level[0] == 1, totals[6:7, :], 0.0)
    number = lax.broadcasted_iota(jnp.int32, (SHARDS, 8), 0)
    first = lax.broadcasted_iota(jnp.int32, (SHARDS, 8), 1) * 15
    chosen = jnp.where((number >= first) & (number < first + 15) & (number < 90), 1.0, 0.0)
    repeated = dot(chosen.astype(bf16), totals[...].astype(bf16))
    within = lax.broadcasted_iota(jnp.int32, (SHARDS, 1), 0)
    group = sum((within >= 15 * r).astype(jnp.int32) for r in range(1, 7))
    repeated = jnp.where(within - group * 15 == marks[1:2, :], repeated, 0.0).astype(bf16)
    spread[...] = cols_dot(hot(shard_column[:, 2:3], marks[0:1, :]), repeated).astype(bf16)


def last(d_packed, stream, d_mid, vectors, sums, level, target_columns, shard_column, marks, qkv):
    vmem = pl.BlockSpec(memory_space=pltpu.VMEM)
    return call(
        last_kernel,
        (shape(TOKENS, D, f32), shape(TOKENS, 1024), shape(TOKENS, 896), shape(SHARDS, 128)),
        vmem=40,
        in_specs=[vmem] * 5
        + [pl.BlockSpec(memory_space=pltpu.SMEM)]
        + [vmem] * 3
        + [pl.BlockSpec(memory_space=pl.ANY)] * 4,
        out_specs=[vmem] * 4,
        scratch_shapes=fetched(qkv)
        + [
            pltpu.VMEM((TOKENS, D), f32),
            pltpu.VMEM((TOKENS, 2 * HALF), bf16),
            pltpu.VMEM((8, D), f32),
        ],
    )(d_packed, stream, d_mid, vectors, sums, level, target_columns, shard_column, marks, *qkv)


def finish_kernel(kept0, got0, kept1, got1, kept2, got2, *outs):
    grad_qkv, grad_attn, grad_expand, grad_reduce, table, levels, gains, shifts = outs

    def total(kept, got, start, stop):
        return kept[:, start:stop].astype(f32) + got[:, start:stop].astype(f32)

    grad_attn[...] = total(kept0, got0, 0, 480)[:15]
    grad_qkv[...] = total(kept0, got0, 512, 1952)[:15]
    grad_expand[...] = total(kept1, got1, 0, 1920)[:15]
    table[:, 0:1024] = total(kept1, got1, 1920, 2944)
    grad_reduce[...] = total(kept2, got2, 0, 1920)[:15]
    table[:, 1024:1920] = total(kept2, got2, 1920, 2816)
    line = total(kept2, got2, 2816, 2944)[0:1]
    for target, first in ((gains, 0), (shifts, 2), (levels, 4)):
        for row in range(2):
            start = (first + row) * 15
            target[row : row + 1, :] = line[:, start : start + 15]


def finish(*pairs):
    vmem = pl.BlockSpec(memory_space=pltpu.VMEM)
    return call(
        finish_kernel,
        tuple(
            shape(*s, f32)
            for s in ((15, 1440), (15, 480), (15, D), (15, D), (16, D), (2, 15), (2, 15), (2, 15))
        ),
        in_specs=[vmem] * 6,
        out_specs=[vmem] * 8,
    )(*pairs)


def body(
    hidden_in,
    cond_codes,
    level_ids,
    qkv_weight,
    attn_out_weight,
    mlp_in_weight,
    mlp_out_weight,
    code_table,
    level_table,
    norm_gain,
    norm_bias,
    grad_out,
):
    yl, co, yh, z, x = (lax.axis_index(name) for name in AXES)
    me = yl * 64 + co * 32 + yh * 16 + z * 4 + x
    targets, target_columns, shard_column, codes = places(jnp.stack((me, co)), cond_codes)
    shards = prepare(
        qkv_weight,
        attn_out_weight.T,
        mlp_in_weight,
        mlp_out_weight,
        code_table,
        norm_gain,
        norm_bias,
        level_table,
    )
    feature = np.arange(D, dtype=np.int32)
    marks = jnp.asarray(np.stack((feature // 15, feature % 15)))

    small = [join(buf, exchange(buf, order, 0)) for buf, order in zip(shards, ORDERS)]
    small, (targets, target_columns, shard_column, codes) = lax.optimization_barrier(
        (small, (targets, target_columns, shard_column, codes))
    )
    for step in (1, 2):
        small = [join(buf, exchange(buf, order, step)) for buf, order in zip(small, ORDERS)]
    small = [
        join(buf, exchange(buf, order, 3), ((0, split), (split, buf.shape[1])))
        for buf, order, split in zip(small, ORDERS, SPLITS)
    ]
    halves = [join(buf, exchange(buf, order, 4)) for (buf, _), order in zip(small, ORDERS)]
    rests = [exchange(half, order, 5) for half, order in zip(halves, ORDERS)]
    pieces = [(h, r, swap_cores(h), swap_cores(r)) for h, r in zip(halves, rests)]
    pieces, small = lax.optimization_barrier((pieces, [buf for _, buf in small]))
    qkv, table_a, table_b = pieces
    halves = [join(buf, exchange(buf, order, 4)) for buf, order in zip(small, ORDERS)]

    stream, first_own, first_other, packed, vectors = embed(
        hidden_in[0], codes, level_ids, targets, shard_column, marks, table_a, table_b, qkv
    )
    packed, halves = lax.optimization_barrier((packed, halves))
    rests = [exchange(half, order, 5) for half, order in zip(halves, ORDERS)]
    attn, expand, reduce = [(h, r, swap_cores(h), swap_cores(r)) for h, r in zip(halves, rests)]

    def over_blocks(value):
        return lax.all_to_all(value, BLK, split_axis=0, concat_axis=0, tiled=True)

    columns = over_blocks(packed)
    mixed = over_blocks(attend(columns))
    upstream = grad_out[0]
    (
        block_out,
        d_mid,
        second_own,
        second_other,
        active_own,
        active_other,
        attn_own,
        attn_other,
        d_upward,
        mixed,
        d_mixed,
        sums,
    ) = middle(mixed, stream, vectors, upstream, targets, target_columns, qkv, attn, expand, reduce)
    d_mixed = over_blocks(d_mixed)
    early = [
        outer(own, swap_cores(other), right, swap_cores(right))
        for own, other, right in (
            (attn_own, attn_other, mixed),
            (second_own, second_other, d_upward),
            (active_own, active_other, upstream),
        )
    ]
    early_got = [exchange(sent, order, 5) for (_, sent), order in zip(early, ORDERS)]
    first_got = swap_cores(first_other)
    codes_got = swap_cores(codes)

    d_packed = attend_back(columns, d_mixed)
    d_packed, early_got = lax.optimization_barrier((d_packed, early_got))
    d_packed = over_blocks(d_packed)
    early = [add_halves(kept, got) for (kept, _), got in zip(early, early_got)]
    d_packed, early = lax.optimization_barrier((d_packed, early))
    early_got = [exchange(sent, order, 4) for (_, sent), order in zip(early, ORDERS)]
    qkv_grad = outer(first_own, first_got, d_packed, swap_cores(d_packed))
    d_packed, qkv_grad = lax.optimization_barrier((d_packed, qkv_grad))

    d_stream, low_a, low_b, small = last(
        d_packed, stream, d_mid, vectors, sums, level_ids, target_columns, shard_column, marks, qkv
    )
    small = small[:64] + swap_cores(small[64:])
    grad_a = outer(codes, codes_got, low_a, swap_cores(low_a), 3, targets)
    grad_b = outer(codes, codes_got, low_b, swap_cores(low_b), 4, targets, small)
    pairs = []
    for (kept, sent), (before, _), before_got, order in zip(
        (qkv_grad, grad_a, grad_b), early, early_got, ORDERS
    ):
        kept, sent = add_halves(kept, exchange(sent, order, 5))
        kept, sent = merge_halves(before, before_got, kept, exchange(sent, order, 4))
        for step in (3, 2, 1):
            kept, sent = add_halves(kept, exchange(sent, order, step))
        pairs += [kept, exchange(sent, order, 0)]
    grad_qkv, grad_attn, grad_expand, grad_reduce, grad_table, levels, gains, shifts = finish(*pairs)
    return (
        block_out[None],
        d_stream[None],
        grad_qkv,
        grad_attn.T,
        grad_expand,
        grad_reduce,
        grad_table,
        levels,
        gains,
        shifts,
    )


def solution(mesh):
    fine = Mesh(mesh.devices.reshape(2, 2, 2, 4, 4), AXES)
    return jax.shard_map(
        body,
        mesh=fine,
        in_specs=(
            P(WIN, BLK, None),
            P(WIN, BLK),
            P(WIN),
            P(AXES, None),
            P(None, AXES),
            P(AXES, None),
            P(AXES, None),
            P(AXES, None),
            P(None, AXES),
            P(None, AXES),
            P(None, AXES),
            P(WIN, BLK, None),
        ),
        out_specs=(
            P(WIN, BLK, None),
            P(WIN, BLK, None),
            P(AXES, None),
            P(None, AXES),
            P(AXES, None),
            P(AXES, None),
            P(AXES, None),
            P(None, AXES),
            P(None, AXES),
            P(None, AXES),
        ),
        check_vma=False,
    )
```

```python
import functools

import jax
import jax.numpy as jnp
import numpy as np
from jax import lax
from jax.experimental import pallas as pl
from jax.experimental.pallas import tpu as pltpu
from jax.sharding import Mesh, PartitionSpec as P

HEAD = 480
BLOCK = 128
RATIO = 4
D = 1920
SHARDS = 128
ROWS = 16
HALF = 1024
HALVES = (slice(0, HALF), slice(HALF, 2 * HALF))
SPLITS = (1536, 1024, 896)
TOKENS = 256
CHUNK = 640
MIB = 2**20
ROW_STEP = 32
epsilon = 1e-05
bf16 = jnp.bfloat16
f32 = jnp.float32
AXES = ("yl", "co", "yh", "z", "x")
WIN = ("yl", "co")
BLK = ("yh", "z", "x")
STEP_BITS = {"x": (1, 3), "z": (4, 12), "y": (64, 80)}
CORE_BIT = 32
ORDERS = (("x", "z", "y"), ("z", "y", "x"), ("y", "x", "z"))


def exchange(value, order, step):
    masks = STEP_BITS[order[step // 2]]
    pairs = [(i, i ^ masks[(step % 2) ^ ((i >> 5) & 1)]) for i in range(SHARDS)]
    return lax.ppermute(value, AXES, pairs)


def swap_cores(value):
    return lax.ppermute(value, AXES, [(i, i ^ CORE_BIT) for i in range(SHARDS)])


def call(kernel, out_shape, vmem=32, flops=0, **options):
    params = pltpu.CompilerParams(vmem_limit_bytes=vmem * MIB)

    def run(*args):
        outs = out_shape if isinstance(out_shape, tuple) else (out_shape,)
        size = sum(v.size * v.dtype.itemsize for v in args + outs)
        cost = pl.CostEstimate(flops=int(flops), bytes_accessed=size, transcendentals=0)
        return pl.pallas_call(
            kernel, out_shape=out_shape, compiler_params=params, cost_estimate=cost, **options
        )(*args)

    return run


def whole(v):
    return pl.BlockSpec(
        v.shape, lambda i: (0,) * len(v.shape), pipeline_mode=pl.Buffered(buffer_count=1)
    )


def outs_whole(shapes):
    return tuple(pl.BlockSpec(v.shape, lambda i: (0, 0)) for v in shapes)


def shape(rows, columns, dtype=bf16):
    return jax.ShapeDtypeStruct((rows, columns), dtype)


def dot(left, right):
    return jnp.dot(left, right, preferred_element_type=f32)


def rows_dot(left, right):
    return lax.dot_general(left, right, (((0,), (0,)), ((), ())), preferred_element_type=f32)


def cols_dot(left, right):
    return lax.dot_general(left, right, (((1,), (1,)), ((), ())), preferred_element_type=f32)


def hot(left, right):
    return jnp.where(left == right, 1.0, 0.0).astype(bf16)


def join_kernel(tiles, cuts, *refs):
    count = len(cuts)
    sources, targets = refs[: 2 * count], list(refs[2 * count :])
    step = pl.program_id(0)
    for i, spans in enumerate(cuts):
        mine, targets = targets[: len(spans)], targets[len(spans) :]
        for source, here in ((sources[2 * i], step < tiles), (sources[2 * i + 1], step >= tiles)):

            @pl.when(here)
            def _(source=source, mine=mine, spans=spans):
                for target, (start, stop) in zip(mine, spans):
                    target[...] = source[:, start:stop]


def join(firsts, seconds, cuts=None):
    rows = firsts[0].shape[0]
    cuts = cuts or [((0, v.shape[1]),) for v in firsts]
    tiles = max(rows // 128, 1)
    tile = rows // tiles
    specs, args = [], []
    for first, second in zip(firsts, seconds):
        columns = first.shape[1]
        specs += [
            pl.BlockSpec((tile, columns), lambda i: (jnp.minimum(i, tiles - 1), 0)),
            pl.BlockSpec((tile, columns), lambda i: (jnp.maximum(i - tiles, 0), 0)),
        ]
        args += [first, second]
    widths = [stop - start for spans in cuts for start, stop in spans]
    out = call(
        functools.partial(join_kernel, tiles, cuts),
        tuple(shape(2 * rows, width) for width in widths),
        grid=(2 * tiles,),
        in_specs=specs,
        out_specs=tuple(pl.BlockSpec((tile, width), lambda i: (i, 0)) for width in widths),
    )(*args)
    out = list(out)
    return [[out.pop(0) for _ in spans] for spans in cuts]


def add_kernel(counts, *refs):
    arrays = sum(counts)
    sources, targets = refs[: 4 * arrays], refs[4 * arrays :]
    number = 0
    for i, count in enumerate(counts):
        start = 0
        for _ in range(count):
            kept_low, kept_high, got_low, got_high = sources[4 * number : 4 * number + 4]
            span = slice(start, start + kept_low.shape[1])
            targets[2 * i][:, span] = (kept_low[...].astype(f32) + got_low[...].astype(f32)).astype(bf16)
            targets[2 * i + 1][:, span] = (
                kept_high[...].astype(f32) + got_high[...].astype(f32)
            ).astype(bf16)
            start, number = span.stop, number + 1


def add_halves(groups):
    rows = groups[0][0][0].shape[0] // 2
    tiles = max(rows // 128, 1)
    tile = rows // tiles
    specs, args, widths = [], [], []
    for group in groups:
        for kept, got in group:
            columns = kept.shape[1]
            low = pl.BlockSpec((tile, columns), lambda i: (i, 0))
            high = pl.BlockSpec((tile, columns), lambda i: (i + tiles, 0))
            specs += [low, high, low, high]
            args += [kept, kept, got, got]
        widths.append(sum(kept.shape[1] for kept, _ in group))
    out = call(
        functools.partial(add_kernel, [len(group) for group in groups]),
        tuple(shape(rows, width) for width in widths for _ in range(2)),
        vmem=48,
        grid=(tiles,),
        in_specs=specs,
        out_specs=tuple(pl.BlockSpec((tile, width), lambda i: (i, 0)) for width in widths for _ in range(2)),
    )(*args)
    return [(out[2 * i], out[2 * i + 1]) for i in range(len(groups))]


def outer_kernel(tiles, line, extra, left, left_got, right, right_got, *refs):
    kept, sent = refs[-2:]
    rows = HALF // 2 // tiles
    columns = right.shape[1]
    step = pl.program_id(0)
    for target, base in ((kept, 0), (sent, HALF // 2)):
        start = pl.multiple_of(base + step * rows, rows)
        if line is None:
            one, two = left[:, pl.ds(start, rows)], left_got[:, pl.ds(start, rows)]
        else:
            places_here = refs[0][line : line + 1, pl.ds(start, rows)]
            one, two = hot(left[...], places_here), hot(left_got[...], places_here)
        for cut in range(0, columns, 512):
            span = slice(cut, min(cut + 512, columns))
            total = rows_dot(one, right[:, span]) + rows_dot(two, right_got[:, span])
            target[:, span] = total.astype(bf16)
        if extra == "small":
            row = lax.broadcasted_iota(jnp.int32, (rows, 64), 0) + start
            chunk = lax.broadcasted_iota(jnp.int32, (rows, 64), 1)
            target[:, columns:] = dot(hot(row, chunk * ROWS), refs[1][...]).astype(bf16)
        elif extra == "zero":
            target[:, columns:] = jnp.zeros((rows, target.shape[1] - columns), bf16)


def outer(left, left_got, right, right_got, line=None, targets=None, small=None):
    tiles = 4
    args = (left, left_got, right, right_got)
    columns = right.shape[1]
    extra = None
    if line is not None:
        args += (targets,)
    if small is not None:
        args += (small,)
        extra = "small"
        columns += 128
    elif columns % 128:
        extra = "zero"
        columns += 128 - columns % 128
    half = shape(HALF // 2, columns)
    tile = pl.BlockSpec((HALF // 2 // tiles, columns), lambda i: (i, 0))
    return call(
        functools.partial(outer_kernel, tiles, line, extra),
        (half, half),
        flops=2 * 512 * HALF * columns,
        grid=(tiles,),
        in_specs=[whole(v) for v in args],
        out_specs=(tile, tile),
    )(*args)


def shard_tables():
    table = np.zeros((2, 8, SHARDS), np.int32)
    for core in range(2):
        for number, order in enumerate(ORDERS):
            for place in range(SHARDS):
                here = core ^ (place >> 6)
                mask = (place >> 6) * CORE_BIT
                for step in range(6):
                    if (place >> step) & 1:
                        mask ^= STEP_BITS[order[step // 2]][(step % 2) ^ here]
                table[core, number, place] = mask
    table[:, 3:5] = table[:, 1:3]
    lines = np.repeat(table, ROWS, axis=2)
    return lines, lines.transpose(0, 2, 1).copy(), table.transpose(0, 2, 1).copy()


def prepare_kernel(qkv, attn, expand, reduce, table, gain, shift, level, *outs):
    for target in outs:
        target[...] = jnp.zeros(target.shape, bf16)
    first, second, third = outs
    first[0:15, 0:1440] = qkv[...]
    first[0:15, 1440:1536] = attn[:, 384:480]
    first[0:15, 1536:1920] = attn[:, 0:384]
    second[:, 0:1024] = table[:, 0:1024]
    second[0:15, 1024:2944] = expand[...]
    third[:, 0:896] = table[:, 1024:1920]
    third[0:15, 896:2816] = reduce[...]
    for number, ref in enumerate((gain, shift, level)):
        for row in range(2):
            start = (2 * number + row) * 15
            first[15:16, start : start + 15] = ref[row : row + 1, :]


def prepare(*args):
    outs = (shape(16, 1920), shape(16, 2944), shape(16, 2816))
    return call(
        prepare_kernel,
        outs,
        grid=(1,),
        in_specs=[whole(v) for v in args],
        out_specs=outs_whole(outs),
    )(*args)


def places_kernel(here, codes_line, lines, columns, shards, targets, target_columns, shard_column, codes):
    me, core = here[0], here[1]

    def feature_of(place, inside):
        return jnp.where(inside < 15, place * 15 + inside, -1)

    place = jnp.where(core == 0, lines[0], lines[1]) ^ me
    inside = lax.broadcasted_iota(jnp.int32, place.shape, 1) & 15
    line = lax.broadcasted_iota(jnp.int32, place.shape, 0)
    targets[...] = jnp.where(line < 3, feature_of(place, inside), place * 16 + inside)
    place = jnp.where(core == 0, columns[0], columns[1]) ^ me
    inside = lax.broadcasted_iota(jnp.int32, place.shape, 0) & 15
    target_columns[...] = feature_of(place, inside)
    shard_column[...] = jnp.where(core == 0, shards[0], shards[1]) ^ me
    row = jnp.right_shift(lax.broadcasted_iota(jnp.int32, (TOKENS, 64), 0), 2)
    column = lax.broadcasted_iota(jnp.int32, (TOKENS, 64), 1)
    spread = jnp.where(row == column, codes_line[...], 0)
    codes[...] = jnp.sum(spread, axis=1, keepdims=True)


def places(here, codes_line):
    i32 = jnp.int32
    args = (codes_line, *(jnp.asarray(t) for t in shard_tables()))
    outs = (shape(8, 2048, i32), shape(2048, 8, i32), shape(SHARDS, 8, i32), shape(TOKENS, 1, i32))
    return call(
        places_kernel,
        outs,
        grid=(1,),
        in_specs=[pl.BlockSpec(memory_space=pltpu.SMEM)] + [whole(v) for v in args],
        out_specs=outs_whole(outs),
    )(here, *args)


class Fetch:
    def __init__(self, sources, targets, sem):
        self.copies = [
            pltpu.make_async_copy(source, target, sem.at[i])
            for i, (source, target) in enumerate(zip(sources, targets))
        ]
        self.targets = targets
        for copy in self.copies:
            copy.start()

    def __call__(self, *numbers):
        for number in numbers:
            self.copies[number].wait()
        return [self.targets[number] for number in numbers]


def fetched(arrays):
    return [pltpu.VMEM(v.shape, v.dtype) for v in arrays] + [pltpu.SemaphoreType.DMA((len(arrays),))]


def tail_lanes(value):
    source = lax.broadcasted_iota(jnp.int32, (480, 256), 0)
    target = lax.broadcasted_iota(jnp.int32, (480, 256), 1)
    return dot(value, hot(source, jnp.where(target >= 160, target + 224, -1))).astype(bf16)


def split_refs(refs, *counts):
    out, start = [], 0
    for count in counts:
        out.append(refs[start : start + count])
        start += count
    return out


def each_chunk(columns, body, width=CHUNK):
    @pl.loop(0, columns // width)
    def _(i):
        body(pl.ds(pl.multiple_of(i * width, 128), width))


def each_rows(body):
    @pl.loop(0, TOKENS // ROW_STEP)
    def _(i):
        body(pl.ds(pl.multiple_of(i * ROW_STEP, ROW_STEP), ROW_STEP))


def shuffle(value, targets, line, own, other):
    for half, target in enumerate((own, other)):

        def part(span, half=half, target=target):
            place = targets[line : line + 1, pl.ds(pl.multiple_of(span.start + half * HALF, 128), 256)]
            feature = lax.broadcasted_iota(jnp.int32, (D, 256), 0)
            target[:, span] = dot(value[...], hot(feature, place)).astype(bf16)

        each_chunk(HALF, part, 256)


def unshuffle(value, target_columns, line, out):
    def part(span):
        feature = lax.broadcasted_iota(jnp.int32, (512, CHUNK), 1) + span.start
        total = None
        for k in range(4):
            cut = slice(512 * k, 512 * k + 512)
            place = target_columns[cut, line : line + 1]
            term = dot(value[:, cut], hot(place, feature))
            total = term if total is None else total + term
        out[:, span] = total

    each_chunk(D, part)


def pieces_of(own, other):
    return [ref[:, cut] for ref in (own, other) for cut in (slice(0, 512), slice(512, 1024))]


def row_move(transposed=False):
    row = lax.broadcasted_iota(jnp.int32, (TOKENS, TOKENS), 1 if transposed else 0)
    token = lax.broadcasted_iota(jnp.int32, (TOKENS, TOKENS), 0 if transposed else 1)
    moved = jnp.right_shift(row, 3) * 4 + (row & 3) + (jnp.right_shift(row, 2) & 1) * 128
    return hot(token, moved)


def moments(value):
    average = jnp.mean(value, axis=-1, keepdims=True)
    centered = value - average
    variance = jnp.mean(centered * centered, axis=-1, keepdims=True)
    return centered, lax.rsqrt(variance + epsilon)


def norm_back(value, grad, gain, base):
    centered, scale = moments(value)
    normed = centered * scale
    scaled = grad * gain
    inner = scaled - jnp.mean(scaled, axis=-1, keepdims=True)
    inner = inner - normed * jnp.mean(scaled * normed, axis=-1, keepdims=True)
    return base + scale * inner, grad * normed


def embed_kernel(*refs):
    small, big, outs, scratch = split_refs(refs, 6, 12, 5, len(refs) - 23)
    level, hidden, codes, targets, shard_column, marks = small
    stream, own, other, packed, vectors = outs
    normed = scratch[-1]
    fetch = Fetch(big, scratch[:12], scratch[12])
    tables_a, tables_b, weights = range(0, 4), range(4, 8), range(8, 12)
    for line, numbers, start in ((3, tables_a, 0), (4, tables_b, 1024)):
        table = fetch(*numbers)
        total = None
        for k in range(4):
            term = dot(hot(codes[...], targets[line : line + 1, 512 * k : 512 * k + 512]), table[k][...])
            total = term if total is None else total + term
        stream[:, start : start + table[0].shape[1]] = total
    weight = fetch(*weights)
    chunk = lax.broadcasted_iota(jnp.int32, (SHARDS, 512), 0)
    row = lax.broadcasted_iota(jnp.int32, (SHARDS, 512), 1)
    lines = None
    for k in range(4):
        term = dot(hot(row + 512 * k, chunk * ROWS + 15), weight[k][:, :128])
        lines = term if lines is None else lines + term
    spread = rows_dot(lines.astype(bf16), hot(shard_column[:, 0:1], marks[0:1, :]))
    within = lax.broadcasted_iota(jnp.int32, (SHARDS, 1), 0)
    group = sum((within >= 15 * r).astype(jnp.int32) for r in range(1, 7))
    spread = jnp.where(within - group * 15 == marks[1:2, :], spread, 0.0).astype(bf16)
    number = lax.broadcasted_iota(jnp.int32, (8, SHARDS), 1)
    first = lax.broadcasted_iota(jnp.int32, (8, SHARDS), 0) * 15
    chosen = jnp.where((number >= first) & (number < first + 15), 1.0, 0.0).astype(bf16)
    vectors[...] = dot(chosen, spread)
    level_row = jnp.where(level[0] == 0, vectors[4:5, :], vectors[5:6, :])

    def rows(span):
        value = stream[span, :] + hidden[span, :].astype(f32) + level_row
        stream[span, :] = value
        centered, scale = moments(value)
        normed[span, :] = (centered * scale * vectors[0:1, :] + vectors[2:3, :]).astype(bf16)

    each_rows(rows)
    normed[...] = dot(row_move(), normed[...]).astype(bf16)
    shuffle(normed, targets, 0, own, other)
    packed[...] = sum(dot(p, w[:, 0:1440]) for p, w in zip(pieces_of(own, other), weight)).astype(bf16)


def embed(level, hidden, codes, targets, shard_column, marks, tables_a, tables_b, qkv):
    big = (*tables_a, *tables_b, *qkv)
    args = (hidden, codes, targets, shard_column, marks)
    outs = (
        shape(TOKENS, D, f32),
        shape(TOKENS, HALF),
        shape(TOKENS, HALF),
        shape(TOKENS, 1440),
        shape(8, D, f32),
    )
    return call(
        embed_kernel,
        outs,
        vmem=52,
        flops=8e9,
        grid=(1,),
        in_specs=[pl.BlockSpec(memory_space=pltpu.SMEM)]
        + [whole(v) for v in args]
        + [pl.BlockSpec(memory_space=pl.ANY)] * 12,
        out_specs=outs_whole(outs),
        scratch_shapes=fetched(big) + [pltpu.VMEM((TOKENS, D), bf16)],
    )(level, *args, *big)


def probabilities(columns):
    query, key = columns[:, 0:480], columns[:, 480:960]
    row = lax.broadcasted_iota(jnp.int32, (TOKENS, TOKENS), 0)
    other = lax.broadcasted_iota(jnp.int32, (TOKENS, TOKENS), 1)
    mask = ((row & 3) == (other & 3)) & (jnp.right_shift(row, 2) >= jnp.right_shift(other, 2))
    scores = jnp.where(mask, cols_dot(query, key) * HEAD ** (-0.5), -1e30)
    top = jnp.max(scores, axis=-1, keepdims=True)
    total = top + jnp.log(jnp.sum(jnp.exp(scores - top), axis=-1, keepdims=True))
    return jnp.exp(scores - total)


def attend_kernel(columns, mixed):
    mixed[...] = dot(probabilities(columns).astype(bf16), columns[:, 960:1440]).astype(bf16)


def attend(columns):
    out = shape(TOKENS, 480)
    return call(
        attend_kernel, out, grid=(1,), in_specs=[whole(columns)], out_specs=whole(out)
    )(columns)


def attend_back_kernel(columns, d_mixed, d_packed):
    probs = probabilities(columns)
    low = probs.astype(bf16)
    d_probs = cols_dot(d_mixed[...], columns[:, 960:1440])
    d_scores = (probs * (d_probs - jnp.sum(probs * d_probs, axis=-1, keepdims=True))).astype(bf16)
    scale = HEAD ** (-0.5)
    d_packed[:, 0:480] = (dot(d_scores, columns[:, 480:960]) * scale).astype(bf16)
    d_packed[:, 480:960] = (rows_dot(d_scores, columns[:, 0:480]) * scale).astype(bf16)
    d_packed[:, 960:1440] = rows_dot(low, d_mixed[...]).astype(bf16)
    d_packed[:, 1440:1536] = jnp.zeros((TOKENS, 96), bf16)


def attend_back(columns, d_mixed):
    out = shape(TOKENS, 1536)
    return call(
        attend_back_kernel,
        out,
        grid=(1,),
        in_specs=[whole(columns), whole(d_mixed)],
        out_specs=whole(out),
    )(columns, d_mixed)


def middle_kernel(*refs):
    small, big, outs, scratch = split_refs(refs, 6, 16, 12, len(refs) - 34)
    mixed_columns, stream, vectors, upstream, targets, target_columns = small
    block_out, d_mid, second_own, second_other, active_own, active_other = outs[:6]
    attn_own, attn_other, d_upward, mixed, d_mixed, sums = outs[6:]
    fetch = Fetch([ref.at[:, 1280:1536] for ref in big[:4]] + list(big[4:]), scratch[:16], scratch[16])
    mid, work, slope, wide, low = scratch[17:]
    rest, attn = fetch(*range(0, 4)), fetch(*range(4, 8))
    mixed[:, 480:512] = jnp.zeros((TOKENS, 32), bf16)
    mixed[:, 0:480] = dot(row_move(True), mixed_columns[...]).astype(bf16)
    end = tail_lanes(mixed[:, 0:480])
    for k in range(4):
        total = cols_dot(mixed[:, 0:384], attn[k][...]) + cols_dot(end, rest[k][...])
        wide[:, 512 * k : 512 * k + 512] = total.astype(bf16)
    unshuffle(wide, target_columns, 0, work)

    def rows_first(span):
        value = stream[span, :] + work[span, :]
        mid[span, :] = value
        centered, scale = moments(value)
        low[span, :] = (centered * scale * vectors[1:2, :] + vectors[3:4, :]).astype(bf16)

    each_rows(rows_first)
    shuffle(low, targets, 1, second_own, second_other)
    expand = fetch(*range(8, 12))

    def up(span):
        parts = zip(pieces_of(second_own, second_other), expand)
        work[:, span] = sum(dot(p, w[:, span]) for p, w in parts)

    each_chunk(D, up)

    def rows_active(span):
        value = work[span, :]
        root = np.float32(np.sqrt(2 / np.pi))
        square = value * value
        bend = jnp.tanh(root * value * (1.0 + 0.044715 * square))
        low[span, :] = (0.5 * value * (1.0 + bend)).astype(bf16)
        inner = root * (1.0 + 3 * 0.044715 * square)
        slope[span, :] = 0.5 * (1.0 + bend) + 0.5 * value * (1.0 - bend * bend) * inner

    each_rows(rows_active)
    shuffle(low, targets, 2, active_own, active_other)
    reduce = fetch(*range(12, 16))

    def down(span):
        parts = zip(pieces_of(active_own, active_other), reduce)
        total = sum(dot(p, w[:, span]) for p, w in parts)
        block_out[:, span] = (mid[:, span] + total).astype(bf16)

    each_chunk(D, down)
    for k in range(4):
        wide[:, 512 * k : 512 * k + 512] = cols_dot(upstream[...], reduce[k][...]).astype(bf16)
    unshuffle(wide, target_columns, 2, work)

    def rows_upward(span):
        d_upward[span, :] = (slope[span, :] * work[span, :]).astype(bf16)

    each_rows(rows_upward)
    for k in range(4):
        wide[:, 512 * k : 512 * k + 512] = cols_dot(d_upward[...], expand[k][...]).astype(bf16)
    unshuffle(wide, target_columns, 1, work)
    sums[...] = jnp.zeros(sums.shape, f32)

    def rows_back(span):
        base = upstream[span, :].astype(f32)
        grad = work[span, :]
        value, gain_part = norm_back(mid[span, :], grad, vectors[1:2, :], base)
        d_mid[span, :] = value
        low[span, :] = value.astype(bf16)
        sums[0:1, :] += jnp.sum(gain_part, axis=0, keepdims=True)
        sums[1:2, :] += jnp.sum(grad, axis=0, keepdims=True)

    each_rows(rows_back)
    shuffle(low, targets, 0, attn_own, attn_other)
    parts = pieces_of(attn_own, attn_other)
    back = sum(dot(p, w[...]) for p, w in zip(parts, attn)).astype(bf16)
    d_mixed[:, 0:384] = dot(row_move(), back).astype(bf16)
    back = sum(dot(p, w[...]) for p, w in zip(parts, rest)).astype(bf16)
    back = dot(row_move(), back).astype(bf16)
    source = lax.broadcasted_iota(jnp.int32, (256, 128), 0)
    target = lax.broadcasted_iota(jnp.int32, (256, 128), 1)
    d_mixed[:, 384:480] = dot(back, hot(source - 160, target))[:, 0:96].astype(bf16)


def middle(mixed_columns, stream, vectors, upstream, targets, target_columns, qkv, attn, expand, reduce):
    big = (*qkv, *attn, *expand, *reduce)
    scratch = [jax.ShapeDtypeStruct((512, 256), bf16)] * 4 + list(big[4:])
    args = (mixed_columns, stream, vectors, upstream, targets, target_columns)
    half = shape(TOKENS, HALF)
    outs = (
        (shape(TOKENS, D), shape(TOKENS, D, f32))
        + (half,) * 6
        + (shape(TOKENS, D), shape(TOKENS, 512), shape(TOKENS, 480), shape(8, D, f32))
    )
    return call(
        middle_kernel,
        outs,
        vmem=60,
        flops=25e9,
        grid=(1,),
        in_specs=[whole(v) for v in args] + [pl.BlockSpec(memory_space=pl.ANY)] * 16,
        out_specs=tuple(whole(v) for v in outs),
        scratch_shapes=fetched(scratch)
        + [pltpu.VMEM((TOKENS, D), f32)] * 3
        + [pltpu.VMEM((TOKENS, 2 * HALF), bf16), pltpu.VMEM((TOKENS, D), bf16)],
    )(*args, *big)


def last_kernel(*refs):
    small, big, outs, scratch = split_refs(refs, 9, 4, 4, len(refs) - 17)
    level, d_packed, stream, d_mid, vectors, sums, target_columns, shard_column, marks = small
    d_stream, low_a, low_b, spread = outs
    fetch = Fetch(big, scratch[:4], scratch[4])
    work, wide, totals = scratch[5:]
    weight = fetch(*range(4))
    for k in range(4):
        wide[:, 512 * k : 512 * k + 512] = cols_dot(d_packed[:, 0:1440], weight[k][:, 0:1440]).astype(bf16)
    wide[...] = dot(row_move(True), wide[...]).astype(bf16)
    unshuffle(wide, target_columns, 0, work)
    totals[...] = jnp.zeros(totals.shape, f32)

    def rows(span):
        grad = work[span, :]
        value, gain_part = norm_back(stream[span, :], grad, vectors[0:1, :], d_mid[span, :])
        d_stream[span, :] = value
        low_a[span, :] = value[:, 0:1024].astype(bf16)
        low_b[span, :] = value[:, 1024:1920].astype(bf16)
        totals[0:1, :] += jnp.sum(gain_part, axis=0, keepdims=True)
        totals[2:3, :] += jnp.sum(grad, axis=0, keepdims=True)
        totals[6:7, :] += jnp.sum(value, axis=0, keepdims=True)

    each_rows(rows)
    totals[1:2, :] = sums[0:1, :]
    totals[3:4, :] = sums[1:2, :]
    totals[4:5, :] = jnp.where(level[0] == 0, totals[6:7, :], 0.0)
    totals[5:6, :] = jnp.where(level[0] == 1, totals[6:7, :], 0.0)
    number = lax.broadcasted_iota(jnp.int32, (SHARDS, 8), 0)
    first = lax.broadcasted_iota(jnp.int32, (SHARDS, 8), 1) * 15
    chosen = jnp.where((number >= first) & (number < first + 15) & (number < 90), 1.0, 0.0)
    repeated = dot(chosen.astype(bf16), totals[...].astype(bf16))
    within = lax.broadcasted_iota(jnp.int32, (SHARDS, 1), 0)
    group = sum((within >= 15 * r).astype(jnp.int32) for r in range(1, 7))
    repeated = jnp.where(within - group * 15 == marks[1:2, :], repeated, 0.0).astype(bf16)
    spread[...] = cols_dot(hot(shard_column[:, 2:3], marks[0:1, :]), repeated).astype(bf16)


def last(level, d_packed, stream, d_mid, vectors, sums, target_columns, shard_column, marks, qkv):
    args = (d_packed, stream, d_mid, vectors, sums, target_columns, shard_column, marks)
    outs = (shape(TOKENS, D, f32), shape(TOKENS, 1024), shape(TOKENS, 896), shape(SHARDS, 128))
    return call(
        last_kernel,
        outs,
        vmem=48,
        flops=6e9,
        grid=(1,),
        in_specs=[pl.BlockSpec(memory_space=pltpu.SMEM)]
        + [whole(v) for v in args]
        + [pl.BlockSpec(memory_space=pl.ANY)] * 4,
        out_specs=tuple(whole(v) for v in outs),
        scratch_shapes=fetched(qkv)
        + [
            pltpu.VMEM((TOKENS, D), f32),
            pltpu.VMEM((TOKENS, 2 * HALF), bf16),
            pltpu.VMEM((8, D), f32),
        ],
    )(level, *args, *qkv)


def finish_kernel(kept0, got0, kept1, got1, kept2, got2, *outs):
    grad_qkv, grad_attn, grad_expand, grad_reduce, table, levels, gains, shifts = outs

    def total(kept, got, start, stop):
        return kept[:, start:stop].astype(f32) + got[:, start:stop].astype(f32)

    grad_attn[...] = total(kept0, got0, 0, 480)[:15]
    grad_qkv[...] = total(kept0, got0, 512, 1952)[:15]
    grad_expand[...] = total(kept1, got1, 0, 1920)[:15]
    table[:, 0:1024] = total(kept1, got1, 1920, 2944)
    grad_reduce[...] = total(kept2, got2, 0, 1920)[:15]
    table[:, 1024:1920] = total(kept2, got2, 1920, 2816)
    line = total(kept2, got2, 2816, 2944)[0:1]
    for target, first in ((gains, 0), (shifts, 2), (levels, 4)):
        for row in range(2):
            start = (first + row) * 15
            target[row : row + 1, :] = line[:, start : start + 15]


def finish(*pairs):
    outs = tuple(
        shape(*s, f32)
        for s in ((15, 1440), (15, 480), (15, D), (15, D), (16, D), (2, 15), (2, 15), (2, 15))
    )
    return call(
        finish_kernel,
        outs,
        grid=(1,),
        in_specs=[whole(v) for v in pairs],
        out_specs=outs_whole(outs),
    )(*pairs)


def body(
    hidden_in,
    cond_codes,
    level_ids,
    qkv_weight,
    attn_out_weight,
    mlp_in_weight,
    mlp_out_weight,
    code_table,
    level_table,
    norm_gain,
    norm_bias,
    grad_out,
):
    yl, co, yh, z, x = (lax.axis_index(name) for name in AXES)
    me = yl * 64 + co * 32 + yh * 16 + z * 4 + x
    targets, target_columns, shard_column, codes = places(jnp.stack((me, co)), cond_codes)
    shards = prepare(
        qkv_weight,
        attn_out_weight.T,
        mlp_in_weight,
        mlp_out_weight,
        code_table,
        norm_gain,
        norm_bias,
        level_table,
    )
    feature = np.arange(D, dtype=np.int32)
    marks = jnp.asarray(np.stack((feature // 15, feature % 15)))

    def exchanged(values, step):
        return [exchange(v, order, step) for v, order in zip(values, ORDERS)]

    def singles(lists):
        return [v for (v,) in lists]

    small = singles(join(shards, exchanged(shards, 0)))
    small, (targets, target_columns, shard_column, codes) = lax.optimization_barrier(
        (small, (targets, target_columns, shard_column, codes))
    )
    for step in (1, 2):
        small = singles(join(small, exchanged(small, step)))
    cuts = [((0, split), (split, v.shape[1])) for v, split in zip(small, SPLITS)]
    small = join(small, exchanged(small, 3), cuts)
    first, second = [v for v, _ in small], [v for _, v in small]
    first = singles(join(first, exchanged(first, 4)))
    first, second = lax.optimization_barrier((first, second))
    rests = exchanged(first, 5)
    second_got = exchanged(second, 4)
    pieces = [(h, r, swap_cores(h), swap_cores(r)) for h, r in zip(first, rests)]
    second = singles(join(second, second_got))
    pieces, second = lax.optimization_barrier((pieces, second))
    qkv, table_a, table_b = pieces
    rests = exchanged(second, 5)

    stream, first_own, first_other, packed, vectors = embed(
        level_ids, hidden_in[0], codes, targets, shard_column, marks, table_a, table_b, qkv
    )

    def over_blocks(value):
        return lax.all_to_all(value, BLK, split_axis=0, concat_axis=0, tiled=True)

    columns = over_blocks(packed)
    mixed = attend(columns)
    mixed, rests = lax.optimization_barrier((mixed, rests))
    mixed = over_blocks(mixed)
    attn, expand, reduce = [(h, r, swap_cores(h), swap_cores(r)) for h, r in zip(second, rests)]
    upstream = grad_out[0]
    (
        block_out,
        d_mid,
        second_own,
        second_other,
        active_own,
        active_other,
        attn_own,
        attn_other,
        d_upward,
        mixed,
        d_mixed,
        sums,
    ) = middle(mixed, stream, vectors, upstream, targets, target_columns, qkv, attn, expand, reduce)
    d_mixed = over_blocks(d_mixed)
    early = [
        outer(own, swap_cores(other), right, swap_cores(right))
        for own, other, right in (
            (attn_own, attn_other, mixed),
            (second_own, second_other, d_upward),
            (active_own, active_other, upstream),
        )
    ]
    early_got = exchanged([sent for _, sent in early], 5)
    first_got = swap_cores(first_other)
    codes_got = swap_cores(codes)

    d_packed = over_blocks(attend_back(columns, d_mixed))
    early = add_halves([[(kept, got)] for (kept, _), got in zip(early, early_got)])
    d_packed, early = lax.optimization_barrier((d_packed, early))
    early_got = exchanged([sent for _, sent in early], 4)
    qkv_grad = outer(first_own, first_got, d_packed, swap_cores(d_packed))
    d_packed, qkv_grad = lax.optimization_barrier((d_packed, qkv_grad))

    d_stream, low_a, low_b, small = last(
        level_ids, d_packed, stream, d_mid, vectors, sums, target_columns, shard_column, marks, qkv
    )
    small = small[:64] + swap_cores(small[64:])
    grad_a = outer(codes, codes_got, low_a, swap_cores(low_a), 3, targets)
    grad_b = outer(codes, codes_got, low_b, swap_cores(low_b), 4, targets, small)
    late = [qkv_grad, grad_a, grad_b]
    late_got = exchanged([sent for _, sent in late], 5)
    late = add_halves([[(kept, got)] for (kept, _), got in zip(late, late_got)])
    late_got = exchanged([sent for _, sent in late], 4)
    sums = add_halves(
        [
            [(before, before_got), (kept, got)]
            for (before, _), before_got, (kept, _), got in zip(early, early_got, late, late_got)
        ]
    )
    for step in (3, 2, 1):
        got = exchanged([sent for _, sent in sums], step)
        sums = add_halves([[(kept, v)] for (kept, _), v in zip(sums, got)])
    got = exchanged([sent for _, sent in sums], 0)
    pairs = [v for (kept, _), mine in zip(sums, got) for v in (kept, mine)]
    grad_qkv, grad_attn, grad_expand, grad_reduce, grad_table, levels, gains, shifts = finish(*pairs)
    return (
        block_out[None],
        d_stream[None],
        grad_qkv,
        grad_attn.T,
        grad_expand,
        grad_reduce,
        grad_table,
        levels,
        gains,
        shifts,
    )


def solution(mesh):
    fine = Mesh(mesh.devices.reshape(2, 2, 2, 4, 4), AXES)
    return jax.shard_map(
        body,
        mesh=fine,
        in_specs=(
            P(WIN, BLK, None),
            P(WIN, BLK),
            P(WIN),
            P(AXES, None),
            P(None, AXES),
            P(AXES, None),
            P(AXES, None),
            P(AXES, None),
            P(None, AXES),
            P(None, AXES),
            P(None, AXES),
            P(WIN, BLK, None),
        ),
        out_specs=(
            P(WIN, BLK, None),
            P(WIN, BLK, None),
            P(AXES, None),
            P(None, AXES),
            P(AXES, None),
            P(AXES, None),
            P(AXES, None),
            P(None, AXES),
            P(None, AXES),
            P(None, AXES),
        ),
        check_vma=False,
    )
```

```python
import functools

import jax
import jax.numpy as jnp
import numpy as np
from jax import lax
from jax.experimental import pallas as pl
from jax.experimental.pallas import tpu as pltpu
from jax.sharding import Mesh, PartitionSpec as P

HEAD = 480
BLOCK = 128
RATIO = 4
D = 1920
SHARDS = 128
ROWS = 16
HALF = 1024
HALVES = (slice(0, HALF), slice(HALF, 2 * HALF))
SPLITS = (1536, 1024, 896)
TOKENS = 256
CHUNK = 640
MIB = 2**20
ROW_STEP = 32
epsilon = 1e-05
bf16 = jnp.bfloat16
f32 = jnp.float32
AXES = ("yl", "co", "yh", "z", "x")
WIN = ("yl", "co")
BLK = ("yh", "z", "x")
STEP_BITS = {"x": (1, 3), "z": (4, 12), "y": (64, 80)}
CORE_BIT = 32
ORDERS = (("x", "z", "y"), ("z", "y", "x"), ("y", "x", "z"))


def exchange(value, order, step):
    masks = STEP_BITS[order[step // 2]]
    pairs = [(i, i ^ masks[(step % 2) ^ ((i >> 5) & 1)]) for i in range(SHARDS)]
    return lax.ppermute(value, AXES, pairs)


def swap_cores(value):
    return lax.ppermute(value, AXES, [(i, i ^ CORE_BIT) for i in range(SHARDS)])


def call(kernel, out_shape, vmem=60, flops=0, **options):
    params = pltpu.CompilerParams(vmem_limit_bytes=vmem * MIB)

    def run(*args):
        outs = out_shape if isinstance(out_shape, tuple) else (out_shape,)
        size = sum(v.size * v.dtype.itemsize for v in args + outs)
        cost = pl.CostEstimate(flops=int(flops), bytes_accessed=size, transcendentals=0)
        return pl.pallas_call(
            kernel, out_shape=out_shape, compiler_params=params, cost_estimate=cost, **options
        )(*args)

    return run


def whole(v):
    return pl.BlockSpec(
        v.shape, lambda i: (0,) * len(v.shape), pipeline_mode=pl.Buffered(buffer_count=1)
    )


def outs_whole(shapes):
    return tuple(pl.BlockSpec(v.shape, lambda i: (0, 0)) for v in shapes)


def shape(rows, columns, dtype=bf16):
    return jax.ShapeDtypeStruct((rows, columns), dtype)


def dot(left, right):
    return jnp.dot(left, right, preferred_element_type=f32)


def rows_dot(left, right):
    return lax.dot_general(left, right, (((0,), (0,)), ((), ())), preferred_element_type=f32)


def cols_dot(left, right):
    return lax.dot_general(left, right, (((1,), (1,)), ((), ())), preferred_element_type=f32)


def hot(left, right):
    return jnp.where(left == right, 1.0, 0.0).astype(bf16)


def join_kernel(tiles, cuts, *refs):
    count = len(cuts)
    sources, targets = refs[: 2 * count], list(refs[2 * count :])
    step = pl.program_id(0)
    for i, spans in enumerate(cuts):
        mine, targets = targets[: len(spans)], targets[len(spans) :]
        for source, here in ((sources[2 * i], step < tiles), (sources[2 * i + 1], step >= tiles)):

            @pl.when(here)
            def _(source=source, mine=mine, spans=spans):
                for target, (start, stop) in zip(mine, spans):
                    target[...] = source[:, start:stop]


def join(firsts, seconds, cuts=None):
    rows = firsts[0].shape[0]
    cuts = cuts or [((0, v.shape[1]),) for v in firsts]
    tiles = max(rows // 128, 1)
    tile = rows // tiles
    specs, args = [], []
    for first, second in zip(firsts, seconds):
        columns = first.shape[1]
        specs += [
            pl.BlockSpec((tile, columns), lambda i: (jnp.minimum(i, tiles - 1), 0)),
            pl.BlockSpec((tile, columns), lambda i: (jnp.maximum(i - tiles, 0), 0)),
        ]
        args += [first, second]
    widths = [stop - start for spans in cuts for start, stop in spans]
    out = call(
        functools.partial(join_kernel, tiles, cuts),
        tuple(shape(2 * rows, width) for width in widths),
        grid=(2 * tiles,),
        in_specs=specs,
        out_specs=tuple(pl.BlockSpec((tile, width), lambda i: (i, 0)) for width in widths),
    )(*args)
    out = list(out)
    return [[out.pop(0) for _ in spans] for spans in cuts]


def add_kernel(counts, *refs):
    arrays = sum(counts)
    sources, targets = refs[: 4 * arrays], refs[4 * arrays :]
    number = 0
    for i, count in enumerate(counts):
        start = 0
        for _ in range(count):
            kept_low, kept_high, got_low, got_high = sources[4 * number : 4 * number + 4]
            span = slice(start, start + kept_low.shape[1])
            targets[2 * i][:, span] = (kept_low[...].astype(f32) + got_low[...].astype(f32)).astype(bf16)
            targets[2 * i + 1][:, span] = (
                kept_high[...].astype(f32) + got_high[...].astype(f32)
            ).astype(bf16)
            start, number = span.stop, number + 1


def add_halves(groups):
    rows = groups[0][0][0].shape[0] // 2
    tiles = max(rows // 128, 1)
    tile = rows // tiles
    specs, args, widths = [], [], []
    for group in groups:
        for kept, got in group:
            columns = kept.shape[1]
            low = pl.BlockSpec((tile, columns), lambda i: (i, 0))
            high = pl.BlockSpec((tile, columns), lambda i: (i + tiles, 0))
            specs += [low, high, low, high]
            args += [kept, kept, got, got]
        widths.append(sum(kept.shape[1] for kept, _ in group))
    out = call(
        functools.partial(add_kernel, [len(group) for group in groups]),
        tuple(shape(rows, width) for width in widths for _ in range(2)),
        grid=(tiles,),
        in_specs=specs,
        out_specs=tuple(pl.BlockSpec((tile, width), lambda i: (i, 0)) for width in widths for _ in range(2)),
    )(*args)
    return [(out[2 * i], out[2 * i + 1]) for i in range(len(groups))]


def store_group(order, group, kept, sent, span, total):
    if order == 0:

        @pl.when(group < 2)
        def _():
            kept[pl.ds(pl.multiple_of(group * 256, 256), 256), span] = total

        @pl.when(group >= 2)
        def _():
            sent[pl.ds(pl.multiple_of((group - 2) * 256, 256), 256), span] = total

    for number in range(4 if order == 1 else 16 if order == 2 else 0):
        rows = 64 if order == 1 else ROWS
        half, offset = piece_place(order, number)
        start = pl.multiple_of(offset + group * rows, ROWS)
        (kept, sent)[half][pl.ds(start, rows), span] = total[number * rows : number * rows + rows]


def piece_place(order, number):
    if order == 1:
        return number >> 1, 256 * (number & 1)
    return number >> 3, 256 * ((number >> 2) & 1) + 64 * (number & 3)


def outer_kernel(order, left, left_got, right, right_got, kept, sent):
    group = pl.program_id(0)
    columns = right.shape[1]
    one, two = left[...], left_got[...]
    for cut in range(0, columns, 512):
        span = slice(cut, min(cut + 512, columns))
        total = rows_dot(one, right[:, span]) + rows_dot(two, right_got[:, span])
        store_group(order, group, kept, sent, span, total.astype(bf16))


def outer(order, left, left_got, right, right_got):
    columns = right.shape[1]
    outs = (shape(HALF // 2, columns), shape(HALF // 2, columns))
    group = pl.BlockSpec((TOKENS, 256), lambda i: (0, i))
    return call(
        functools.partial(outer_kernel, order),
        outs,
        flops=2 * 512 * HALF * columns,
        grid=(4,),
        in_specs=[group, group, whole(right), whole(right_got)],
        out_specs=tuple(whole(v) for v in outs),
    )(left, left_got, right, right_got)


def table_kernel(line, small, codes, codes_got, right, right_got, targets, *refs):
    kept, sent = refs[-2:]
    columns = right.shape[1]
    step = pl.program_id(0)
    for target, base in ((kept, 0), (sent, HALF // 2)):
        start = pl.multiple_of(base + step * 256, 256)
        here = targets[line : line + 1, pl.ds(start, 256)]
        one, two = hot(codes[...], here), hot(codes_got[...], here)
        for cut in range(0, columns, 512):
            span = slice(cut, min(cut + 512, columns))
            total = rows_dot(one, right[:, span]) + rows_dot(two, right_got[:, span])
            target[:, span] = total.astype(bf16)
        if small:
            row = lax.broadcasted_iota(jnp.int32, (256, 64), 0) + start
            chunk = lax.broadcasted_iota(jnp.int32, (256, 64), 1)
            target[:, columns:] = dot(hot(row, chunk * ROWS), refs[0][...]).astype(bf16)


def table_outer(line, codes, codes_got, right, right_got, targets, small=None):
    args = (codes, codes_got, right, right_got, targets) + (() if small is None else (small,))
    columns = right.shape[1] + (0 if small is None else 128)
    half = shape(HALF // 2, columns)
    tile = pl.BlockSpec((256, columns), lambda i: (i, 0))
    return call(
        functools.partial(table_kernel, line, small is not None),
        (half, half),
        flops=2 * 512 * HALF * columns,
        grid=(2,),
        in_specs=[whole(v) for v in args],
        out_specs=(tile, tile),
    )(*args)


def shard_tables():
    table = np.zeros((2, 8, SHARDS), np.int32)
    groups = np.zeros((2, 8, 16), np.int32)
    inside = (("x", "z"), ("z", "x"), ("x", "z"))
    for core in range(2):
        for number, order in enumerate(ORDERS):
            for place in range(SHARDS):
                here = core ^ (place >> 6)
                mask = (place >> 6) * CORE_BIT
                for step in range(6):
                    if (place >> step) & 1:
                        mask ^= STEP_BITS[order[step // 2]][(step % 2) ^ here]
                table[core, number, place] = mask
            for half in range(2):
                for place in range(16):
                    mask = 0
                    for step in range(4):
                        if (place >> step) & 1:
                            mask ^= STEP_BITS[inside[number][step // 2]][(step % 2) ^ core ^ half]
                    groups[core, 2 * number + half, place] = mask
    table[:, 3:5] = table[:, 1:3]
    lines = np.repeat(table, ROWS, axis=2)
    return lines, np.repeat(groups, ROWS, axis=2), table.transpose(0, 2, 1).copy()


def prepare_kernel(qkv, attn, expand, reduce, table, gain, shift, level, *outs):
    for target in outs:
        target[...] = jnp.zeros(target.shape, bf16)
    first, second, third = outs
    first[0:15, 0:1440] = qkv[...]
    first[0:15, 1440:1536] = attn[:, 384:480]
    first[0:15, 1536:1920] = attn[:, 0:384]
    second[:, 0:1024] = table[:, 0:1024]
    second[0:15, 1024:2944] = expand[...]
    third[:, 0:896] = table[:, 1024:1920]
    third[0:15, 896:2816] = reduce[...]
    for number, ref in enumerate((gain, shift, level)):
        for row in range(2):
            start = (2 * number + row) * 15
            first[15:16, start : start + 15] = ref[row : row + 1, :]


def prepare(*args):
    outs = (shape(16, 1920), shape(16, 2944), shape(16, 2816))
    return call(
        prepare_kernel,
        outs,
        grid=(1,),
        in_specs=[whole(v) for v in args],
        out_specs=outs_whole(outs),
    )(*args)


def places_kernel(here, codes_line, lines, groups, shards, targets, offsets, shard_column, codes):
    me, core = here[0], here[1]
    place = jnp.where(core == 0, lines[0], lines[1]) ^ me
    inside = lax.broadcasted_iota(jnp.int32, place.shape, 1) & 15
    targets[...] = place * 16 + inside
    place = jnp.where(core == 0, groups[0], groups[1]) ^ (me & 15)
    inside = lax.broadcasted_iota(jnp.int32, place.shape, 1) & 15
    offsets[...] = jnp.where(inside < 15, place * 15 + inside, -8192)
    shard_column[...] = jnp.where(core == 0, shards[0], shards[1]) ^ me
    row = jnp.right_shift(lax.broadcasted_iota(jnp.int32, (TOKENS, 64), 0), 2)
    column = lax.broadcasted_iota(jnp.int32, (TOKENS, 64), 1)
    spread = jnp.where(row == column, codes_line[...], 0)
    codes[...] = jnp.sum(spread, axis=1, keepdims=True)


def places(here, codes_line):
    i32 = jnp.int32
    args = (codes_line, *(jnp.asarray(t) for t in shard_tables()))
    outs = (shape(8, 2048, i32), shape(8, 256, i32), shape(SHARDS, 8, i32), shape(TOKENS, 1, i32))
    return call(
        places_kernel,
        outs,
        grid=(1,),
        in_specs=[pl.BlockSpec(memory_space=pltpu.SMEM)] + [whole(v) for v in args],
        out_specs=outs_whole(outs),
    )(here, *args)


class Fetch:
    def __init__(self, sources, targets, sem):
        self.copies = [
            pltpu.make_async_copy(source, target, sem.at[i])
            for i, (source, target) in enumerate(zip(sources, targets))
        ]
        self.targets = targets
        for copy in self.copies:
            copy.start()

    def __call__(self, *numbers):
        for number in numbers:
            self.copies[number].wait()
        return [self.targets[number] for number in numbers]


def fetched(arrays):
    return [pltpu.VMEM(v.shape, v.dtype) for v in arrays] + [pltpu.SemaphoreType.DMA((len(arrays),))]


def tail_lanes(value):
    source = lax.broadcasted_iota(jnp.int32, (480, 256), 0)
    target = lax.broadcasted_iota(jnp.int32, (480, 256), 1)
    return dot(value, hot(source, jnp.where(target >= 160, target + 224, -1))).astype(bf16)


def split_refs(refs, *counts):
    out, start = [], 0
    for count in counts:
        out.append(refs[start : start + count])
        start += count
    return out


def each_chunk(columns, body, width=CHUNK):
    @pl.loop(0, columns // width)
    def _(i):
        body(pl.ds(pl.multiple_of(i * width, 128), width))


def each_rows(body):
    @pl.loop(0, TOKENS // ROW_STEP)
    def _(i):
        body(pl.ds(pl.multiple_of(i * ROW_STEP, ROW_STEP), ROW_STEP))


def group_window(here, offsets, order, half, group):
    core = here[1] ^ half
    number = jnp.right_shift(here[0], 4) ^ (2 * half)
    number = number ^ ((group & 1) * (4 + core)) ^ (jnp.right_shift(group, 1) * (5 - core))
    first = number * 240
    start = jnp.minimum(jnp.right_shift(first, 7) * 128, D - 384)
    line = 2 * order + half
    feature = lax.broadcasted_iota(jnp.int32, (384, 256), 0)
    return pl.ds(pl.multiple_of(start, 128), 384), hot(feature, offsets[line : line + 1, :] + (first - start))


def slot(group):
    return pl.ds(pl.multiple_of(group * 256, 256), 256)


def shuffle(here, offsets, order, value, own, other):
    for half, target in enumerate((own, other)):

        @pl.loop(0, 4)
        def _(group, half=half, target=target):
            window, chosen = group_window(here, offsets, order, half, group)
            target[:, slot(group)] = dot(value[:, window], chosen).astype(bf16)


def unshuffle(here, offsets, order, value, out):
    out[...] = jnp.zeros(out.shape, f32)
    for half in range(2):

        @pl.loop(0, 4)
        def _(group, half=half):
            window, chosen = group_window(here, offsets, order, half, group)
            out[:, window] += cols_dot(value[:, slot(group + 4 * half)], chosen)


def group_rows(order, pieces, half, group, span=slice(None)):
    if order == 0:
        raise NotImplementedError
    rows = 64 if order == 1 else ROWS
    parts = []
    for number in range(256 // rows):
        piece, offset = piece_place(order, number)
        start = offset + group * rows
        start = start if isinstance(start, int) else pl.multiple_of(start, ROWS)
        parts.append(pieces[2 * half + piece][pl.ds(start, rows), span])
    return jnp.concatenate(parts, axis=0)


def group_sum(order, own, other, pieces, span):
    total = None
    for half, value in enumerate((own, other)):
        for group in range(4):
            term = dot(value[:, slice(group * 256, group * 256 + 256)], group_rows(order, pieces, half, group, span))
            total = term if total is None else total + term
    return total


def group_back(order, value, pieces, wide):
    for half in range(2):

        @pl.loop(0, 4)
        def _(group, half=half):
            term = cols_dot(value[...], group_rows(order, pieces, half, group))
            wide[:, slot(group + 4 * half)] = term.astype(bf16)


def pieces_of(own, other):
    return [ref[:, cut] for ref in (own, other) for cut in (slice(0, 512), slice(512, 1024))]


def row_move(transposed=False):
    row = lax.broadcasted_iota(jnp.int32, (TOKENS, TOKENS), 1 if transposed else 0)
    token = lax.broadcasted_iota(jnp.int32, (TOKENS, TOKENS), 0 if transposed else 1)
    moved = jnp.right_shift(row, 3) * 4 + (row & 3) + (jnp.right_shift(row, 2) & 1) * 128
    return hot(token, moved)


def moments(value):
    average = jnp.mean(value, axis=-1, keepdims=True)
    centered = value - average
    variance = jnp.mean(centered * centered, axis=-1, keepdims=True)
    return centered, lax.rsqrt(variance + epsilon)


def norm_back(value, grad, gain, base):
    centered, scale = moments(value)
    normed = centered * scale
    scaled = grad * gain
    inner = scaled - jnp.mean(scaled, axis=-1, keepdims=True)
    inner = inner - normed * jnp.mean(scaled * normed, axis=-1, keepdims=True)
    return base + scale * inner, grad * normed


def embed_kernel(*refs):
    small, big, outs, scratch = split_refs(refs, 8, 12, 5, len(refs) - 25)
    here, level, hidden, codes, targets, offsets, shard_column, marks = small
    stream, own, other, packed, vectors = outs
    normed = scratch[-1]
    fetch = Fetch(big, scratch[:12], scratch[12])
    tables_a, tables_b, weights = range(0, 4), range(4, 8), range(8, 12)
    for line, numbers, start in ((3, tables_a, 0), (4, tables_b, 1024)):
        table = fetch(*numbers)
        total = None
        for k in range(4):
            term = dot(hot(codes[...], targets[line : line + 1, 512 * k : 512 * k + 512]), table[k][...])
            total = term if total is None else total + term
        stream[:, start : start + table[0].shape[1]] = total
    weight = fetch(*weights)
    chunk = lax.broadcasted_iota(jnp.int32, (SHARDS, 512), 0)
    row = lax.broadcasted_iota(jnp.int32, (SHARDS, 512), 1)
    lines = None
    for k in range(4):
        term = dot(hot(row + 512 * k, chunk * ROWS + 15), weight[k][:, :128])
        lines = term if lines is None else lines + term
    spread = rows_dot(lines.astype(bf16), hot(shard_column[:, 0:1], marks[0:1, :]))
    within = lax.broadcasted_iota(jnp.int32, (SHARDS, 1), 0)
    group = sum((within >= 15 * r).astype(jnp.int32) for r in range(1, 7))
    spread = jnp.where(within - group * 15 == marks[1:2, :], spread, 0.0).astype(bf16)
    number = lax.broadcasted_iota(jnp.int32, (8, SHARDS), 1)
    first = lax.broadcasted_iota(jnp.int32, (8, SHARDS), 0) * 15
    chosen = jnp.where((number >= first) & (number < first + 15), 1.0, 0.0).astype(bf16)
    vectors[...] = dot(chosen, spread)
    level_row = jnp.where(level[0] == 0, vectors[4:5, :], vectors[5:6, :])

    def rows(span):
        value = stream[span, :] + hidden[span, :].astype(f32) + level_row
        stream[span, :] = value
        centered, scale = moments(value)
        normed[span, :] = (centered * scale * vectors[0:1, :] + vectors[2:3, :]).astype(bf16)

    each_rows(rows)
    normed[...] = dot(row_move(), normed[...]).astype(bf16)
    shuffle(here, offsets, 0, normed, own, other)
    packed[...] = sum(dot(p, w[:, 0:1440]) for p, w in zip(pieces_of(own, other), weight)).astype(bf16)


def embed(here, level, hidden, codes, targets, offsets, shard_column, marks, tables_a, tables_b, qkv):
    big = (*tables_a, *tables_b, *qkv)
    args = (hidden, codes, targets, offsets, shard_column, marks)
    outs = (
        shape(TOKENS, D, f32),
        shape(TOKENS, HALF),
        shape(TOKENS, HALF),
        shape(TOKENS, 1440),
        shape(8, D, f32),
    )
    return call(
        embed_kernel,
        outs,
        flops=8e9,
        grid=(1,),
        in_specs=[pl.BlockSpec(memory_space=pltpu.SMEM)] * 2
        + [whole(v) for v in args]
        + [pl.BlockSpec(memory_space=pl.ANY)] * 12,
        out_specs=outs_whole(outs),
        scratch_shapes=fetched(big) + [pltpu.VMEM((TOKENS, D), bf16)],
    )(here, level, *args, *big)


def probabilities(columns):
    query, key = columns[:, 0:480], columns[:, 480:960]
    row = lax.broadcasted_iota(jnp.int32, (TOKENS, TOKENS), 0)
    other = lax.broadcasted_iota(jnp.int32, (TOKENS, TOKENS), 1)
    mask = ((row & 3) == (other & 3)) & (jnp.right_shift(row, 2) >= jnp.right_shift(other, 2))
    scores = jnp.where(mask, cols_dot(query, key) * HEAD ** (-0.5), -1e30)
    top = jnp.max(scores, axis=-1, keepdims=True)
    total = top + jnp.log(jnp.sum(jnp.exp(scores - top), axis=-1, keepdims=True))
    return jnp.exp(scores - total)


def attend_kernel(columns, mixed):
    mixed[...] = dot(probabilities(columns).astype(bf16), columns[:, 960:1440]).astype(bf16)


def attend(columns):
    out = shape(TOKENS, 480)
    return call(
        attend_kernel, out, grid=(1,), in_specs=[whole(columns)], out_specs=whole(out)
    )(columns)


def attend_back_kernel(columns, d_mixed, d_packed):
    probs = probabilities(columns)
    low = probs.astype(bf16)
    d_probs = cols_dot(d_mixed[...], columns[:, 960:1440])
    d_scores = (probs * (d_probs - jnp.sum(probs * d_probs, axis=-1, keepdims=True))).astype(bf16)
    scale = HEAD ** (-0.5)
    d_packed[:, 0:480] = (dot(d_scores, columns[:, 480:960]) * scale).astype(bf16)
    d_packed[:, 480:960] = (rows_dot(d_scores, columns[:, 0:480]) * scale).astype(bf16)
    d_packed[:, 960:1440] = rows_dot(low, d_mixed[...]).astype(bf16)
    d_packed[:, 1440:1536] = jnp.zeros((TOKENS, 96), bf16)


def attend_back(columns, d_mixed):
    out = shape(TOKENS, 1536)
    return call(
        attend_back_kernel,
        out,
        grid=(1,),
        in_specs=[whole(columns), whole(d_mixed)],
        out_specs=whole(out),
    )(columns, d_mixed)


def cut_rest(pieces):
    return [ref.at[:, 1280:1536] for ref in pieces]


REST = [jax.ShapeDtypeStruct((512, 256), bf16)] * 4


def rise_kernel(*refs):
    small, big, outs, scratch = split_refs(refs, 5, 12, 7, len(refs) - 24)
    here, mixed_columns, stream, vectors, offsets = small
    mixed, mid, second_own, second_other, active_own, active_other, slope = outs
    fetch = Fetch(cut_rest(big[:4]) + list(big[4:]), scratch[:12], scratch[12])
    work, wide, low = scratch[13:]
    mixed[:, 480:512] = jnp.zeros((TOKENS, 32), bf16)
    mixed[:, 0:480] = dot(row_move(True), mixed_columns[...]).astype(bf16)
    end = tail_lanes(mixed[:, 0:480])
    rest, attn = fetch(*range(0, 4)), fetch(*range(4, 8))
    for k in range(4):
        total = cols_dot(mixed[:, 0:384], attn[k][...]) + cols_dot(end, rest[k][...])
        wide[:, 512 * k : 512 * k + 512] = total.astype(bf16)
    unshuffle(here, offsets, 0, wide, work)

    def rows_first(span):
        value = stream[span, :] + work[span, :]
        mid[span, :] = value
        centered, scale = moments(value)
        low[span, :] = (centered * scale * vectors[1:2, :] + vectors[3:4, :]).astype(bf16)

    each_rows(rows_first)
    shuffle(here, offsets, 1, low, second_own, second_other)
    expand = fetch(*range(8, 12))

    def up(span):
        work[:, span] = group_sum(1, second_own, second_other, expand, span)

    each_chunk(D, up)

    def rows_active(span):
        value = work[span, :]
        root = np.float32(np.sqrt(2 / np.pi))
        square = value * value
        bend = jnp.tanh(root * value * (1.0 + 0.044715 * square))
        low[span, :] = (0.5 * value * (1.0 + bend)).astype(bf16)
        inner = root * (1.0 + 3 * 0.044715 * square)
        slope[span, :] = 0.5 * (1.0 + bend) + 0.5 * value * (1.0 - bend * bend) * inner

    each_rows(rows_active)
    shuffle(here, offsets, 2, low, active_own, active_other)


def rise(here, mixed_columns, stream, vectors, offsets, qkv, attn, expand):
    big = (*qkv, *attn, *expand)
    args = (mixed_columns, stream, vectors, offsets)
    outs = (
        (shape(TOKENS, 512), shape(TOKENS, D, f32))
        + (shape(TOKENS, HALF),) * 4
        + (shape(TOKENS, D, f32),)
    )
    return call(
        rise_kernel,
        outs,
        flops=6e9,
        grid=(1,),
        in_specs=[pl.BlockSpec(memory_space=pltpu.SMEM)]
        + [whole(v) for v in args]
        + [pl.BlockSpec(memory_space=pl.ANY)] * 12,
        out_specs=tuple(whole(v) for v in outs),
        scratch_shapes=fetched(REST + list(big[4:]))
        + [
            pltpu.VMEM((TOKENS, D), f32),
            pltpu.VMEM((TOKENS, 2 * HALF), bf16),
            pltpu.VMEM((TOKENS, D), bf16),
        ],
    )(here, *args, *big)


def turn_kernel(*refs):
    small, big, outs, scratch = split_refs(refs, 7, 4, 2, len(refs) - 13)
    here, mid, active_own, active_other, slope, upstream, offsets = small
    block_out, d_upward = outs
    fetch = Fetch(big, scratch[:4], scratch[4])
    work, wide = scratch[5:]
    reduce = fetch(*range(4))
    group_back(2, upstream, reduce, wide)
    unshuffle(here, offsets, 2, wide, work)

    def rows_upward(span):
        d_upward[span, :] = (slope[span, :] * work[span, :]).astype(bf16)

    each_rows(rows_upward)

    def down(span):
        total = group_sum(2, active_own, active_other, reduce, span)
        block_out[:, span] = (mid[:, span] + total).astype(bf16)

    each_chunk(D, down)


def turn(here, mid, active_own, active_other, slope, upstream, offsets, reduce):
    args = (mid, active_own, active_other, slope, upstream, offsets)
    outs = (shape(TOKENS, D), shape(TOKENS, D))
    return call(
        turn_kernel,
        outs,
        flops=6e9,
        grid=(1,),
        in_specs=[pl.BlockSpec(memory_space=pltpu.SMEM)]
        + [whole(v) for v in args]
        + [pl.BlockSpec(memory_space=pl.ANY)] * 4,
        out_specs=tuple(whole(v) for v in outs),
        scratch_shapes=fetched(reduce)
        + [pltpu.VMEM((TOKENS, D), f32), pltpu.VMEM((TOKENS, 2 * HALF), bf16)],
    )(here, *args, *reduce)


def fall_kernel(*refs):
    small, big, outs, scratch = split_refs(refs, 6, 12, 5, len(refs) - 23)
    here, d_upward, mid, upstream, vectors, offsets = small
    d_mid, attn_own, attn_other, d_mixed, sums = outs
    fetch = Fetch(list(big[:4]) + cut_rest(big[4:8]) + list(big[8:]), scratch[:12], scratch[12])
    work, wide, low = scratch[13:]
    group_back(1, d_upward, fetch(*range(0, 4)), wide)
    unshuffle(here, offsets, 1, wide, work)
    sums[...] = jnp.zeros(sums.shape, f32)

    def rows_back(span):
        base = upstream[span, :].astype(f32)
        grad = work[span, :]
        value, gain_part = norm_back(mid[span, :], grad, vectors[1:2, :], base)
        d_mid[span, :] = value
        low[span, :] = value.astype(bf16)
        sums[0:1, :] += jnp.sum(gain_part, axis=0, keepdims=True)
        sums[1:2, :] += jnp.sum(grad, axis=0, keepdims=True)

    each_rows(rows_back)
    shuffle(here, offsets, 0, low, attn_own, attn_other)
    rest, attn = fetch(*range(4, 8)), fetch(*range(8, 12))
    parts = pieces_of(attn_own, attn_other)
    back = sum(dot(p, w[...]) for p, w in zip(parts, attn)).astype(bf16)
    d_mixed[:, 0:384] = dot(row_move(), back).astype(bf16)
    back = sum(dot(p, w[...]) for p, w in zip(parts, rest)).astype(bf16)
    back = dot(row_move(), back).astype(bf16)
    source = lax.broadcasted_iota(jnp.int32, (256, 128), 0)
    target = lax.broadcasted_iota(jnp.int32, (256, 128), 1)
    d_mixed[:, 384:480] = dot(back, hot(source - 160, target))[:, 0:96].astype(bf16)


def fall(here, d_upward, mid, upstream, vectors, offsets, expand, qkv, attn):
    big = (*expand, *qkv, *attn)
    args = (d_upward, mid, upstream, vectors, offsets)
    outs = (
        shape(TOKENS, D, f32),
        shape(TOKENS, HALF),
        shape(TOKENS, HALF),
        shape(TOKENS, 480),
        shape(8, D, f32),
    )
    return call(
        fall_kernel,
        outs,
        flops=5e9,
        grid=(1,),
        in_specs=[pl.BlockSpec(memory_space=pltpu.SMEM)]
        + [whole(v) for v in args]
        + [pl.BlockSpec(memory_space=pl.ANY)] * 12,
        out_specs=tuple(whole(v) for v in outs),
        scratch_shapes=fetched(list(expand) + REST + list(attn))
        + [
            pltpu.VMEM((TOKENS, D), f32),
            pltpu.VMEM((TOKENS, 2 * HALF), bf16),
            pltpu.VMEM((TOKENS, D), bf16),
        ],
    )(here, *args, *big)


def last_kernel(*refs):
    small, big, outs, scratch = split_refs(refs, 10, 4, 4, len(refs) - 18)
    here, level, d_packed, stream, d_mid, vectors, sums, offsets, shard_column, marks = small
    d_stream, low_a, low_b, spread = outs
    fetch = Fetch(big, scratch[:4], scratch[4])
    work, wide, totals = scratch[5:]
    weight = fetch(*range(4))
    for k in range(4):
        wide[:, 512 * k : 512 * k + 512] = cols_dot(d_packed[:, 0:1440], weight[k][:, 0:1440]).astype(bf16)
    wide[...] = dot(row_move(True), wide[...]).astype(bf16)
    unshuffle(here, offsets, 0, wide, work)
    totals[...] = jnp.zeros(totals.shape, f32)

    def rows(span):
        grad = work[span, :]
        value, gain_part = norm_back(stream[span, :], grad, vectors[0:1, :], d_mid[span, :])
        d_stream[span, :] = value
        low_a[span, :] = value[:, 0:1024].astype(bf16)
        low_b[span, :] = value[:, 1024:1920].astype(bf16)
        totals[0:1, :] += jnp.sum(gain_part, axis=0, keepdims=True)
        totals[2:3, :] += jnp.sum(grad, axis=0, keepdims=True)
        totals[6:7, :] += jnp.sum(value, axis=0, keepdims=True)

    each_rows(rows)
    totals[1:2, :] = sums[0:1, :]
    totals[3:4, :] = sums[1:2, :]
    totals[4:5, :] = jnp.where(level[0] == 0, totals[6:7, :], 0.0)
    totals[5:6, :] = jnp.where(level[0] == 1, totals[6:7, :], 0.0)
    number = lax.broadcasted_iota(jnp.int32, (SHARDS, 8), 0)
    first = lax.broadcasted_iota(jnp.int32, (SHARDS, 8), 1) * 15
    chosen = jnp.where((number >= first) & (number < first + 15) & (number < 90), 1.0, 0.0)
    repeated = dot(chosen.astype(bf16), totals[...].astype(bf16))
    within = lax.broadcasted_iota(jnp.int32, (SHARDS, 1), 0)
    group = sum((within >= 15 * r).astype(jnp.int32) for r in range(1, 7))
    repeated = jnp.where(within - group * 15 == marks[1:2, :], repeated, 0.0).astype(bf16)
    spread[...] = cols_dot(hot(shard_column[:, 2:3], marks[0:1, :]), repeated).astype(bf16)


def last(here, level, d_packed, stream, d_mid, vectors, sums, offsets, shard_column, marks, qkv):
    args = (d_packed, stream, d_mid, vectors, sums, offsets, shard_column, marks)
    outs = (shape(TOKENS, D, f32), shape(TOKENS, 1024), shape(TOKENS, 896), shape(SHARDS, 128))
    return call(
        last_kernel,
        outs,
        flops=6e9,
        grid=(1,),
        in_specs=[pl.BlockSpec(memory_space=pltpu.SMEM)] * 2
        + [whole(v) for v in args]
        + [pl.BlockSpec(memory_space=pl.ANY)] * 4,
        out_specs=tuple(whole(v) for v in outs),
        scratch_shapes=fetched(qkv)
        + [
            pltpu.VMEM((TOKENS, D), f32),
            pltpu.VMEM((TOKENS, 2 * HALF), bf16),
            pltpu.VMEM((8, D), f32),
        ],
    )(here, level, *args, *qkv)


def finish_kernel(kept0, got0, kept1, got1, kept2, got2, *outs):
    grad_qkv, grad_attn, grad_expand, grad_reduce, table, levels, gains, shifts = outs

    def total(kept, got, start, stop):
        return kept[:, start:stop].astype(f32) + got[:, start:stop].astype(f32)

    grad_attn[...] = total(kept0, got0, 0, 480)[:15]
    grad_qkv[...] = total(kept0, got0, 512, 1952)[:15]
    grad_expand[...] = total(kept1, got1, 0, 1920)[:15]
    table[:, 0:1024] = total(kept1, got1, 1920, 2944)
    grad_reduce[...] = total(kept2, got2, 0, 1920)[:15]
    table[:, 1024:1920] = total(kept2, got2, 1920, 2816)
    line = total(kept2, got2, 2816, 2944)[0:1]
    for target, first in ((gains, 0), (shifts, 2), (levels, 4)):
        for row in range(2):
            start = (first + row) * 15
            target[row : row + 1, :] = line[:, start : start + 15]


def finish(*pairs):
    outs = tuple(
        shape(*s, f32)
        for s in ((15, 1440), (15, 480), (15, D), (15, D), (16, D), (2, 15), (2, 15), (2, 15))
    )
    return call(
        finish_kernel,
        outs,
        grid=(1,),
        in_specs=[whole(v) for v in pairs],
        out_specs=outs_whole(outs),
    )(*pairs)


def body(
    hidden_in,
    cond_codes,
    level_ids,
    qkv_weight,
    attn_out_weight,
    mlp_in_weight,
    mlp_out_weight,
    code_table,
    level_table,
    norm_gain,
    norm_bias,
    grad_out,
):
    yl, co, yh, z, x = (lax.axis_index(name) for name in AXES)
    me = yl * 64 + co * 32 + yh * 16 + z * 4 + x
    here = jnp.stack((me, co))
    targets, offsets, shard_column, codes = places(here, cond_codes)
    shards = prepare(
        qkv_weight,
        attn_out_weight.T,
        mlp_in_weight,
        mlp_out_weight,
        code_table,
        norm_gain,
        norm_bias,
        level_table,
    )
    feature = np.arange(D, dtype=np.int32)
    marks = jnp.asarray(np.stack((feature // 15, feature % 15)))

    def exchanged(values, step):
        return [exchange(v, order, step) for v, order in zip(values, ORDERS)]

    def singles(lists):
        return [v for (v,) in lists]

    small = singles(join(shards, exchanged(shards, 0)))
    small, (targets, offsets, shard_column, codes) = lax.optimization_barrier(
        (small, (targets, offsets, shard_column, codes))
    )
    for step in (1, 2):
        small = singles(join(small, exchanged(small, step)))
    cuts = [((0, split), (split, v.shape[1])) for v, split in zip(small, SPLITS)]
    small = join(small, exchanged(small, 3), cuts)
    first, second = [v for v, _ in small], [v for _, v in small]
    first = singles(join(first, exchanged(first, 4)))
    first, second = lax.optimization_barrier((first, second))
    rests = exchanged(first, 5)
    second_got = exchanged(second, 4)
    pieces = [(h, r, swap_cores(h), swap_cores(r)) for h, r in zip(first, rests)]
    second = singles(join(second, second_got))
    pieces, second = lax.optimization_barrier((pieces, second))
    qkv, table_a, table_b = pieces
    rests = exchanged(second, 5)

    stream, first_own, first_other, packed, vectors = embed(
        here, level_ids, hidden_in[0], codes, targets, offsets, shard_column, marks, table_a, table_b, qkv
    )

    def over_blocks(value):
        return lax.all_to_all(value, BLK, split_axis=0, concat_axis=0, tiled=True)

    columns = over_blocks(packed)
    mixed = attend(columns)
    mixed, rests = lax.optimization_barrier((mixed, rests))
    mixed = over_blocks(mixed)
    attn, expand, reduce = [(h, r, swap_cores(h), swap_cores(r)) for h, r in zip(second, rests)]
    upstream = grad_out[0]
    upstream_got = swap_cores(upstream)
    mixed, mid, second_own, second_other, active_own, active_other, slope = rise(
        here, mixed, stream, vectors, offsets, qkv, attn, expand
    )
    reduce_grad = outer(2, active_own, swap_cores(active_other), upstream, upstream_got)
    second_got, mixed_got = swap_cores(second_other), swap_cores(mixed)
    active_own, reduce_grad = lax.optimization_barrier((active_own, reduce_grad))
    reduce_got = exchange(reduce_grad[1], ORDERS[2], 5)
    block_out, d_upward = turn(
        here, mid, active_own, active_other, slope, upstream, offsets, reduce
    )
    expand_grad = outer(1, second_own, second_got, d_upward, swap_cores(d_upward))
    d_upward, expand_grad = lax.optimization_barrier((d_upward, expand_grad))
    expand_got = exchange(expand_grad[1], ORDERS[1], 5)
    d_mid, attn_own, attn_other, d_mixed, sums = fall(
        here, d_upward, mid, upstream, vectors, offsets, expand, qkv, attn
    )
    d_mixed = over_blocks(d_mixed)
    attn_grad = outer(0, attn_own, swap_cores(attn_other), mixed, mixed_got)
    attn_got = exchange(attn_grad[1], ORDERS[0], 5)
    early = (attn_grad, expand_grad, reduce_grad)
    early_got = (attn_got, expand_got, reduce_got)
    first_got = swap_cores(first_other)
    codes_got = swap_cores(codes)

    d_packed = over_blocks(attend_back(columns, d_mixed))
    early = add_halves([[(kept, got)] for (kept, _), got in zip(early, early_got)])
    d_packed, early = lax.optimization_barrier((d_packed, early))
    early_got = exchanged([sent for _, sent in early], 4)
    qkv_grad = outer(0, first_own, first_got, d_packed, swap_cores(d_packed))
    d_packed, qkv_grad = lax.optimization_barrier((d_packed, qkv_grad))

    d_stream, low_a, low_b, small = last(
        here, level_ids, d_packed, stream, d_mid, vectors, sums, offsets, shard_column, marks, qkv
    )
    small = small[:64] + swap_cores(small[64:])
    grad_a = table_outer(3, codes, codes_got, low_a, swap_cores(low_a), targets)
    grad_b = table_outer(4, codes, codes_got, low_b, swap_cores(low_b), targets, small)
    late = [qkv_grad, grad_a, grad_b]
    late_got = exchanged([sent for _, sent in late], 5)
    late = add_halves([[(kept, got)] for (kept, _), got in zip(late, late_got)])
    late_got = exchanged([sent for _, sent in late], 4)
    sums = add_halves(
        [
            [(before, before_got), (kept, got)]
            for (before, _), before_got, (kept, _), got in zip(early, early_got, late, late_got)
        ]
    )
    for step in (3, 2, 1):
        got = exchanged([sent for _, sent in sums], step)
        sums = add_halves([[(kept, v)] for (kept, _), v in zip(sums, got)])
    got = exchanged([sent for _, sent in sums], 0)
    pairs = [v for (kept, _), mine in zip(sums, got) for v in (kept, mine)]
    grad_qkv, grad_attn, grad_expand, grad_reduce, grad_table, levels, gains, shifts = finish(*pairs)
    return (
        block_out[None],
        d_stream[None],
        grad_qkv,
        grad_attn.T,
        grad_expand,
        grad_reduce,
        grad_table,
        levels,
        gains,
        shifts,
    )


def solution(mesh):
    fine = Mesh(mesh.devices.reshape(2, 2, 2, 4, 4), AXES)
    return jax.shard_map(
        body,
        mesh=fine,
        in_specs=(
            P(WIN, BLK, None),
            P(WIN, BLK),
            P(WIN),
            P(AXES, None),
            P(None, AXES),
            P(AXES, None),
            P(AXES, None),
            P(AXES, None),
            P(None, AXES),
            P(None, AXES),
            P(None, AXES),
            P(WIN, BLK, None),
        ),
        out_specs=(
            P(WIN, BLK, None),
            P(WIN, BLK, None),
            P(AXES, None),
            P(None, AXES),
            P(AXES, None),
            P(AXES, None),
            P(AXES, None),
            P(None, AXES),
            P(None, AXES),
            P(None, AXES),
        ),
        check_vma=False,
    )
```

```python
import functools

import jax
import jax.numpy as jnp
import numpy as np
from jax import lax
from jax.experimental import pallas as pl
from jax.experimental.pallas import tpu as pltpu
from jax.sharding import Mesh, PartitionSpec as P

HEAD = 480
BLOCK = 128
RATIO = 4
D = 1920
SHARDS = 128
ROWS = 16
HALF = 1024
HALVES = (slice(0, HALF), slice(HALF, 2 * HALF))
SPLITS = (1536, 1024, 896)
TOKENS = 256
CHUNK = 640
MIB = 2**20
ROW_STEP = 128
epsilon = 1e-05
bf16 = jnp.bfloat16
f32 = jnp.float32
AXES = ("yl", "co", "yh", "z", "x")
WIN = ("yl", "co")
BLK = ("yh", "z", "x")
STEP_BITS = {"x": (1, 3), "z": (4, 12), "y": (64, 80)}
CORE_BIT = 32
ORDERS = (("x", "z", "y"), ("z", "y", "x"), ("y", "x", "z"))


def exchange(value, order, step):
    masks = STEP_BITS[order[step // 2]]
    pairs = [(i, i ^ masks[(step % 2) ^ ((i >> 5) & 1)]) for i in range(SHARDS)]
    return lax.ppermute(value, AXES, pairs)


def swap_cores(value):
    return lax.ppermute(value, AXES, [(i, i ^ CORE_BIT) for i in range(SHARDS)])


def call(kernel, out_shape, vmem=16, flops=0, **options):
    params = pltpu.CompilerParams(vmem_limit_bytes=vmem * MIB)

    def run(*args):
        outs = out_shape if isinstance(out_shape, tuple) else (out_shape,)
        size = sum(v.size * v.dtype.itemsize for v in args + outs)
        cost = pl.CostEstimate(flops=int(flops), bytes_accessed=size, transcendentals=0)
        return pl.pallas_call(
            kernel, out_shape=out_shape, compiler_params=params, cost_estimate=cost, **options
        )(*args)

    return run


def whole(v):
    return pl.BlockSpec(
        v.shape, lambda i: (0,) * len(v.shape), pipeline_mode=pl.Buffered(buffer_count=1)
    )


def outs_whole(shapes):
    return tuple(pl.BlockSpec(v.shape, lambda i: (0, 0)) for v in shapes)


def shape(rows, columns, dtype=bf16):
    return jax.ShapeDtypeStruct((rows, columns), dtype)


def dot(left, right):
    return jnp.dot(left, right, preferred_element_type=f32)


def rows_dot(left, right):
    return lax.dot_general(left, right, (((0,), (0,)), ((), ())), preferred_element_type=f32)


def cols_dot(left, right):
    return lax.dot_general(left, right, (((1,), (1,)), ((), ())), preferred_element_type=f32)


def hot(left, right):
    return jnp.where(left == right, 1.0, 0.0).astype(bf16)


def join_kernel(tiles, cuts, *refs):
    count = len(cuts)
    sources, targets = refs[: 2 * count], list(refs[2 * count :])
    step = pl.program_id(0)
    for i, spans in enumerate(cuts):
        mine, targets = targets[: len(spans)], targets[len(spans) :]
        for source, here in ((sources[2 * i], step < tiles), (sources[2 * i + 1], step >= tiles)):

            @pl.when(here)
            def _(source=source, mine=mine, spans=spans):
                for target, (start, stop) in zip(mine, spans):
                    target[...] = source[:, start:stop]


def join(firsts, seconds, cuts=None):
    rows = firsts[0].shape[0]
    cuts = cuts or [((0, v.shape[1]),) for v in firsts]
    tiles = max(rows // 128, 1)
    tile = rows // tiles
    specs, args = [], []
    for first, second in zip(firsts, seconds):
        columns = first.shape[1]
        specs += [
            pl.BlockSpec((tile, columns), lambda i: (jnp.minimum(i, tiles - 1), 0)),
            pl.BlockSpec((tile, columns), lambda i: (jnp.maximum(i - tiles, 0), 0)),
        ]
        args += [first, second]
    widths = [stop - start for spans in cuts for start, stop in spans]
    out = call(
        functools.partial(join_kernel, tiles, cuts),
        tuple(shape(2 * rows, width) for width in widths),
        grid=(2 * tiles,),
        in_specs=specs,
        out_specs=tuple(pl.BlockSpec((tile, width), lambda i: (i, 0)) for width in widths),
    )(*args)
    out = list(out)
    return [[out.pop(0) for _ in spans] for spans in cuts]


def add_kernel(counts, *refs):
    arrays = sum(counts)
    sources, targets = refs[: 4 * arrays], refs[4 * arrays :]
    number = 0
    for i, count in enumerate(counts):
        start = 0
        for _ in range(count):
            kept_low, kept_high, got_low, got_high = sources[4 * number : 4 * number + 4]
            span = slice(start, start + kept_low.shape[1])
            targets[2 * i][:, span] = (kept_low[...].astype(f32) + got_low[...].astype(f32)).astype(bf16)
            targets[2 * i + 1][:, span] = (
                kept_high[...].astype(f32) + got_high[...].astype(f32)
            ).astype(bf16)
            start, number = span.stop, number + 1


def add_halves(groups):
    rows = groups[0][0][0].shape[0] // 2
    tiles = max(rows // 128, 1)
    tile = rows // tiles
    specs, args, widths = [], [], []
    for group in groups:
        for kept, got in group:
            columns = kept.shape[1]
            low = pl.BlockSpec((tile, columns), lambda i: (i, 0))
            high = pl.BlockSpec((tile, columns), lambda i: (i + tiles, 0))
            specs += [low, high, low, high]
            args += [kept, kept, got, got]
        widths.append(sum(kept.shape[1] for kept, _ in group))
    out = call(
        functools.partial(add_kernel, [len(group) for group in groups]),
        tuple(shape(rows, width) for width in widths for _ in range(2)),
        grid=(tiles,),
        in_specs=specs,
        out_specs=tuple(pl.BlockSpec((tile, width), lambda i: (i, 0)) for width in widths for _ in range(2)),
    )(*args)
    return [(out[2 * i], out[2 * i + 1]) for i in range(len(groups))]


def store_group(order, group, kept, sent, total):
    if order == 0:
        start = 256 * (group & 1)
        (kept, sent)[group >> 1][start : start + 256, :] = total
    for number in range(4 if order == 1 else 16 if order == 2 else 0):
        rows = 64 if order == 1 else ROWS
        half, offset = piece_place(order, number)
        start = offset + group * rows
        (kept, sent)[half][start : start + rows, :] = total[number * rows : number * rows + rows]


def piece_place(order, number):
    if order == 1:
        return number >> 1, 256 * (number & 1)
    return number >> 3, 256 * ((number >> 2) & 1) + 64 * (number & 3)


def outer_kernel(order, left, left_got, right, right_got, kept, sent, turned):
    @pl.when(pl.program_id(0) == 0)
    def _():
        turned[:, 0:256] = left[...].T
        turned[:, 256:512] = left_got[...].T

    for group in range(4):
        rows = slice(256 * group, 256 * group + 256)
        total = dot(turned[rows, 0:256], right[...]) + dot(turned[rows, 256:512], right_got[...])
        store_group(order, group, kept, sent, total.astype(bf16))


def outer(order, left, left_got, right, right_got):
    columns = right.shape[1]
    width = 640 if columns % 640 == 0 else 512
    outs = (shape(HALF // 2, columns), shape(HALF // 2, columns))
    tile = pl.BlockSpec((TOKENS, width), lambda i: (0, i))
    out = pl.BlockSpec((HALF // 2, width), lambda i: (0, i))
    return call(
        functools.partial(outer_kernel, order),
        outs,
        flops=2 * 512 * HALF * columns,
        grid=(columns // width,),
        in_specs=[whole(left), whole(left_got), tile, tile],
        out_specs=(out, out),
        scratch_shapes=[pltpu.VMEM((HALF, 512), bf16)],
    )(left, left_got, right, right_got)


def table_kernel(line, small, codes, codes_got, right, right_got, targets, *refs):
    kept, sent = refs[-2:]
    columns = right.shape[1]
    step = pl.program_id(0)
    for target, base in ((kept, 0), (sent, HALF // 2)):
        start = pl.multiple_of(base + step * 256, 256)
        here = targets[line : line + 1, pl.ds(start, 256)]
        one, two = hot(codes[...], here), hot(codes_got[...], here)
        for cut in range(0, columns, 512):
            span = slice(cut, min(cut + 512, columns))
            total = rows_dot(one, right[:, span]) + rows_dot(two, right_got[:, span])
            target[:, span] = total.astype(bf16)
        if small:
            row = lax.broadcasted_iota(jnp.int32, (256, 64), 0) + start
            chunk = lax.broadcasted_iota(jnp.int32, (256, 64), 1)
            target[:, columns:] = dot(hot(row, chunk * ROWS), refs[0][...]).astype(bf16)


def table_outer(line, codes, codes_got, right, right_got, targets, small=None):
    args = (codes, codes_got, right, right_got, targets) + (() if small is None else (small,))
    columns = right.shape[1] + (0 if small is None else 128)
    half = shape(HALF // 2, columns)
    tile = pl.BlockSpec((256, columns), lambda i: (i, 0))
    return call(
        functools.partial(table_kernel, line, small is not None),
        (half, half),
        flops=2 * 512 * HALF * columns,
        grid=(2,),
        in_specs=[whole(v) for v in args],
        out_specs=(tile, tile),
    )(*args)


def shard_tables():
    table = np.zeros((2, 8, SHARDS), np.int32)
    groups = np.zeros((2, 8, 16), np.int32)
    inside = (("x", "z"), ("z", "x"), ("x", "z"))
    for core in range(2):
        for number, order in enumerate(ORDERS):
            for place in range(SHARDS):
                here = core ^ (place >> 6)
                mask = (place >> 6) * CORE_BIT
                for step in range(6):
                    if (place >> step) & 1:
                        mask ^= STEP_BITS[order[step // 2]][(step % 2) ^ here]
                table[core, number, place] = mask
            for half in range(2):
                for place in range(16):
                    mask = 0
                    for step in range(4):
                        if (place >> step) & 1:
                            mask ^= STEP_BITS[inside[number][step // 2]][(step % 2) ^ core ^ half]
                    groups[core, 2 * number + half, place] = mask
    table[:, 3:5] = table[:, 1:3]
    lines = np.repeat(table, ROWS, axis=2)
    return lines, np.repeat(groups, ROWS, axis=2), table.transpose(0, 2, 1).copy()


def prepare_kernel(qkv, attn, expand, reduce, table, gain, shift, level, *outs):
    for target in outs:
        target[...] = jnp.zeros(target.shape, bf16)
    first, second, third = outs
    first[0:15, 0:1440] = qkv[...]
    first[0:15, 1440:1536] = attn[:, 384:480]
    first[0:15, 1536:1920] = attn[:, 0:384]
    second[:, 0:1024] = table[:, 0:1024]
    second[0:15, 1024:2944] = expand[...]
    third[:, 0:896] = table[:, 1024:1920]
    third[0:15, 896:2816] = reduce[...]
    for number, ref in enumerate((gain, shift, level)):
        for row in range(2):
            start = (2 * number + row) * 15
            first[15:16, start : start + 15] = ref[row : row + 1, :]


def prepare(*args):
    outs = (shape(16, 1920), shape(16, 2944), shape(16, 2816))
    return call(
        prepare_kernel,
        outs,
        grid=(1,),
        in_specs=[whole(v) for v in args],
        out_specs=outs_whole(outs),
    )(*args)


def places_kernel(here, codes_line, lines, groups, shards, targets, offsets, shard_column, codes):
    me, core = here[0], here[1]
    place = jnp.where(core == 0, lines[0], lines[1]) ^ me
    inside = lax.broadcasted_iota(jnp.int32, place.shape, 1) & 15
    targets[...] = place * 16 + inside
    place = jnp.where(core == 0, groups[0], groups[1]) ^ (me & 15)
    inside = lax.broadcasted_iota(jnp.int32, place.shape, 1) & 15
    offsets[...] = jnp.where(inside < 15, place * 15 + inside, -8192)
    shard_column[...] = jnp.where(core == 0, shards[0], shards[1]) ^ me
    row = jnp.right_shift(lax.broadcasted_iota(jnp.int32, (TOKENS, 64), 0), 2)
    column = lax.broadcasted_iota(jnp.int32, (TOKENS, 64), 1)
    spread = jnp.where(row == column, codes_line[...], 0)
    codes[...] = jnp.sum(spread, axis=1, keepdims=True)


def places(here, codes_line):
    i32 = jnp.int32
    args = (codes_line, *(jnp.asarray(t) for t in shard_tables()))
    outs = (shape(8, 2048, i32), shape(8, 256, i32), shape(SHARDS, 8, i32), shape(TOKENS, 1, i32))
    return call(
        places_kernel,
        outs,
        grid=(1,),
        in_specs=[pl.BlockSpec(memory_space=pltpu.SMEM)] + [whole(v) for v in args],
        out_specs=outs_whole(outs),
    )(here, *args)


class Flow:
    def __init__(self, sources, buffers, targets, results, sem):
        count = len(sources)
        self.copies = [
            pltpu.make_async_copy(source, buffer, sem.at[i])
            for i, (source, buffer) in enumerate(zip(sources, buffers))
        ]
        self.buffers = buffers
        self.leaving = [
            pltpu.make_async_copy(result, target, sem.at[count + i])
            for i, (result, target) in enumerate(zip(results, targets))
        ]
        for copy in self.copies:
            copy.start()

    def __call__(self, *numbers):
        for number in numbers:
            self.copies[number].wait()
        return [self.buffers[number] for number in numbers]

    def out(self, *numbers):
        for number in numbers:
            self.leaving[number].start()

    def end(self):
        for copy in self.leaving:
            copy.wait()


def tail_lanes(value):
    source = lax.broadcasted_iota(jnp.int32, (480, 256), 0)
    target = lax.broadcasted_iota(jnp.int32, (480, 256), 1)
    return dot(value, hot(source, jnp.where(target >= 160, target + 224, -1))).astype(bf16)


def flowing(body, scalars, args, outs, extra, flops, cuts=None):
    anywhere = pl.BlockSpec(memory_space=pl.ANY)
    cuts = cuts or {}
    shapes = [
        (v.shape[0], cuts[i][1] - cuts[i][0]) if i in cuts else v.shape for i, v in enumerate(args)
    ]

    def kernel(*refs):
        first, sources, targets, buffers, results, (sem,), more = split_refs(
            refs, len(scalars), len(args), len(outs), len(args), len(outs), 1, len(extra)
        )
        sources = [
            ref.at[:, cuts[i][0] : cuts[i][1]] if i in cuts else ref for i, ref in enumerate(sources)
        ]
        flow = Flow(sources, buffers, targets, results, sem)
        body(flow, first, results, more)
        flow.end()

    return call(
        kernel,
        outs,
        vmem=60,
        flops=flops,
        in_specs=[pl.BlockSpec(memory_space=pltpu.SMEM)] * len(scalars) + [anywhere] * len(args),
        out_specs=(anywhere,) * len(outs),
        scratch_shapes=[pltpu.VMEM(dims, v.dtype) for dims, v in zip(shapes, args)]
        + [pltpu.VMEM(v.shape, v.dtype) for v in outs]
        + [pltpu.SemaphoreType.DMA((len(args) + len(outs),))]
        + extra,
    )(*scalars, *args)


def split_refs(refs, *counts):
    out, start = [], 0
    for count in counts:
        out.append(refs[start : start + count])
        start += count
    return out


def each_chunk(columns, body, width=CHUNK):
    for i in range(columns // width):
        body(slice(i * width, i * width + width))


def each_rows(body):
    @pl.loop(0, TOKENS // ROW_STEP)
    def _(i):
        body(pl.ds(pl.multiple_of(i * ROW_STEP, ROW_STEP), ROW_STEP))


SHIFT = 144
HOT = pltpu.VMEM((2, SHIFT + 384, 256), bf16)


def make_hot(offsets, order, chosen):
    for half in range(2):
        line = 2 * order + half
        feature = lax.broadcasted_iota(jnp.int32, (SHIFT + 384, 256), 0) - SHIFT
        chosen[half, :, :] = hot(feature, offsets[line : line + 1, :])


def group_window(here, half, group):
    core = here[1] ^ half
    number = jnp.right_shift(here[0], 4) ^ (2 * half)
    number = number ^ ((group & 1) * (4 + core)) ^ ((group >> 1) * (5 - core))
    first = number * 240
    start = jnp.minimum(jnp.right_shift(first, 7) * 128, D - 384)
    rows = pl.ds(pl.multiple_of(SHIFT + start - first, 16), 384)
    return pl.ds(pl.multiple_of(start, 128), 384), rows


def slot(group):
    return slice(group * 256, group * 256 + 256)


def shuffle(here, chosen, value, own, other):
    for half, target in enumerate((own, other)):
        for group in range(4):
            window, rows = group_window(here, half, group)
            target[:, slot(group)] = dot(value[:, window], chosen[half, rows, :]).astype(bf16)


def unshuffle(here, chosen, value, out):
    out[...] = jnp.zeros(out.shape, f32)
    for number in range(8):
        first = number * 240
        start = min(first // 128 * 128, D - 384)
        apart = jnp.right_shift(here[0], 4) ^ number
        half = jnp.right_shift(apart, 1) & 1
        core = here[1] ^ half
        low = apart & 1
        high = (jnp.right_shift(apart, 2) & 1) ^ low
        group = (high + 2 * low) * (1 - core) + (low + 2 * high) * core
        place = pl.ds(pl.multiple_of((4 * half + group) * 256, 256), 256)
        rows = slice(SHIFT + start - first, SHIFT + start - first + 384)
        out[:, start : start + 384] += cols_dot(value[:, place], chosen[half, rows, :])


def group_rows(order, pieces, half, group, span=slice(None)):
    rows = 64 if order == 1 else ROWS
    parts = []
    for number in range(256 // rows):
        piece, offset = piece_place(order, number)
        start = offset + group * rows
        start = start if isinstance(start, int) else pl.multiple_of(start, ROWS)
        parts.append(pieces[2 * half + piece][pl.ds(start, rows), span])
    return jnp.concatenate(parts, axis=0)


def group_sum(order, own, other, pieces, span):
    total = None
    for half, value in enumerate((own, other)):
        rows = [group_rows(order, pieces, half, group, span) for group in range(4)]
        term = dot(value[...], jnp.concatenate(rows, axis=0))
        total = term if total is None else total + term
    return total


def group_back(order, value, flow, first, wide):
    pieces = []
    for half in range(2):
        pieces += flow(first + 2 * half, first + 2 * half + 1)
        for group in range(4):
            term = cols_dot(value[...], group_rows(order, pieces, half, group))
            wide[:, slot(group + 4 * half)] = term.astype(bf16)
    return pieces


def pieces_of(own, other):
    return [ref[:, cut] for ref in (own, other) for cut in (slice(0, 512), slice(512, 1024))]


def row_move(transposed=False):
    row = lax.broadcasted_iota(jnp.int32, (TOKENS, TOKENS), 1 if transposed else 0)
    token = lax.broadcasted_iota(jnp.int32, (TOKENS, TOKENS), 0 if transposed else 1)
    moved = jnp.right_shift(row, 3) * 4 + (row & 3) + (jnp.right_shift(row, 2) & 1) * 128
    return hot(token, moved)


def moments(value):
    average = jnp.mean(value, axis=-1, keepdims=True)
    centered = value - average
    variance = jnp.mean(centered * centered, axis=-1, keepdims=True)
    return centered, lax.rsqrt(variance + epsilon)


def norm_back(value, grad, gain, base):
    centered, scale = moments(value)
    normed = centered * scale
    scaled = grad * gain
    inner = scaled - jnp.mean(scaled, axis=-1, keepdims=True)
    inner = inner - normed * jnp.mean(scaled * normed, axis=-1, keepdims=True)
    return base + scale * inner, grad * normed


def embed_body(flow, scalars, results, more):
    here, level = scalars
    stream, own, other, packed, vectors = results
    normed, chosen, looked = more
    codes, targets, offsets, shard_column, marks = flow(0, 1, 2, 3, 4)
    make_hot(offsets, 0, chosen)
    row = lax.broadcasted_iota(jnp.int32, (64, TOKENS), 0)
    token = lax.broadcasted_iota(jnp.int32, (64, TOKENS), 1)
    every = hot(row * RATIO, token)
    for line, first, start in ((3, 5, 0), (4, 9, 1024)):
        total = None
        for k in range(4):
            (table,) = flow(first + k)
            spread = hot(codes[...], targets[line : line + 1, 512 * k : 512 * k + 512])
            term = dot(dot(every, spread).astype(bf16), table[...])
            total = term if total is None else total + term
        looked[:, start : start + total.shape[1]] = total.astype(bf16)
    (hidden,) = flow(13)
    heads = flow(14, 15, 16, 17)
    chunk = lax.broadcasted_iota(jnp.int32, (SHARDS, 512), 0)
    row = lax.broadcasted_iota(jnp.int32, (SHARDS, 512), 1)
    lines = None
    for k in range(4):
        term = dot(hot(row + 512 * k, chunk * ROWS + 15), heads[k][...])
        lines = term if lines is None else lines + term
    spread = rows_dot(lines.astype(bf16), hot(shard_column[:, 0:1], marks[0:1, :]))
    within = lax.broadcasted_iota(jnp.int32, (SHARDS, 1), 0)
    group = sum((within >= 15 * r).astype(jnp.int32) for r in range(1, 7))
    spread = jnp.where(within - group * 15 == marks[1:2, :], spread, 0.0).astype(bf16)
    number = lax.broadcasted_iota(jnp.int32, (8, SHARDS), 1)
    first = lax.broadcasted_iota(jnp.int32, (8, SHARDS), 0) * 15
    inside = jnp.where((number >= first) & (number < first + 15), 1.0, 0.0).astype(bf16)
    vectors[...] = dot(inside, spread)
    flow.out(4)
    level_row = jnp.where(level[0] == 0, vectors[4:5, :], vectors[5:6, :])
    token = lax.broadcasted_iota(jnp.int32, (ROW_STEP, 64), 0)
    column = lax.broadcasted_iota(jnp.int32, (ROW_STEP, 64), 1)

    def rows(span):
        four = hot(jnp.right_shift(token + span.start, 2), column)
        value = dot(four, looked[...]) + hidden[span, :].astype(f32) + level_row
        stream[span, :] = value
        centered, scale = moments(value)
        normed[span, :] = (centered * scale * vectors[0:1, :] + vectors[2:3, :]).astype(bf16)

    each_rows(rows)
    flow.out(0)
    normed[...] = dot(row_move(), normed[...]).astype(bf16)
    shuffle(here, chosen, normed, own, other)
    flow.out(1, 2)
    weight = flow(18, 19, 20, 21)
    packed[...] = sum(dot(p, w[:, 0:1440]) for p, w in zip(pieces_of(own, other), weight)).astype(bf16)
    flow.out(3)


def embed(here, level, hidden, codes, targets, offsets, shard_column, marks, tables_a, tables_b, qkv):
    outs = (
        shape(TOKENS, D, f32),
        shape(TOKENS, HALF),
        shape(TOKENS, HALF),
        shape(TOKENS, 1440),
        shape(8, D, f32),
    )
    return flowing(
        embed_body,
        (here, level),
        (codes, targets, offsets, shard_column, marks, *tables_a, *tables_b, hidden, *qkv, *qkv),
        outs,
        [pltpu.VMEM((TOKENS, D), bf16), HOT, pltpu.VMEM((64, D), bf16)],
        8e9,
        {i: (0, 128) for i in (14, 15, 16, 17)},
    )


def probabilities(columns):
    query, key = columns[:, 0:480], columns[:, 480:960]
    row = lax.broadcasted_iota(jnp.int32, (TOKENS, TOKENS), 0)
    other = lax.broadcasted_iota(jnp.int32, (TOKENS, TOKENS), 1)
    mask = ((row & 3) == (other & 3)) & (jnp.right_shift(row, 2) >= jnp.right_shift(other, 2))
    scores = jnp.where(mask, cols_dot(query, key) * HEAD ** (-0.5), -1e30)
    top = jnp.max(scores, axis=-1, keepdims=True)
    total = top + jnp.log(jnp.sum(jnp.exp(scores - top), axis=-1, keepdims=True))
    return jnp.exp(scores - total)


def attend_kernel(columns, mixed):
    mixed[...] = dot(probabilities(columns).astype(bf16), columns[:, 960:1440]).astype(bf16)


def attend(columns):
    out = shape(TOKENS, 480)
    return call(
        attend_kernel, out, grid=(1,), in_specs=[whole(columns)], out_specs=whole(out)
    )(columns)


def attend_back_kernel(columns, d_mixed, d_packed):
    probs = probabilities(columns)
    low = probs.astype(bf16)
    d_probs = cols_dot(d_mixed[...], columns[:, 960:1440])
    d_scores = (probs * (d_probs - jnp.sum(probs * d_probs, axis=-1, keepdims=True))).astype(bf16)
    scale = HEAD ** (-0.5)
    d_packed[:, 0:480] = (dot(d_scores, columns[:, 480:960]) * scale).astype(bf16)
    d_packed[:, 480:960] = (rows_dot(d_scores, columns[:, 0:480]) * scale).astype(bf16)
    d_packed[:, 960:1440] = rows_dot(low, d_mixed[...]).astype(bf16)
    d_packed[:, 1440:1536] = jnp.zeros((TOKENS, 96), bf16)


def attend_back(columns, d_mixed):
    out = shape(TOKENS, 1536)
    return call(
        attend_back_kernel,
        out,
        grid=(1,),
        in_specs=[whole(columns), whole(d_mixed)],
        out_specs=whole(out),
    )(columns, d_mixed)


WORK = pltpu.VMEM((TOKENS, D), f32)
WIDE = pltpu.VMEM((TOKENS, 2 * HALF), bf16)
LOW = pltpu.VMEM((TOKENS, D), bf16)


def rise_body(flow, scalars, results, more):
    (here,) = scalars
    mixed, mid, second_own, second_other, active_own, active_other, slope = results
    work, wide, low, *chosen = more
    mixed_columns, offsets = flow(0, 1)
    for order in range(3):
        make_hot(offsets, order, chosen[order])
    mixed[:, 480:512] = jnp.zeros((TOKENS, 32), bf16)
    mixed[:, 0:480] = dot(row_move(True), mixed_columns[...]).astype(bf16)
    flow.out(0)
    end = tail_lanes(mixed[:, 0:480])
    rest, attn = flow(2, 3, 4, 5), flow(6, 7, 8, 9)
    for k in range(4):
        total = cols_dot(mixed[:, 0:384], attn[k][...]) + cols_dot(end, rest[k][...])
        wide[:, 512 * k : 512 * k + 512] = total.astype(bf16)
    unshuffle(here, chosen[0], wide, work)
    stream, vectors = flow(10, 11)

    def rows_first(span):
        value = stream[span, :] + work[span, :]
        mid[span, :] = value
        centered, scale = moments(value)
        low[span, :] = (centered * scale * vectors[1:2, :] + vectors[3:4, :]).astype(bf16)

    each_rows(rows_first)
    flow.out(1)
    shuffle(here, chosen[1], low, second_own, second_other)
    flow.out(2, 3)
    expand = flow(12, 13, 14, 15)

    def up(span):
        work[:, span] = group_sum(1, second_own, second_other, expand, span)

    each_chunk(D, up)

    def rows_active(span):
        value = work[span, :]
        root = np.float32(np.sqrt(2 / np.pi))
        square = value * value
        bend = jnp.tanh(value * (root + np.float32(root * 0.044715) * square))
        half = 0.5 * value
        low[span, :] = (half + half * bend).astype(bf16)
        inner = root + np.float32(3 * root * 0.044715) * square
        slope[span, :] = 0.5 + 0.5 * bend + (half * inner) * (1.0 - bend * bend)

    each_rows(rows_active)
    flow.out(6)
    shuffle(here, chosen[2], low, active_own, active_other)
    flow.out(4, 5)


def rise(here, mixed_columns, stream, vectors, offsets, qkv, attn, expand):
    outs = (
        (shape(TOKENS, 512), shape(TOKENS, D, f32))
        + (shape(TOKENS, HALF),) * 4
        + (shape(TOKENS, D, f32),)
    )
    return flowing(
        rise_body,
        (here,),
        (mixed_columns, offsets, *qkv, *attn, stream, vectors, *expand),
        outs,
        [WORK, WIDE, LOW, HOT, HOT, HOT],
        6e9,
        {i: (1280, 1536) for i in (2, 3, 4, 5)},
    )


def turn_body(flow, scalars, results, more):
    (here,) = scalars
    block_out, d_upward = results
    work, wide, chosen = more
    upstream, offsets = flow(0, 1)
    make_hot(offsets, 2, chosen)
    reduce = group_back(2, upstream, flow, 2, wide)
    unshuffle(here, chosen, wide, work)
    (slope,) = flow(6)

    def rows_upward(span):
        d_upward[span, :] = (slope[span, :] * work[span, :]).astype(bf16)

    each_rows(rows_upward)
    flow.out(1)
    active_own, active_other, mid = flow(7, 8, 9)

    def down(span):
        total = group_sum(2, active_own, active_other, reduce, span)
        block_out[:, span] = (mid[:, span] + total).astype(bf16)

    each_chunk(D, down)
    flow.out(0)


def turn(here, mid, active_own, active_other, slope, upstream, offsets, reduce):
    return flowing(
        turn_body,
        (here,),
        (upstream, offsets, *reduce, slope, active_own, active_other, mid),
        (shape(TOKENS, D), shape(TOKENS, D)),
        [WORK, WIDE, HOT],
        6e9,
    )


def fall_body(flow, scalars, results, more):
    (here,) = scalars
    d_mid, attn_own, attn_other, d_mixed, sums = results
    work, wide, low, chosen, chosen_next = more
    d_upward, offsets = flow(0, 1)
    make_hot(offsets, 1, chosen)
    make_hot(offsets, 0, chosen_next)
    group_back(1, d_upward, flow, 2, wide)
    unshuffle(here, chosen, wide, work)
    mid, upstream, vectors = flow(6, 7, 8)
    sums[...] = jnp.zeros(sums.shape, f32)

    def rows_back(span):
        base = upstream[span, :].astype(f32)
        grad = work[span, :]
        value, gain_part = norm_back(mid[span, :], grad, vectors[1:2, :], base)
        d_mid[span, :] = value
        low[span, :] = value.astype(bf16)
        sums[0:1, :] += jnp.sum(gain_part, axis=0, keepdims=True)
        sums[1:2, :] += jnp.sum(grad, axis=0, keepdims=True)

    each_rows(rows_back)
    flow.out(0, 4)
    shuffle(here, chosen_next, low, attn_own, attn_other)
    flow.out(1, 2)
    rest, attn = flow(9, 10, 11, 12), flow(13, 14, 15, 16)
    parts = pieces_of(attn_own, attn_other)
    back = sum(dot(p, w[...]) for p, w in zip(parts, attn)).astype(bf16)
    d_mixed[:, 0:384] = dot(row_move(), back).astype(bf16)
    back = sum(dot(p, w[...]) for p, w in zip(parts, rest)).astype(bf16)
    back = dot(row_move(), back).astype(bf16)
    source = lax.broadcasted_iota(jnp.int32, (256, 128), 0)
    target = lax.broadcasted_iota(jnp.int32, (256, 128), 1)
    d_mixed[:, 384:480] = dot(back, hot(source - 160, target))[:, 0:96].astype(bf16)
    flow.out(3)


def fall(here, d_upward, mid, upstream, vectors, offsets, expand, qkv, attn):
    outs = (
        shape(TOKENS, D, f32),
        shape(TOKENS, HALF),
        shape(TOKENS, HALF),
        shape(TOKENS, 480),
        shape(8, D, f32),
    )
    return flowing(
        fall_body,
        (here,),
        (d_upward, offsets, *expand, mid, upstream, vectors, *qkv, *attn),
        outs,
        [WORK, WIDE, LOW, HOT, HOT],
        5e9,
        {i: (1280, 1536) for i in (9, 10, 11, 12)},
    )


def last_body(flow, scalars, results, more):
    here, level = scalars
    d_stream, low_a, low_b, spread = results
    work, wide, totals, chosen = more
    d_packed, offsets = flow(0, 1)
    make_hot(offsets, 0, chosen)
    moved = dot(row_move(True), d_packed[:, 0:1440]).astype(bf16)
    for k in range(4):
        (weight,) = flow(2 + k)
        wide[:, 512 * k : 512 * k + 512] = cols_dot(moved, weight[:, 0:1440]).astype(bf16)
    unshuffle(here, chosen, wide, work)
    totals[...] = jnp.zeros(totals.shape, f32)
    stream, d_mid, vectors, sums, shard_column, marks = flow(6, 7, 8, 9, 10, 11)

    def rows(span):
        grad = work[span, :]
        value, gain_part = norm_back(stream[span, :], grad, vectors[0:1, :], d_mid[span, :])
        d_stream[span, :] = value
        low_a[span, :] = value[:, 0:1024].astype(bf16)
        low_b[span, :] = value[:, 1024:1920].astype(bf16)
        totals[0:1, :] += jnp.sum(gain_part, axis=0, keepdims=True)
        totals[2:3, :] += jnp.sum(grad, axis=0, keepdims=True)
        totals[6:7, :] += jnp.sum(value, axis=0, keepdims=True)

    each_rows(rows)
    flow.out(0, 1, 2)
    totals[1:2, :] = sums[0:1, :]
    totals[3:4, :] = sums[1:2, :]
    totals[4:5, :] = jnp.where(level[0] == 0, totals[6:7, :], 0.0)
    totals[5:6, :] = jnp.where(level[0] == 1, totals[6:7, :], 0.0)
    number = lax.broadcasted_iota(jnp.int32, (SHARDS, 8), 0)
    first = lax.broadcasted_iota(jnp.int32, (SHARDS, 8), 1) * 15
    inside = jnp.where((number >= first) & (number < first + 15) & (number < 90), 1.0, 0.0)
    repeated = dot(inside.astype(bf16), totals[...].astype(bf16))
    within = lax.broadcasted_iota(jnp.int32, (SHARDS, 1), 0)
    group = sum((within >= 15 * r).astype(jnp.int32) for r in range(1, 7))
    repeated = jnp.where(within - group * 15 == marks[1:2, :], repeated, 0.0).astype(bf16)
    spread[...] = cols_dot(hot(shard_column[:, 2:3], marks[0:1, :]), repeated).astype(bf16)
    flow.out(3)


def last(here, level, d_packed, stream, d_mid, vectors, sums, offsets, shard_column, marks, qkv):
    outs = (shape(TOKENS, D, f32), shape(TOKENS, 1024), shape(TOKENS, 896), shape(SHARDS, 128))
    return flowing(
        last_body,
        (here, level),
        (d_packed, offsets, *qkv, stream, d_mid, vectors, sums, shard_column, marks),
        outs,
        [WORK, WIDE, pltpu.VMEM((8, D), f32), HOT],
        6e9,
    )


def finish_kernel(kept0, got0, kept1, got1, kept2, got2, *outs):
    grad_qkv, grad_attn, grad_expand, grad_reduce, table, levels, gains, shifts = outs

    def total(kept, got, start, stop):
        return kept[:, start:stop].astype(f32) + got[:, start:stop].astype(f32)

    grad_attn[...] = total(kept0, got0, 0, 480)[:15]
    grad_qkv[...] = total(kept0, got0, 512, 1952)[:15]
    grad_expand[...] = total(kept1, got1, 0, 1920)[:15]
    table[:, 0:1024] = total(kept1, got1, 1920, 2944)
    grad_reduce[...] = total(kept2, got2, 0, 1920)[:15]
    table[:, 1024:1920] = total(kept2, got2, 1920, 2816)
    line = total(kept2, got2, 2816, 2944)[0:1]
    for target, first in ((gains, 0), (shifts, 2), (levels, 4)):
        for row in range(2):
            start = (first + row) * 15
            target[row : row + 1, :] = line[:, start : start + 15]


def finish(*pairs):
    outs = tuple(
        shape(*s, f32)
        for s in ((15, 1440), (15, 480), (15, D), (15, D), (16, D), (2, 15), (2, 15), (2, 15))
    )
    return call(
        finish_kernel,
        outs,
        grid=(1,),
        in_specs=[whole(v) for v in pairs],
        out_specs=outs_whole(outs),
    )(*pairs)


def body(
    hidden_in,
    cond_codes,
    level_ids,
    qkv_weight,
    attn_out_weight,
    mlp_in_weight,
    mlp_out_weight,
    code_table,
    level_table,
    norm_gain,
    norm_bias,
    grad_out,
):
    yl, co, yh, z, x = (lax.axis_index(name) for name in AXES)
    me = yl * 64 + co * 32 + yh * 16 + z * 4 + x
    here = jnp.stack((me, co))
    targets, offsets, shard_column, codes = places(here, cond_codes)
    shards = prepare(
        qkv_weight,
        attn_out_weight.T,
        mlp_in_weight,
        mlp_out_weight,
        code_table,
        norm_gain,
        norm_bias,
        level_table,
    )
    feature = np.arange(D, dtype=np.int32)
    marks = jnp.asarray(np.stack((feature // 15, feature % 15)))

    def exchanged(values, step):
        return [exchange(v, order, step) for v, order in zip(values, ORDERS)]

    def singles(lists):
        return [v for (v,) in lists]

    small = singles(join(shards, exchanged(shards, 0)))
    small, (targets, offsets, shard_column, codes) = lax.optimization_barrier(
        (small, (targets, offsets, shard_column, codes))
    )
    for step in (1, 2):
        small = singles(join(small, exchanged(small, step)))
    cuts = [((0, split), (split, v.shape[1])) for v, split in zip(small, SPLITS)]
    small = join(small, exchanged(small, 3), cuts)
    first, second = [v for v, _ in small], [v for _, v in small]
    first = singles(join(first, exchanged(first, 4)))
    first, second = lax.optimization_barrier((first, second))
    rests = exchanged(first, 5)
    second_got = exchanged(second, 4)
    pieces = [(h, r, swap_cores(h), swap_cores(r)) for h, r in zip(first, rests)]
    second = singles(join(second, second_got))
    pieces, second = lax.optimization_barrier((pieces, second))
    qkv, table_a, table_b = pieces
    rests = exchanged(second, 5)

    stream, first_own, first_other, packed, vectors = embed(
        here, level_ids, hidden_in[0], codes, targets, offsets, shard_column, marks, table_a, table_b, qkv
    )

    def over_blocks(value):
        return lax.all_to_all(value, BLK, split_axis=0, concat_axis=0, tiled=True)

    columns = over_blocks(packed)
    mixed = attend(columns)
    mixed, rests = lax.optimization_barrier((mixed, rests))
    mixed = over_blocks(mixed)
    attn, expand, reduce = [(h, r, swap_cores(h), swap_cores(r)) for h, r in zip(second, rests)]
    upstream = grad_out[0]
    upstream_got = swap_cores(upstream)
    mixed, mid, second_own, second_other, active_own, active_other, slope = rise(
        here, mixed, stream, vectors, offsets, qkv, attn, expand
    )
    reduce_grad = outer(2, active_own, swap_cores(active_other), upstream, upstream_got)
    second_got, mixed_got = swap_cores(second_other), swap_cores(mixed)
    active_own, reduce_grad = lax.optimization_barrier((active_own, reduce_grad))
    reduce_got = exchange(reduce_grad[1], ORDERS[2], 5)
    block_out, d_upward = turn(
        here, mid, active_own, active_other, slope, upstream, offsets, reduce
    )
    expand_grad = outer(1, second_own, second_got, d_upward, swap_cores(d_upward))
    d_upward, expand_grad = lax.optimization_barrier((d_upward, expand_grad))
    expand_got = exchange(expand_grad[1], ORDERS[1], 5)
    d_mid, attn_own, attn_other, d_mixed, sums = fall(
        here, d_upward, mid, upstream, vectors, offsets, expand, qkv, attn
    )
    d_mixed = over_blocks(d_mixed)
    attn_grad = outer(0, attn_own, swap_cores(attn_other), mixed, mixed_got)
    attn_got = exchange(attn_grad[1], ORDERS[0], 5)
    early = (attn_grad, expand_grad, reduce_grad)
    early_got = (attn_got, expand_got, reduce_got)
    first_got = swap_cores(first_other)
    codes_got = swap_cores(codes)

    d_packed = over_blocks(attend_back(columns, d_mixed))
    early = add_halves([[(kept, got)] for (kept, _), got in zip(early, early_got)])
    d_packed, early = lax.optimization_barrier((d_packed, early))
    early_got = exchanged([sent for _, sent in early], 4)
    qkv_grad = outer(0, first_own, first_got, d_packed, swap_cores(d_packed))
    d_packed, qkv_grad = lax.optimization_barrier((d_packed, qkv_grad))

    d_stream, low_a, low_b, small = last(
        here, level_ids, d_packed, stream, d_mid, vectors, sums, offsets, shard_column, marks, qkv
    )
    small = small[:64] + swap_cores(small[64:])
    grad_a = table_outer(3, codes, codes_got, low_a, swap_cores(low_a), targets)
    grad_b = table_outer(4, codes, codes_got, low_b, swap_cores(low_b), targets, small)
    late = [qkv_grad, grad_a, grad_b]
    late_got = exchanged([sent for _, sent in late], 5)
    late = add_halves([[(kept, got)] for (kept, _), got in zip(late, late_got)])
    late_got = exchanged([sent for _, sent in late], 4)
    sums = add_halves(
        [
            [(before, before_got), (kept, got)]
            for (before, _), before_got, (kept, _), got in zip(early, early_got, late, late_got)
        ]
    )
    for step in (3, 2, 1):
        got = exchanged([sent for _, sent in sums], step)
        sums = add_halves([[(kept, v)] for (kept, _), v in zip(sums, got)])
    got = exchanged([sent for _, sent in sums], 0)
    pairs = [v for (kept, _), mine in zip(sums, got) for v in (kept, mine)]
    grad_qkv, grad_attn, grad_expand, grad_reduce, grad_table, levels, gains, shifts = finish(*pairs)
    return (
        block_out[None],
        d_stream[None],
        grad_qkv,
        grad_attn.T,
        grad_expand,
        grad_reduce,
        grad_table,
        levels,
        gains,
        shifts,
    )


def solution(mesh):
    fine = Mesh(mesh.devices.reshape(2, 2, 2, 4, 4), AXES)
    return jax.shard_map(
        body,
        mesh=fine,
        in_specs=(
            P(WIN, BLK, None),
            P(WIN, BLK),
            P(WIN),
            P(AXES, None),
            P(None, AXES),
            P(AXES, None),
            P(AXES, None),
            P(AXES, None),
            P(None, AXES),
            P(None, AXES),
            P(None, AXES),
            P(WIN, BLK, None),
        ),
        out_specs=(
            P(WIN, BLK, None),
            P(WIN, BLK, None),
            P(AXES, None),
            P(None, AXES),
            P(AXES, None),
            P(AXES, None),
            P(AXES, None),
            P(None, AXES),
            P(None, AXES),
            P(None, AXES),
        ),
        check_vma=False,
    )
```

```python
import functools

import jax
import jax.numpy as jnp
import numpy as np
from jax import lax
from jax.experimental import pallas as pl
from jax.experimental.pallas import tpu as pltpu
from jax.sharding import Mesh, PartitionSpec as P

HEAD = 480
BLOCK = 128
RATIO = 4
D = 1920
SHARDS = 128
ROWS = 16
HALF = 1024
HALVES = (slice(0, HALF), slice(HALF, 2 * HALF))
SPLITS = (1536, 1024, 896)
TOKENS = 256
CHUNK = 640
MIB = 2**20
ROW_STEP = 128
epsilon = 1e-05
bf16 = jnp.bfloat16
f32 = jnp.float32
AXES = ("yl", "co", "yh", "z", "x")
WIN = ("yl", "co")
BLK = ("yh", "z", "x")
STEP_BITS = {"x": (1, 3), "z": (4, 12), "y": (64, 80)}
CORE_BIT = 32
ORDERS = (("x", "z", "y"), ("z", "y", "x"), ("y", "x", "z"))


def exchange(value, order, step):
    masks = STEP_BITS[order[step // 2]]
    pairs = [(i, i ^ masks[(step % 2) ^ ((i >> 5) & 1)]) for i in range(SHARDS)]
    return lax.ppermute(value, AXES, pairs)


def swap_cores(value):
    return lax.ppermute(value, AXES, [(i, i ^ CORE_BIT) for i in range(SHARDS)])


def call(kernel, out_shape, vmem=16, flops=0, **options):
    params = pltpu.CompilerParams(vmem_limit_bytes=vmem * MIB)

    def run(*args):
        outs = out_shape if isinstance(out_shape, tuple) else (out_shape,)
        size = sum(v.size * v.dtype.itemsize for v in args + outs)
        cost = pl.CostEstimate(flops=int(flops), bytes_accessed=size, transcendentals=0)
        return pl.pallas_call(
            kernel, out_shape=out_shape, compiler_params=params, cost_estimate=cost, **options
        )(*args)

    return run


def whole(v):
    return pl.BlockSpec(
        v.shape, lambda i: (0,) * len(v.shape), pipeline_mode=pl.Buffered(buffer_count=1)
    )


def outs_whole(shapes):
    return tuple(pl.BlockSpec(v.shape, lambda i: (0, 0)) for v in shapes)


def shape(rows, columns, dtype=bf16):
    return jax.ShapeDtypeStruct((rows, columns), dtype)


def dot(left, right):
    return jnp.dot(left, right, preferred_element_type=f32)


def rows_dot(left, right):
    return lax.dot_general(left, right, (((0,), (0,)), ((), ())), preferred_element_type=f32)


def cols_dot(left, right):
    return lax.dot_general(left, right, (((1,), (1,)), ((), ())), preferred_element_type=f32)


def hot(left, right):
    return jnp.where(left == right, 1.0, 0.0).astype(bf16)


def join_kernel(tiles, cuts, *refs):
    count = len(cuts)
    sources, targets = refs[: 2 * count], list(refs[2 * count :])
    step = pl.program_id(0)
    for i, spans in enumerate(cuts):
        mine, targets = targets[: len(spans)], targets[len(spans) :]
        for source, here in ((sources[2 * i], step < tiles), (sources[2 * i + 1], step >= tiles)):

            @pl.when(here)
            def _(source=source, mine=mine, spans=spans):
                for target, (start, stop) in zip(mine, spans):
                    target[...] = source[:, start:stop]


def join(firsts, seconds, cuts=None):
    rows = firsts[0].shape[0]
    cuts = cuts or [((0, v.shape[1]),) for v in firsts]
    tiles = max(rows // 128, 1)
    tile = rows // tiles
    specs, args = [], []
    for first, second in zip(firsts, seconds):
        columns = first.shape[1]
        specs += [
            pl.BlockSpec((tile, columns), lambda i: (jnp.minimum(i, tiles - 1), 0)),
            pl.BlockSpec((tile, columns), lambda i: (jnp.maximum(i - tiles, 0), 0)),
        ]
        args += [first, second]
    widths = [stop - start for spans in cuts for start, stop in spans]
    out = call(
        functools.partial(join_kernel, tiles, cuts),
        tuple(shape(2 * rows, width) for width in widths),
        grid=(2 * tiles,),
        in_specs=specs,
        out_specs=tuple(pl.BlockSpec((tile, width), lambda i: (i, 0)) for width in widths),
    )(*args)
    out = list(out)
    return [[out.pop(0) for _ in spans] for spans in cuts]


def add_kernel(groups, *refs):
    count = sum(4 if added else 2 for group in groups for added in group)
    sources, targets = refs[:count], refs[count:]
    for i, group in enumerate(groups):
        start = 0
        for added in group:
            mine, sources = sources[: 4 if added else 2], sources[4 if added else 2 :]
            span = slice(start, start + mine[0].shape[1])
            for half in range(2):
                value = mine[half][...]
                if added:
                    value = (value.astype(f32) + mine[half + 2][...].astype(f32)).astype(bf16)
                targets[2 * i + half][:, span] = value
            start = span.stop


def add_halves(groups):
    rows = groups[0][0][0].shape[0] // 2
    tiles = max(rows // 128, 1)
    tile = rows // tiles
    specs, args, widths = [], [], []
    for group in groups:
        for kept, got in group:
            columns = kept.shape[1]
            low = pl.BlockSpec((tile, columns), lambda i: (i, 0))
            high = pl.BlockSpec((tile, columns), lambda i: (i + tiles, 0))
            specs += [low, high] * (1 if got is None else 2)
            args += [kept, kept] + ([] if got is None else [got, got])
        widths.append(sum(kept.shape[1] for kept, _ in group))
    out = call(
        functools.partial(add_kernel, [[got is not None for _, got in group] for group in groups]),
        tuple(shape(rows, width) for width in widths for _ in range(2)),
        grid=(tiles,),
        in_specs=specs,
        out_specs=tuple(pl.BlockSpec((tile, width), lambda i: (i, 0)) for width in widths for _ in range(2)),
    )(*args)
    return [(out[2 * i], out[2 * i + 1]) for i in range(len(groups))]


def store_group(order, group, kept, sent, total):
    if order == 0:
        start = 256 * (group & 1)
        (kept, sent)[group >> 1][start : start + 256, :] = total
    for number in range(4 if order == 1 else 16 if order == 2 else 0):
        rows = 64 if order == 1 else ROWS
        half, offset = piece_place(order, number)
        start = offset + group * rows
        (kept, sent)[half][start : start + rows, :] = total[number * rows : number * rows + rows]


def piece_place(order, number):
    if order == 1:
        return number >> 1, 256 * (number & 1)
    return number >> 3, 256 * ((number >> 2) & 1) + 64 * (number & 3)


def outer_kernel(order, left, left_got, right, right_got, kept, sent, turned):
    @pl.when(pl.program_id(0) == 0)
    def _():
        turned[:, 0:256] = left[...].T
        turned[:, 256:512] = left_got[...].T

    for group in range(4):
        rows = slice(256 * group, 256 * group + 256)
        total = dot(turned[rows, 0:256], right[...]) + dot(turned[rows, 256:512], right_got[...])
        store_group(order, group, kept, sent, total.astype(bf16))


def outer(order, left, left_got, right, right_got):
    columns = right.shape[1]
    width = 640 if columns % 640 == 0 else 512
    outs = (shape(HALF // 2, columns), shape(HALF // 2, columns))
    tile = pl.BlockSpec((TOKENS, width), lambda i: (0, i))
    out = pl.BlockSpec((HALF // 2, width), lambda i: (0, i))
    return call(
        functools.partial(outer_kernel, order),
        outs,
        vmem=60 if order else 16,
        flops=2 * 512 * HALF * columns,
        grid=(columns // width,),
        in_specs=[whole(left), whole(left_got), tile, tile],
        out_specs=(out, out),
        scratch_shapes=[pltpu.VMEM((HALF, 512), bf16)],
    )(left, left_got, right, right_got)


def spread_kernel(mine, got, small, rows_a, rows_b, kept):
    for i, source in enumerate((mine, got)):
        rows_a[64 * i : 64 * i + 64, :] = source[:, 0:1152]
        rows_b[64 * i : 64 * i + 64, :] = source[:, 1152:2176]
    total = (small[...].astype(f32) + got[:, 2176:2304].astype(f32)).astype(bf16)
    kept[...] = total[0:32]
    rows_b[128:160, :] = jnp.zeros((32, 1024), bf16)
    rows_b[128:160, 0:128] = total[32:64]


def widen_kernel(mine_a, got_a, mine_b, got_b, small, rows_a, rows_b, kept):
    rows_a[0:128, :] = mine_a[...]
    rows_a[128:256, :] = got_a[...]
    rows_b[0:128, :] = mine_b[0:128, :]
    rows_b[128:256, :] = got_b[0:128, :]
    total = (small[...].astype(f32) + got_b[128:160, 0:128].astype(f32)).astype(bf16)
    kept[...] = total[0:16]
    rows_b[256:272, :] = jnp.zeros((16, 1024), bf16)
    rows_b[256:272, 0:128] = total[16:32]


def place_kernel(mine_a, got_a, mine_b, got_b, small, targets, grad_a, grad_b):
    for line, width, sources, target in (
        (3, 1024, (mine_a, got_a), grad_a),
        (4, 896, (mine_b, got_b), grad_b),
    ):
        total = None
        for source in sources:
            code = source[0:256, width : width + 128].astype(f32).astype(jnp.int32)
            chosen = hot(code[:, 0:1] * 16 + code[:, 1:2], targets[line : line + 1, 0:256])
            term = rows_dot(chosen, source[0:256, 0:width])
            total = term if total is None else total + term
        target[:, 0:width] = total.astype(bf16)
    total = (small[...].astype(f32) + got_b[256:272, 0:128].astype(f32)).astype(bf16)
    row = lax.broadcasted_iota(jnp.int32, (256, 16), 0)
    chunk = lax.broadcasted_iota(jnp.int32, (256, 16), 1)
    grad_b[:, 896:1024] = dot(hot(row, chunk * ROWS), total).astype(bf16)


def simple(kernel, outs, *args, flops=0):
    return call(
        kernel,
        outs,
        flops=flops,
        grid=(1,),
        in_specs=[whole(v) for v in args],
        out_specs=outs_whole(outs),
    )(*args)


def shard_tables():
    table = np.zeros((2, 8, SHARDS), np.int32)
    groups = np.zeros((2, 8, 16), np.int32)
    inside = (("x", "z"), ("z", "x"), ("x", "z"))
    for core in range(2):
        for number, order in enumerate(ORDERS):
            for place in range(SHARDS):
                here = core ^ (place >> 6)
                mask = (place >> 6) * CORE_BIT
                for step in range(6):
                    if (place >> step) & 1:
                        mask ^= STEP_BITS[order[step // 2]][(step % 2) ^ here]
                table[core, number, place] = mask
            for half in range(2):
                for place in range(16):
                    mask = 0
                    for step in range(4):
                        if (place >> step) & 1:
                            mask ^= STEP_BITS[inside[number][step // 2]][(step % 2) ^ core ^ half]
                    groups[core, 2 * number + half, place] = mask
    table[:, 3:5] = table[:, 1:3]
    lines = np.repeat(table, ROWS, axis=2)
    return lines, np.repeat(groups, ROWS, axis=2), table.transpose(0, 2, 1).copy()


def prepare_kernel(here, qkv, attn, expand, reduce, table, gain, shift, level, *refs):
    codes_line, lines, groups, shards = refs[:4]
    first, second, third, targets, offsets, shard_column, codes = refs[4:]
    for target in (first, second, third):
        target[...] = jnp.zeros(target.shape, bf16)
    first[0:15, 0:1440] = qkv[...]
    first[0:15, 1440:1536] = attn[:, 384:480]
    first[0:15, 1536:1920] = attn[:, 0:384]
    second[:, 0:1024] = table[:, 0:1024]
    second[0:15, 1024:2944] = expand[...]
    third[:, 0:896] = table[:, 1024:1920]
    third[0:15, 896:2816] = reduce[...]
    for number, ref in enumerate((gain, shift, level)):
        for row in range(2):
            start = (2 * number + row) * 15
            first[15:16, start : start + 15] = ref[row : row + 1, :]
    me, core = here[0], here[1]
    place = jnp.where(core == 0, lines[0], lines[1]) ^ me
    inside = lax.broadcasted_iota(jnp.int32, place.shape, 1) & 15
    targets[...] = place * 16 + inside
    place = jnp.where(core == 0, groups[0], groups[1]) ^ (me & 15)
    inside = lax.broadcasted_iota(jnp.int32, place.shape, 1) & 15
    offsets[...] = jnp.where(inside < 15, place * 15 + inside, -8192)
    shard_column[...] = jnp.where(core == 0, shards[0], shards[1]) ^ me
    row = jnp.right_shift(lax.broadcasted_iota(jnp.int32, (TOKENS, 64), 0), 2)
    column = lax.broadcasted_iota(jnp.int32, (TOKENS, 64), 1)
    spread = jnp.where(row == column, codes_line[...], 0)
    codes[...] = jnp.sum(spread, axis=1, keepdims=True)


def prepare(here, *args):
    i32 = jnp.int32
    args += tuple(jnp.asarray(t) for t in shard_tables())
    outs = (
        shape(16, 1920),
        shape(16, 2944),
        shape(16, 2816),
        shape(8, 2048, i32),
        shape(8, 256, i32),
        shape(SHARDS, 8, i32),
        shape(TOKENS, 1, i32),
    )
    return call(
        prepare_kernel,
        outs,
        vmem=60,
        grid=(1,),
        in_specs=[pl.BlockSpec(memory_space=pltpu.SMEM)] + [whole(v) for v in args],
        out_specs=outs_whole(outs),
    )(here, *args)


class Flow:
    def __init__(self, sources, buffers, targets, results, sem):
        count = len(sources)
        self.copies = [
            pltpu.make_async_copy(source, buffer, sem.at[i])
            for i, (source, buffer) in enumerate(zip(sources, buffers))
        ]
        self.buffers = buffers
        self.leaving = [
            pltpu.make_async_copy(result, target, sem.at[count + i])
            for i, (result, target) in enumerate(zip(results, targets))
        ]
        for copy in self.copies:
            copy.start()

    def __call__(self, *numbers):
        for number in numbers:
            self.copies[number].wait()
        return [self.buffers[number] for number in numbers]

    def out(self, *numbers):
        for number in numbers:
            self.leaving[number].start()

    def end(self):
        for copy in self.leaving:
            copy.wait()


def tail_lanes(value):
    source = lax.broadcasted_iota(jnp.int32, (480, 256), 0)
    target = lax.broadcasted_iota(jnp.int32, (480, 256), 1)
    return dot(value, hot(source, jnp.where(target >= 160, target + 224, -1))).astype(bf16)


def flowing(body, scalars, args, outs, extra, flops, cuts=None):
    anywhere = pl.BlockSpec(memory_space=pl.ANY)
    cuts = cuts or {}
    shapes = [
        (v.shape[0], cuts[i][1] - cuts[i][0]) if i in cuts else v.shape for i, v in enumerate(args)
    ]

    def kernel(*refs):
        first, sources, targets, buffers, results, (sem,), more = split_refs(
            refs, len(scalars), len(args), len(outs), len(args), len(outs), 1, len(extra)
        )
        sources = [
            ref.at[:, cuts[i][0] : cuts[i][1]] if i in cuts else ref for i, ref in enumerate(sources)
        ]
        flow = Flow(sources, buffers, targets, results, sem)
        body(flow, first, results, more)
        flow.end()

    return call(
        kernel,
        outs,
        vmem=60,
        flops=flops,
        in_specs=[pl.BlockSpec(memory_space=pltpu.SMEM)] * len(scalars) + [anywhere] * len(args),
        out_specs=(anywhere,) * len(outs),
        scratch_shapes=[pltpu.VMEM(dims, v.dtype) for dims, v in zip(shapes, args)]
        + [pltpu.VMEM(v.shape, v.dtype) for v in outs]
        + [pltpu.SemaphoreType.DMA((len(args) + len(outs),))]
        + extra,
    )(*scalars, *args)


def split_refs(refs, *counts):
    out, start = [], 0
    for count in counts:
        out.append(refs[start : start + count])
        start += count
    return out


def each_chunk(columns, body, width=CHUNK):
    for i in range(columns // width):
        body(slice(i * width, i * width + width))


def each_rows(body):
    @pl.loop(0, TOKENS // ROW_STEP)
    def _(i):
        body(pl.ds(pl.multiple_of(i * ROW_STEP, ROW_STEP), ROW_STEP))


SHIFT = 144
HOT = pltpu.VMEM((2, SHIFT + 384, 256), bf16)


def make_hot(offsets, order, chosen):
    for half in range(2):
        line = 2 * order + half
        feature = lax.broadcasted_iota(jnp.int32, (SHIFT + 384, 256), 0) - SHIFT
        chosen[half, :, :] = hot(feature, offsets[line : line + 1, :])


def group_window(here, half, group):
    core = here[1] ^ half
    number = jnp.right_shift(here[0], 4) ^ (2 * half)
    number = number ^ ((group & 1) * (4 + core)) ^ ((group >> 1) * (5 - core))
    first = number * 240
    start = jnp.minimum(jnp.right_shift(first, 7) * 128, D - 384)
    rows = pl.ds(pl.multiple_of(SHIFT + start - first, 16), 384)
    return pl.ds(pl.multiple_of(start, 128), 384), rows


def slot(group):
    return slice(group * 256, group * 256 + 256)


def shuffle(here, chosen, value, own, other):
    for half, target in enumerate((own, other)):
        for group in range(4):
            window, rows = group_window(here, half, group)
            target[:, slot(group)] = dot(value[:, window], chosen[half, rows, :]).astype(bf16)


def unshuffle(here, chosen, value, out):
    out[...] = jnp.zeros(out.shape, f32)
    for number in range(8):
        first = number * 240
        start = min(first // 128 * 128, D - 384)
        apart = jnp.right_shift(here[0], 4) ^ number
        half = jnp.right_shift(apart, 1) & 1
        core = here[1] ^ half
        low = apart & 1
        high = (jnp.right_shift(apart, 2) & 1) ^ low
        group = (high + 2 * low) * (1 - core) + (low + 2 * high) * core
        place = pl.ds(pl.multiple_of((4 * half + group) * 256, 256), 256)
        rows = slice(SHIFT + start - first, SHIFT + start - first + 384)
        out[:, start : start + 384] += cols_dot(value[:, place], chosen[half, rows, :])


def group_rows(order, pieces, half, group, span=slice(None)):
    rows = 64 if order == 1 else ROWS
    parts = []
    for number in range(256 // rows):
        piece, offset = piece_place(order, number)
        start = offset + group * rows
        start = start if isinstance(start, int) else pl.multiple_of(start, ROWS)
        parts.append(pieces[2 * half + piece][pl.ds(start, rows), span])
    return jnp.concatenate(parts, axis=0)


def group_sum(order, own, other, pieces, span):
    total = None
    for half, value in enumerate((own, other)):
        rows = [group_rows(order, pieces, half, group, span) for group in range(4)]
        term = dot(value[...], jnp.concatenate(rows, axis=0))
        total = term if total is None else total + term
    return total


def group_back(order, value, flow, first, wide):
    pieces = []
    for half in range(2):
        pieces += flow(first + 2 * half, first + 2 * half + 1)
        for group in range(4):
            term = cols_dot(value[...], group_rows(order, pieces, half, group))
            wide[:, slot(group + 4 * half)] = term.astype(bf16)
    return pieces


def pieces_of(own, other):
    return [ref[:, cut] for ref in (own, other) for cut in (slice(0, 512), slice(512, 1024))]


def row_move(transposed=False):
    row = lax.broadcasted_iota(jnp.int32, (TOKENS, TOKENS), 1 if transposed else 0)
    token = lax.broadcasted_iota(jnp.int32, (TOKENS, TOKENS), 0 if transposed else 1)
    moved = jnp.right_shift(row, 3) * 4 + (row & 3) + (jnp.right_shift(row, 2) & 1) * 128
    return hot(token, moved)


def moments(value):
    average = jnp.mean(value, axis=-1, keepdims=True)
    centered = value - average
    variance = jnp.mean(centered * centered, axis=-1, keepdims=True)
    return centered, lax.rsqrt(variance + epsilon)


def norm_back(value, grad, gain, base):
    centered, scale = moments(value)
    normed = centered * scale
    scaled = grad * gain
    inner = scaled - jnp.mean(scaled, axis=-1, keepdims=True)
    inner = inner - normed * jnp.mean(scaled * normed, axis=-1, keepdims=True)
    return base + scale * inner, grad * normed


def embed_body(flow, scalars, results, more):
    here, level = scalars
    stream, own, other, packed, vectors = results
    normed, chosen, looked = more
    codes, targets, offsets, shard_column, marks = flow(0, 1, 2, 3, 4)
    make_hot(offsets, 0, chosen)
    row = lax.broadcasted_iota(jnp.int32, (64, TOKENS), 0)
    token = lax.broadcasted_iota(jnp.int32, (64, TOKENS), 1)
    every = hot(row * RATIO, token)
    for line, first, start in ((3, 5, 0), (4, 9, 1024)):
        total = None
        for k in range(4):
            (table,) = flow(first + k)
            spread = hot(codes[...], targets[line : line + 1, 512 * k : 512 * k + 512])
            term = dot(dot(every, spread).astype(bf16), table[...])
            total = term if total is None else total + term
        looked[:, start : start + total.shape[1]] = total.astype(bf16)
    (hidden,) = flow(13)
    heads = flow(14, 15, 16, 17)
    chunk = lax.broadcasted_iota(jnp.int32, (SHARDS, 512), 0)
    row = lax.broadcasted_iota(jnp.int32, (SHARDS, 512), 1)
    lines = None
    for k in range(4):
        term = dot(hot(row + 512 * k, chunk * ROWS + 15), heads[k][...])
        lines = term if lines is None else lines + term
    spread = rows_dot(lines.astype(bf16), hot(shard_column[:, 0:1], marks[0:1, :]))
    within = lax.broadcasted_iota(jnp.int32, (SHARDS, 1), 0)
    group = sum((within >= 15 * r).astype(jnp.int32) for r in range(1, 7))
    spread = jnp.where(within - group * 15 == marks[1:2, :], spread, 0.0).astype(bf16)
    number = lax.broadcasted_iota(jnp.int32, (8, SHARDS), 1)
    first = lax.broadcasted_iota(jnp.int32, (8, SHARDS), 0) * 15
    inside = jnp.where((number >= first) & (number < first + 15), 1.0, 0.0).astype(bf16)
    vectors[...] = dot(inside, spread)
    flow.out(4)
    level_row = jnp.where(level[0] == 0, vectors[4:5, :], vectors[5:6, :])
    token = lax.broadcasted_iota(jnp.int32, (ROW_STEP, 64), 0)
    column = lax.broadcasted_iota(jnp.int32, (ROW_STEP, 64), 1)

    def rows(span):
        four = hot(jnp.right_shift(token + span.start, 2), column)
        value = dot(four, looked[...]) + hidden[span, :].astype(f32) + level_row
        stream[span, :] = value
        centered, scale = moments(value)
        normed[span, :] = (centered * scale * vectors[0:1, :] + vectors[2:3, :]).astype(bf16)

    each_rows(rows)
    flow.out(0)
    normed[...] = dot(row_move(), normed[...]).astype(bf16)
    shuffle(here, chosen, normed, own, other)
    flow.out(1, 2)
    weight = flow(18, 19, 20, 21)
    packed[...] = sum(dot(p, w[:, 0:1440]) for p, w in zip(pieces_of(own, other), weight)).astype(bf16)
    flow.out(3)


def embed(here, level, hidden, codes, targets, offsets, shard_column, marks, tables_a, tables_b, qkv):
    outs = (
        shape(TOKENS, D, f32),
        shape(TOKENS, HALF),
        shape(TOKENS, HALF),
        shape(TOKENS, 1440),
        shape(8, D, f32),
    )
    return flowing(
        embed_body,
        (here, level),
        (codes, targets, offsets, shard_column, marks, *tables_a, *tables_b, hidden, *qkv, *qkv),
        outs,
        [pltpu.VMEM((TOKENS, D), bf16), HOT, pltpu.VMEM((64, D), bf16)],
        8e9,
        {i: (0, 128) for i in (14, 15, 16, 17)},
    )


def probabilities(columns):
    query, key = columns[:, 0:480], columns[:, 480:960]
    row = lax.broadcasted_iota(jnp.int32, (TOKENS, TOKENS), 0)
    other = lax.broadcasted_iota(jnp.int32, (TOKENS, TOKENS), 1)
    mask = ((row & 3) == (other & 3)) & (jnp.right_shift(row, 2) >= jnp.right_shift(other, 2))
    scores = jnp.where(mask, cols_dot(query, key) * HEAD ** (-0.5), -1e30)
    top = jnp.max(scores, axis=-1, keepdims=True)
    total = top + jnp.log(jnp.sum(jnp.exp(scores - top), axis=-1, keepdims=True))
    return jnp.exp(scores - total)


def attend_kernel(columns, mixed):
    mixed[...] = dot(probabilities(columns).astype(bf16), columns[:, 960:1440]).astype(bf16)


def attend(columns):
    out = shape(TOKENS, 480)
    return call(
        attend_kernel, out, grid=(1,), in_specs=[whole(columns)], out_specs=whole(out)
    )(columns)


def attend_back_kernel(columns, d_mixed, d_packed):
    probs = probabilities(columns)
    low = probs.astype(bf16)
    d_probs = cols_dot(d_mixed[...], columns[:, 960:1440])
    d_scores = (probs * (d_probs - jnp.sum(probs * d_probs, axis=-1, keepdims=True))).astype(bf16)
    scale = HEAD ** (-0.5)
    d_packed[:, 0:480] = (dot(d_scores, columns[:, 480:960]) * scale).astype(bf16)
    d_packed[:, 480:960] = (rows_dot(d_scores, columns[:, 0:480]) * scale).astype(bf16)
    d_packed[:, 960:1440] = rows_dot(low, d_mixed[...]).astype(bf16)
    d_packed[:, 1440:1536] = jnp.zeros((TOKENS, 96), bf16)


def attend_back(columns, d_mixed):
    out = shape(TOKENS, 1536)
    return call(
        attend_back_kernel,
        out,
        grid=(1,),
        in_specs=[whole(columns), whole(d_mixed)],
        out_specs=whole(out),
    )(columns, d_mixed)


WORK = pltpu.VMEM((TOKENS, D), f32)
WIDE = pltpu.VMEM((TOKENS, 2 * HALF), bf16)
LOW = pltpu.VMEM((TOKENS, D), bf16)


def rise_body(flow, scalars, results, more):
    (here,) = scalars
    mixed, mid, second_own, second_other, active_own, active_other, slope = results
    work, wide, low, *chosen = more
    mixed_columns, offsets = flow(0, 1)
    for order in range(3):
        make_hot(offsets, order, chosen[order])
    mixed[:, 480:512] = jnp.zeros((TOKENS, 32), bf16)
    mixed[:, 0:480] = dot(row_move(True), mixed_columns[...]).astype(bf16)
    flow.out(0)
    end = tail_lanes(mixed[:, 0:480])
    rest, attn = flow(2, 3, 4, 5), flow(6, 7, 8, 9)
    for k in range(4):
        total = cols_dot(mixed[:, 0:384], attn[k][...]) + cols_dot(end, rest[k][...])
        wide[:, 512 * k : 512 * k + 512] = total.astype(bf16)
    unshuffle(here, chosen[0], wide, work)
    stream, vectors = flow(10, 11)

    def rows_first(span):
        value = stream[span, :] + work[span, :]
        mid[span, :] = value
        centered, scale = moments(value)
        low[span, :] = (centered * scale * vectors[1:2, :] + vectors[3:4, :]).astype(bf16)

    each_rows(rows_first)
    flow.out(1)
    shuffle(here, chosen[1], low, second_own, second_other)
    flow.out(2, 3)
    expand = flow(12, 13, 14, 15)

    def up(span):
        work[:, span] = group_sum(1, second_own, second_other, expand, span)

    each_chunk(D, up)

    def rows_active(span):
        value = work[span, :]
        root = np.float32(np.sqrt(2 / np.pi))
        square = value * value
        bend = jnp.tanh(value * (root + np.float32(root * 0.044715) * square))
        half = 0.5 * value
        low[span, :] = (half + half * bend).astype(bf16)
        inner = root + np.float32(3 * root * 0.044715) * square
        slope[span, :] = 0.5 + 0.5 * bend + (half * inner) * (1.0 - bend * bend)

    each_rows(rows_active)
    flow.out(6)
    shuffle(here, chosen[2], low, active_own, active_other)
    flow.out(4, 5)


def rise(here, mixed_columns, stream, vectors, offsets, qkv, attn, expand):
    outs = (
        (shape(TOKENS, 512), shape(TOKENS, D, f32))
        + (shape(TOKENS, HALF),) * 4
        + (shape(TOKENS, D, f32),)
    )
    return flowing(
        rise_body,
        (here,),
        (mixed_columns, offsets, *qkv, *attn, stream, vectors, *expand),
        outs,
        [WORK, WIDE, LOW, HOT, HOT, HOT],
        6e9,
        {i: (1280, 1536) for i in (2, 3, 4, 5)},
    )


def turn_body(flow, scalars, results, more):
    (here,) = scalars
    block_out, d_upward = results
    work, wide, chosen = more
    upstream, offsets = flow(0, 1)
    make_hot(offsets, 2, chosen)
    reduce = group_back(2, upstream, flow, 2, wide)
    unshuffle(here, chosen, wide, work)
    (slope,) = flow(6)

    def rows_upward(span):
        d_upward[span, :] = (slope[span, :] * work[span, :]).astype(bf16)

    each_rows(rows_upward)
    flow.out(1)
    active_own, active_other, mid = flow(7, 8, 9)

    def down(span):
        total = group_sum(2, active_own, active_other, reduce, span)
        block_out[:, span] = (mid[:, span] + total).astype(bf16)

    each_chunk(D, down)
    flow.out(0)


def turn(here, mid, active_own, active_other, slope, upstream, offsets, reduce):
    return flowing(
        turn_body,
        (here,),
        (upstream, offsets, *reduce, slope, active_own, active_other, mid),
        (shape(TOKENS, D), shape(TOKENS, D)),
        [WORK, WIDE, HOT],
        6e9,
    )


def fall_body(flow, scalars, results, more):
    (here,) = scalars
    d_mid, attn_own, attn_other, d_mixed, sums = results
    work, wide, low, chosen, chosen_next = more
    d_upward, offsets = flow(0, 1)
    make_hot(offsets, 1, chosen)
    make_hot(offsets, 0, chosen_next)
    group_back(1, d_upward, flow, 2, wide)
    unshuffle(here, chosen, wide, work)
    mid, upstream, vectors = flow(6, 7, 8)
    sums[...] = jnp.zeros(sums.shape, f32)

    def rows_back(span):
        base = upstream[span, :].astype(f32)
        grad = work[span, :]
        value, gain_part = norm_back(mid[span, :], grad, vectors[1:2, :], base)
        d_mid[span, :] = value
        low[span, :] = value.astype(bf16)
        sums[0:1, :] += jnp.sum(gain_part, axis=0, keepdims=True)
        sums[1:2, :] += jnp.sum(grad, axis=0, keepdims=True)

    each_rows(rows_back)
    flow.out(0, 4)
    shuffle(here, chosen_next, low, attn_own, attn_other)
    flow.out(1, 2)
    rest, attn = flow(9, 10, 11, 12), flow(13, 14, 15, 16)
    parts = pieces_of(attn_own, attn_other)
    back = sum(dot(p, w[...]) for p, w in zip(parts, attn)).astype(bf16)
    d_mixed[:, 0:384] = dot(row_move(), back).astype(bf16)
    back = sum(dot(p, w[...]) for p, w in zip(parts, rest)).astype(bf16)
    back = dot(row_move(), back).astype(bf16)
    source = lax.broadcasted_iota(jnp.int32, (256, 128), 0)
    target = lax.broadcasted_iota(jnp.int32, (256, 128), 1)
    d_mixed[:, 384:480] = dot(back, hot(source - 160, target))[:, 0:96].astype(bf16)
    flow.out(3)


def fall(here, d_upward, mid, upstream, vectors, offsets, expand, qkv, attn):
    outs = (
        shape(TOKENS, D, f32),
        shape(TOKENS, HALF),
        shape(TOKENS, HALF),
        shape(TOKENS, 480),
        shape(8, D, f32),
    )
    return flowing(
        fall_body,
        (here,),
        (d_upward, offsets, *expand, mid, upstream, vectors, *qkv, *attn),
        outs,
        [WORK, WIDE, LOW, HOT, HOT],
        5e9,
        {i: (1280, 1536) for i in (9, 10, 11, 12)},
    )


def last_body(flow, scalars, results, more):
    here, level = scalars
    d_stream, sums_out, small = results
    work, wide, totals, chosen, low = more
    d_packed, offsets = flow(0, 1)
    make_hot(offsets, 0, chosen)
    moved = dot(row_move(True), d_packed[:, 0:1440]).astype(bf16)
    for k in range(4):
        (weight,) = flow(2 + k)
        wide[:, 512 * k : 512 * k + 512] = cols_dot(moved, weight[:, 0:1440]).astype(bf16)
    unshuffle(here, chosen, wide, work)
    totals[...] = jnp.zeros(totals.shape, f32)
    stream, d_mid, vectors, sums, shard_column, marks, codes = flow(6, 7, 8, 9, 10, 11, 12)

    def rows(span):
        grad = work[span, :]
        value, gain_part = norm_back(stream[span, :], grad, vectors[0:1, :], d_mid[span, :])
        d_stream[span, :] = value
        low[span, :] = value.astype(bf16)
        totals[0:1, :] += jnp.sum(gain_part, axis=0, keepdims=True)
        totals[2:3, :] += jnp.sum(grad, axis=0, keepdims=True)
        totals[6:7, :] += jnp.sum(value, axis=0, keepdims=True)

    each_rows(rows)
    flow.out(0)
    row = lax.broadcasted_iota(jnp.int32, (64, TOKENS), 0)
    token = lax.broadcasted_iota(jnp.int32, (64, TOKENS), 1)
    every = hot(row, jnp.right_shift(token, 2))
    sums_out[:, 0:1024] = dot(every, low[:, 0:1024]).astype(bf16)
    sums_out[:, 1152:2048] = dot(every, low[:, 1024:1920]).astype(bf16)
    lane = lax.broadcasted_iota(jnp.int32, (TOKENS, 128), 1)
    code = codes[...]
    code = jnp.where(lane == 0, jnp.right_shift(code, 4), jnp.where(lane == 1, code & 15, 0))
    code = dot(hot(row * RATIO, token), code.astype(f32).astype(bf16)).astype(bf16)
    sums_out[:, 1024:1152] = code
    sums_out[:, 2048:2176] = code
    totals[1:2, :] = sums[0:1, :]
    totals[3:4, :] = sums[1:2, :]
    totals[4:5, :] = jnp.where(level[0] == 0, totals[6:7, :], 0.0)
    totals[5:6, :] = jnp.where(level[0] == 1, totals[6:7, :], 0.0)
    number = lax.broadcasted_iota(jnp.int32, (SHARDS, 8), 0)
    first = lax.broadcasted_iota(jnp.int32, (SHARDS, 8), 1) * 15
    inside = jnp.where((number >= first) & (number < first + 15) & (number < 90), 1.0, 0.0)
    repeated = dot(inside.astype(bf16), totals[...].astype(bf16))
    within = lax.broadcasted_iota(jnp.int32, (SHARDS, 1), 0)
    group = sum((within >= 15 * r).astype(jnp.int32) for r in range(1, 7))
    repeated = jnp.where(within - group * 15 == marks[1:2, :], repeated, 0.0).astype(bf16)
    spread = cols_dot(hot(shard_column[:, 2:3], marks[0:1, :]), repeated).astype(bf16)
    small[...] = spread[0:64]
    sums_out[:, 2176:2304] = spread[64:128]
    flow.out(1, 2)


def last(here, level, d_packed, stream, d_mid, vectors, sums, offsets, shard_column, marks, codes, qkv):
    outs = (shape(TOKENS, D, f32), shape(64, 2304), shape(64, 128))
    return flowing(
        last_body,
        (here, level),
        (d_packed, offsets, *qkv, stream, d_mid, vectors, sums, shard_column, marks, codes),
        outs,
        [WORK, WIDE, pltpu.VMEM((8, D), f32), HOT, LOW],
        6e9,
    )


def finish_kernel(kept0, got0, kept1, got1, kept2, got2, *outs):
    grad_qkv, grad_attn, grad_expand, grad_reduce, table, levels, gains, shifts = outs

    def total(kept, got, start, stop):
        return kept[:, start:stop].astype(f32) + got[:, start:stop].astype(f32)

    grad_attn[...] = total(kept0, got0, 0, 480)[:15]
    grad_qkv[...] = total(kept0, got0, 512, 1952)[:15]
    grad_expand[...] = total(kept1, got1, 0, 1920)[:15]
    table[:, 0:1024] = total(kept1, got1, 1920, 2944)
    grad_reduce[...] = total(kept2, got2, 0, 1920)[:15]
    table[:, 1024:1920] = total(kept2, got2, 1920, 2816)
    line = total(kept2, got2, 2816, 2944)[0:1]
    for target, first in ((gains, 0), (shifts, 2), (levels, 4)):
        for row in range(2):
            start = (first + row) * 15
            target[row : row + 1, :] = line[:, start : start + 15]


def finish(*pairs):
    outs = tuple(
        shape(*s, f32)
        for s in ((15, 1440), (15, 480), (15, D), (15, D), (16, D), (2, 15), (2, 15), (2, 15))
    )
    return call(
        finish_kernel,
        outs,
        grid=(1,),
        in_specs=[whole(v) for v in pairs],
        out_specs=outs_whole(outs),
    )(*pairs)


def body(
    hidden_in,
    cond_codes,
    level_ids,
    qkv_weight,
    attn_out_weight,
    mlp_in_weight,
    mlp_out_weight,
    code_table,
    level_table,
    norm_gain,
    norm_bias,
    grad_out,
):
    yl, co, yh, z, x = (lax.axis_index(name) for name in AXES)
    me = yl * 64 + co * 32 + yh * 16 + z * 4 + x
    here = jnp.stack((me, co))
    *shards, targets, offsets, shard_column, codes = prepare(
        here,
        qkv_weight,
        attn_out_weight.T,
        mlp_in_weight,
        mlp_out_weight,
        code_table,
        norm_gain,
        norm_bias,
        level_table,
        cond_codes,
    )
    feature = np.arange(D, dtype=np.int32)
    marks = jnp.asarray(np.stack((feature // 15, feature % 15)))

    def exchanged(values, step):
        return [exchange(v, order, step) for v, order in zip(values, ORDERS)]

    def singles(lists):
        return [v for (v,) in lists]

    small = singles(join(shards, exchanged(shards, 0)))
    for step in (1, 2):
        small = singles(join(small, exchanged(small, step)))
    cuts = [((0, split), (split, v.shape[1])) for v, split in zip(small, SPLITS)]
    small = join(small, exchanged(small, 3), cuts)
    first, second = [v for v, _ in small], [v for _, v in small]
    first = singles(join(first, exchanged(first, 4)))
    first, second = lax.optimization_barrier((first, second))
    rests = exchanged(first, 5)
    second_got = exchanged(second, 4)
    pieces = [(h, r, swap_cores(h), swap_cores(r)) for h, r in zip(first, rests)]
    second = singles(join(second, second_got))
    pieces, second = lax.optimization_barrier((pieces, second))
    qkv, table_a, table_b = pieces
    rests = exchanged(second, 5)

    stream, first_own, first_other, packed, vectors = embed(
        here, level_ids, hidden_in[0], codes, targets, offsets, shard_column, marks, table_a, table_b, qkv
    )

    def over_blocks(value):
        return lax.all_to_all(value, BLK, split_axis=0, concat_axis=0, tiled=True)

    columns = over_blocks(packed)
    mixed = attend(columns)
    mixed, rests = lax.optimization_barrier((mixed, rests))
    mixed = over_blocks(mixed)
    attn, expand, reduce = [(h, r, swap_cores(h), swap_cores(r)) for h, r in zip(second, rests)]
    upstream = grad_out[0]
    upstream_got = swap_cores(upstream)
    mixed, mid, second_own, second_other, active_own, active_other, slope = rise(
        here, mixed, stream, vectors, offsets, qkv, attn, expand
    )
    reduce_grad = outer(2, active_own, swap_cores(active_other), upstream, upstream_got)
    second_got, mixed_got = swap_cores(second_other), swap_cores(mixed)
    active_own, reduce_grad = lax.optimization_barrier((active_own, reduce_grad))
    reduce_got = exchange(reduce_grad[1], ORDERS[2], 5)
    block_out, d_upward = turn(
        here, mid, active_own, active_other, slope, upstream, offsets, reduce
    )
    expand_grad = outer(1, second_own, second_got, d_upward, swap_cores(d_upward))
    d_upward, expand_grad = lax.optimization_barrier((d_upward, expand_grad))
    expand_got = exchange(expand_grad[1], ORDERS[1], 5)
    d_mid, attn_own, attn_other, d_mixed, sums = fall(
        here, d_upward, mid, upstream, vectors, offsets, expand, qkv, attn
    )
    d_mixed = over_blocks(d_mixed)
    attn_grad = outer(0, attn_own, swap_cores(attn_other), mixed, mixed_got)
    attn_got = exchange(attn_grad[1], ORDERS[0], 5)
    d_mixed, attn_grad = lax.optimization_barrier((d_mixed, attn_grad))
    first_got = swap_cores(first_other)

    d_packed = over_blocks(attend_back(columns, d_mixed))
    early = add_halves([[(expand_grad[0], expand_got)], [(reduce_grad[0], reduce_got)]])
    early_got = [exchange(sent, order, 4) for (_, sent), order in zip(early, ORDERS[1:])]
    d_packed, early = lax.optimization_barrier((d_packed, early))
    qkv_grad = outer(0, first_own, first_got, d_packed, swap_cores(d_packed))
    qkv_got = exchange(qkv_grad[1], ORDERS[0], 5)
    d_packed, qkv_grad, early_got, attn_got = lax.optimization_barrier(
        (d_packed, qkv_grad, early_got, attn_got)
    )

    d_stream, code_sums, small = last(
        here, level_ids, d_packed, stream, d_mid, vectors, sums, offsets, shard_column, marks, codes, qkv
    )
    outs = (shape(128, 1152), shape(160, 1024), shape(32, 128))
    rows_a, rows_b, small = simple(spread_kernel, outs, code_sums, swap_cores(code_sums), small)
    got_a, got_b = exchange(rows_a, ORDERS[1], 5), exchange(rows_b, ORDERS[2], 5)
    qkv_got, _ = lax.optimization_barrier((qkv_got, (got_a, got_b)))
    (first_sums,) = add_halves([[(attn_grad[0], attn_got), (qkv_grad[0], qkv_got)]])
    first_got = exchange(first_sums[1], ORDERS[0], 4)
    outs = (shape(256, 1152), shape(272, 1024), shape(16, 128))
    rows_a, rows_b, small = simple(widen_kernel, outs, rows_a, got_a, rows_b, got_b, small)
    got_a, got_b = exchange(rows_a, ORDERS[1], 4), exchange(rows_b, ORDERS[2], 4)
    outs = (shape(256, 1024), shape(256, 1024))
    grad_a, grad_b = simple(
        place_kernel, outs, rows_a, got_a, rows_b, got_b, small, targets, flops=1e9
    )
    sums = add_halves(
        [
            [(first_sums[0], first_got)],
            [(early[0][0], early_got[0]), (grad_a, None)],
            [(early[1][0], early_got[1]), (grad_b, None)],
        ]
    )
    for step in (3, 2, 1):
        got = exchanged([sent for _, sent in sums], step)
        sums = add_halves([[(kept, v)] for (kept, _), v in zip(sums, got)])
    got = exchanged([sent for _, sent in sums], 0)
    pairs = [v for (kept, _), mine in zip(sums, got) for v in (kept, mine)]
    grad_qkv, grad_attn, grad_expand, grad_reduce, grad_table, levels, gains, shifts = finish(*pairs)
    return (
        block_out[None],
        d_stream[None],
        grad_qkv,
        grad_attn.T,
        grad_expand,
        grad_reduce,
        grad_table,
        levels,
        gains,
        shifts,
    )


def solution(mesh):
    fine = Mesh(mesh.devices.reshape(2, 2, 2, 4, 4), AXES)
    return jax.shard_map(
        body,
        mesh=fine,
        in_specs=(
            P(WIN, BLK, None),
            P(WIN, BLK),
            P(WIN),
            P(AXES, None),
            P(None, AXES),
            P(AXES, None),
            P(AXES, None),
            P(AXES, None),
            P(None, AXES),
            P(None, AXES),
            P(None, AXES),
            P(WIN, BLK, None),
        ),
        out_specs=(
            P(WIN, BLK, None),
            P(WIN, BLK, None),
            P(AXES, None),
            P(None, AXES),
            P(AXES, None),
            P(AXES, None),
            P(AXES, None),
            P(None, AXES),
            P(None, AXES),
            P(None, AXES),
        ),
        check_vma=False,
    )
```

```python
import functools

import jax
import jax.numpy as jnp
import numpy as np
from jax import lax
from jax.experimental import pallas as pl
from jax.experimental.pallas import tpu as pltpu
from jax.sharding import Mesh, PartitionSpec as P

HEAD = 480
BLOCK = 128
RATIO = 4
D = 1920
SHARDS = 128
ROWS = 16
HALF = 1024
HALVES = (slice(0, HALF), slice(HALF, 2 * HALF))
SPLITS = (1536, 1024, 896)
TOKENS = 256
CHUNK = 640
MIB = 2**20
ROW_STEP = 128
epsilon = 1e-05
bf16 = jnp.bfloat16
f32 = jnp.float32
AXES = ("yl", "co", "yh", "z", "x")
WIN = ("yl", "co")
BLK = ("yh", "z", "x")
STEP_BITS = {"x": (1, 3), "z": (4, 12), "y": (64, 80)}
CORE_BIT = 32
ORDERS = (("x", "z", "y"), ("z", "y", "x"), ("y", "x", "z"))


def exchange(value, order, step):
    masks = STEP_BITS[order[step // 2]]
    pairs = [(i, i ^ masks[(step % 2) ^ ((i >> 5) & 1)]) for i in range(SHARDS)]
    return lax.ppermute(value, AXES, pairs)


def swap_cores(value):
    return lax.ppermute(value, AXES, [(i, i ^ CORE_BIT) for i in range(SHARDS)])


def call(kernel, out_shape, vmem=16, flops=0, **options):
    params = pltpu.CompilerParams(vmem_limit_bytes=vmem * MIB)

    def run(*args):
        outs = out_shape if isinstance(out_shape, tuple) else (out_shape,)
        size = sum(v.size * v.dtype.itemsize for v in args + outs)
        cost = pl.CostEstimate(flops=int(flops), bytes_accessed=size, transcendentals=0)
        return pl.pallas_call(
            kernel, out_shape=out_shape, compiler_params=params, cost_estimate=cost, **options
        )(*args)

    return run


def whole(v):
    return pl.BlockSpec(
        v.shape, lambda i: (0,) * len(v.shape), pipeline_mode=pl.Buffered(buffer_count=1)
    )


def outs_whole(shapes):
    return tuple(pl.BlockSpec(v.shape, lambda i: (0, 0)) for v in shapes)


def shape(rows, columns, dtype=bf16):
    return jax.ShapeDtypeStruct((rows, columns), dtype)


def dot(left, right):
    return jnp.dot(left, right, preferred_element_type=f32)


def rows_dot(left, right):
    return lax.dot_general(left, right, (((0,), (0,)), ((), ())), preferred_element_type=f32)


def cols_dot(left, right):
    return lax.dot_general(left, right, (((1,), (1,)), ((), ())), preferred_element_type=f32)


def hot(left, right):
    return jnp.where(left == right, 1.0, 0.0).astype(bf16)


def join_kernel(tiles, cuts, *refs):
    count = len(cuts)
    sources, targets = refs[: 2 * count], list(refs[2 * count :])
    step = pl.program_id(0)
    for i, spans in enumerate(cuts):
        mine, targets = targets[: len(spans)], targets[len(spans) :]
        for source, here in ((sources[2 * i], step < tiles), (sources[2 * i + 1], step >= tiles)):

            @pl.when(here)
            def _(source=source, mine=mine, spans=spans):
                for target, (start, stop) in zip(mine, spans):
                    target[...] = source[:, start:stop]


def join(firsts, seconds, cuts=None):
    rows = firsts[0].shape[0]
    cuts = cuts or [((0, v.shape[1]),) for v in firsts]
    tiles = max(rows // 128, 1)
    tile = rows // tiles
    specs, args = [], []
    for first, second in zip(firsts, seconds):
        columns = first.shape[1]
        specs += [
            pl.BlockSpec((tile, columns), lambda i: (jnp.minimum(i, tiles - 1), 0)),
            pl.BlockSpec((tile, columns), lambda i: (jnp.maximum(i - tiles, 0), 0)),
        ]
        args += [first, second]
    widths = [stop - start for spans in cuts for start, stop in spans]
    out = call(
        functools.partial(join_kernel, tiles, cuts),
        tuple(shape(2 * rows, width) for width in widths),
        grid=(2 * tiles,),
        in_specs=specs,
        out_specs=tuple(pl.BlockSpec((tile, width), lambda i: (i, 0)) for width in widths),
    )(*args)
    out = list(out)
    return [[out.pop(0) for _ in spans] for spans in cuts]


def add_kernel(groups, *refs):
    count = sum(4 if added else 2 for group in groups for added in group)
    sources, targets = refs[:count], refs[count:]
    for i, group in enumerate(groups):
        start = 0
        for added in group:
            mine, sources = sources[: 4 if added else 2], sources[4 if added else 2 :]
            span = slice(start, start + mine[0].shape[1])
            for half in range(2):
                value = mine[half][...]
                if added:
                    value = (value.astype(f32) + mine[half + 2][...].astype(f32)).astype(bf16)
                targets[2 * i + half][:, span] = value
            start = span.stop


def add_halves(groups):
    rows = groups[0][0][0].shape[0] // 2
    tiles = max(rows // 128, 1)
    tile = rows // tiles
    specs, args, widths = [], [], []
    for group in groups:
        for kept, got in group:
            columns = kept.shape[1]
            low = pl.BlockSpec((tile, columns), lambda i: (i, 0))
            high = pl.BlockSpec((tile, columns), lambda i: (i + tiles, 0))
            specs += [low, high] * (1 if got is None else 2)
            args += [kept, kept] + ([] if got is None else [got, got])
        widths.append(sum(kept.shape[1] for kept, _ in group))
    out = call(
        functools.partial(add_kernel, [[got is not None for _, got in group] for group in groups]),
        tuple(shape(rows, width) for width in widths for _ in range(2)),
        grid=(tiles,),
        in_specs=specs,
        out_specs=tuple(pl.BlockSpec((tile, width), lambda i: (i, 0)) for width in widths for _ in range(2)),
    )(*args)
    return [(out[2 * i], out[2 * i + 1]) for i in range(len(groups))]


def store_group(order, group, kept, sent, total):
    if order == 0:
        start = 256 * (group & 1)
        (kept, sent)[group >> 1][start : start + 256, :] = total
    for number in range(4 if order == 1 else 16 if order == 2 else 0):
        rows = 64 if order == 1 else ROWS
        half, offset = piece_place(order, number)
        start = offset + group * rows
        (kept, sent)[half][start : start + rows, :] = total[number * rows : number * rows + rows]


def piece_place(order, number):
    if order == 1:
        return number >> 1, 256 * (number & 1)
    return number >> 3, 256 * ((number >> 2) & 1) + 64 * (number & 3)


def outer_kernel(order, left, left_got, right, right_got, kept, sent, turned):
    @pl.when(pl.program_id(0) == 0)
    def _():
        turned[:, 0:256] = left[...].T
        turned[:, 256:512] = left_got[...].T

    for group in range(4):
        rows = slice(256 * group, 256 * group + 256)
        total = dot(turned[rows, 0:256], right[...]) + dot(turned[rows, 256:512], right_got[...])
        store_group(order, group, kept, sent, total.astype(bf16))


def outer(order, left, left_got, right, right_got):
    columns = right.shape[1]
    width = 640 if columns % 640 == 0 else 512
    outs = (shape(HALF // 2, columns), shape(HALF // 2, columns))
    tile = pl.BlockSpec((TOKENS, width), lambda i: (0, i))
    out = pl.BlockSpec((HALF // 2, width), lambda i: (0, i))
    return call(
        functools.partial(outer_kernel, order),
        outs,
        vmem=60 if order else 16,
        flops=2 * 512 * HALF * columns,
        grid=(columns // width,),
        in_specs=[whole(left), whole(left_got), tile, tile],
        out_specs=(out, out),
        scratch_shapes=[pltpu.VMEM((HALF, 512), bf16)],
    )(left, left_got, right, right_got)


def pair_kernel(one, one_got, two, two_got, right, right_got, other, other_got, kept, sent, turned):
    def run(left, left_got, right, right_got):
        turned[:, 0:256] = left[...].T
        turned[:, 256:512] = left_got[...].T
        for cut in range(0, right.shape[1], 512):
            span = slice(cut, cut + 512)
            for half, target in enumerate((kept, sent)):
                rows = slice(512 * half, 512 * half + 512)
                total = dot(turned[rows, 0:256], right[:, span])
                total = total + dot(turned[rows, 256:512], right_got[:, span])
                target[:, span] = total.astype(bf16)

    @pl.when(pl.program_id(0) == 0)
    def _():
        run(one, one_got, other, other_got)

    @pl.when(pl.program_id(0) > 0)
    def _():
        run(two, two_got, right, right_got)


def outer_pair(first, second):
    one, one_got, other, other_got = first
    two, two_got, right, right_got = second
    outs = (shape(HALF // 2, 2048), shape(HALF // 2, 2048))
    tile = pl.BlockSpec((TOKENS, 512), lambda i: (0, jnp.maximum(i - 1, 0)))
    out = pl.BlockSpec((HALF // 2, 512), lambda i: (0, i))
    return call(
        pair_kernel,
        outs,
        flops=2 * 512 * HALF * 2048,
        grid=(4,),
        in_specs=[whole(v) for v in (one, one_got, two, two_got)]
        + [tile, tile, whole(other), whole(other_got)],
        out_specs=(out, out),
        scratch_shapes=[pltpu.VMEM((HALF, 512), bf16)],
    )(one, one_got, two, two_got, right, right_got, other, other_got)


def spread_kernel(mine, got, small, rows_a, rows_b, kept):
    for i, source in enumerate((mine, got)):
        rows_a[64 * i : 64 * i + 64, :] = source[:, 0:1152]
        rows_b[64 * i : 64 * i + 64, :] = source[:, 1152:2176]
    total = (small[...].astype(f32) + got[:, 2176:2304].astype(f32)).astype(bf16)
    kept[...] = total[0:32]
    rows_b[128:160, :] = jnp.zeros((32, 1024), bf16)
    rows_b[128:160, 0:128] = total[32:64]


def widen_kernel(mine_a, got_a, mine_b, got_b, small, rows_a, rows_b, kept):
    rows_a[0:128, :] = mine_a[...]
    rows_a[128:256, :] = got_a[...]
    rows_b[0:128, :] = mine_b[0:128, :]
    rows_b[128:256, :] = got_b[0:128, :]
    total = (small[...].astype(f32) + got_b[128:160, 0:128].astype(f32)).astype(bf16)
    kept[...] = total[0:16]
    rows_b[256:272, :] = jnp.zeros((16, 1024), bf16)
    rows_b[256:272, 0:128] = total[16:32]


def place_kernel(mine_a, got_a, mine_b, got_b, small, targets, grad_a, grad_b):
    for line, width, sources, target in (
        (3, 1024, (mine_a, got_a), grad_a),
        (4, 896, (mine_b, got_b), grad_b),
    ):
        total = None
        for source in sources:
            code = source[0:256, width : width + 128].astype(f32).astype(jnp.int32)
            chosen = hot(code[:, 0:1] * 16 + code[:, 1:2], targets[line : line + 1, 0:256])
            term = rows_dot(chosen, source[0:256, 0:width])
            total = term if total is None else total + term
        target[:, 0:width] = total.astype(bf16)
    total = (small[...].astype(f32) + got_b[256:272, 0:128].astype(f32)).astype(bf16)
    row = lax.broadcasted_iota(jnp.int32, (256, 16), 0)
    chunk = lax.broadcasted_iota(jnp.int32, (256, 16), 1)
    grad_b[:, 896:1024] = dot(hot(row, chunk * ROWS), total).astype(bf16)


def simple(kernel, outs, *args, flops=0):
    return call(
        kernel,
        outs,
        flops=flops,
        grid=(1,),
        in_specs=[whole(v) for v in args],
        out_specs=outs_whole(outs),
    )(*args)


def shard_tables():
    table = np.zeros((2, 8, SHARDS), np.int32)
    groups = np.zeros((2, 8, 16), np.int32)
    inside = (("x", "z"), ("z", "x"), ("x", "z"))
    for core in range(2):
        for number, order in enumerate(ORDERS):
            for place in range(SHARDS):
                here = core ^ (place >> 6)
                mask = (place >> 6) * CORE_BIT
                for step in range(6):
                    if (place >> step) & 1:
                        mask ^= STEP_BITS[order[step // 2]][(step % 2) ^ here]
                table[core, number, place] = mask
            for half in range(2):
                for place in range(16):
                    mask = 0
                    for step in range(4):
                        if (place >> step) & 1:
                            mask ^= STEP_BITS[inside[number][step // 2]][(step % 2) ^ core ^ half]
                    groups[core, 2 * number + half, place] = mask
    table[:, 3:5] = table[:, 1:3]
    lines = np.repeat(table, ROWS, axis=2)
    return lines, np.repeat(groups, ROWS, axis=2), table.transpose(0, 2, 1).copy()


def prepare_kernel(here, qkv, attn, expand, reduce, table, gain, shift, level, *refs):
    codes_line, lines, groups, shards = refs[:4]
    first, second, third, targets, offsets, shard_column, codes = refs[4:]
    for target in (first, second, third):
        target[...] = jnp.zeros(target.shape, bf16)
    first[0:15, 0:1440] = qkv[...]
    first[0:15, 1440:1536] = attn[:, 384:480]
    first[0:15, 1536:1920] = attn[:, 0:384]
    second[:, 0:1024] = table[:, 0:1024]
    second[0:15, 1024:2944] = expand[...]
    third[:, 0:896] = table[:, 1024:1920]
    third[0:15, 896:2816] = reduce[...]
    for number, ref in enumerate((gain, shift, level)):
        for row in range(2):
            start = (2 * number + row) * 15
            first[15:16, start : start + 15] = ref[row : row + 1, :]
    me, core = here[0], here[1]
    place = jnp.where(core == 0, lines[0], lines[1]) ^ me
    inside = lax.broadcasted_iota(jnp.int32, place.shape, 1) & 15
    targets[...] = place * 16 + inside
    place = jnp.where(core == 0, groups[0], groups[1]) ^ (me & 15)
    inside = lax.broadcasted_iota(jnp.int32, place.shape, 1) & 15
    offsets[...] = jnp.where(inside < 15, place * 15 + inside, -8192)
    shard_column[...] = jnp.where(core == 0, shards[0], shards[1]) ^ me
    row = jnp.right_shift(lax.broadcasted_iota(jnp.int32, (TOKENS, 64), 0), 2)
    column = lax.broadcasted_iota(jnp.int32, (TOKENS, 64), 1)
    spread = jnp.where(row == column, codes_line[...], 0)
    codes[...] = jnp.sum(spread, axis=1, keepdims=True)


def prepare(here, *args):
    i32 = jnp.int32
    args += tuple(jnp.asarray(t) for t in shard_tables())
    outs = (
        shape(16, 1920),
        shape(16, 2944),
        shape(16, 2816),
        shape(8, 2048, i32),
        shape(8, 256, i32),
        shape(SHARDS, 8, i32),
        shape(TOKENS, 1, i32),
    )
    return call(
        prepare_kernel,
        outs,
        vmem=60,
        grid=(1,),
        in_specs=[pl.BlockSpec(memory_space=pltpu.SMEM)] + [whole(v) for v in args],
        out_specs=outs_whole(outs),
    )(here, *args)


class Flow:
    def __init__(self, sources, buffers, targets, results, sem):
        count = len(sources)
        self.copies = [
            pltpu.make_async_copy(source, buffer, sem.at[i])
            for i, (source, buffer) in enumerate(zip(sources, buffers))
        ]
        self.buffers = buffers
        self.leaving = [
            pltpu.make_async_copy(result, target, sem.at[count + i])
            for i, (result, target) in enumerate(zip(results, targets))
        ]
        for copy in self.copies:
            copy.start()

    def __call__(self, *numbers):
        for number in numbers:
            self.copies[number].wait()
        return [self.buffers[number] for number in numbers]

    def out(self, *numbers):
        for number in numbers:
            self.leaving[number].start()

    def end(self):
        for copy in self.leaving:
            copy.wait()


def tail_lanes(value):
    source = lax.broadcasted_iota(jnp.int32, (480, 256), 0)
    target = lax.broadcasted_iota(jnp.int32, (480, 256), 1)
    return dot(value, hot(source, jnp.where(target >= 160, target + 224, -1))).astype(bf16)


def flowing(body, scalars, args, outs, extra, flops, cuts=None):
    anywhere = pl.BlockSpec(memory_space=pl.ANY)
    cuts = cuts or {}
    shapes = [
        (v.shape[0], cuts[i][1] - cuts[i][0]) if i in cuts else v.shape for i, v in enumerate(args)
    ]

    def kernel(*refs):
        first, sources, targets, buffers, results, (sem,), more = split_refs(
            refs, len(scalars), len(args), len(outs), len(args), len(outs), 1, len(extra)
        )
        sources = [
            ref.at[:, cuts[i][0] : cuts[i][1]] if i in cuts else ref for i, ref in enumerate(sources)
        ]
        flow = Flow(sources, buffers, targets, results, sem)
        body(flow, first, results, more)
        flow.end()

    return call(
        kernel,
        outs,
        vmem=60,
        flops=flops,
        in_specs=[pl.BlockSpec(memory_space=pltpu.SMEM)] * len(scalars) + [anywhere] * len(args),
        out_specs=(anywhere,) * len(outs),
        scratch_shapes=[pltpu.VMEM(dims, v.dtype) for dims, v in zip(shapes, args)]
        + [pltpu.VMEM(v.shape, v.dtype) for v in outs]
        + [pltpu.SemaphoreType.DMA((len(args) + len(outs),))]
        + extra,
    )(*scalars, *args)


def split_refs(refs, *counts):
    out, start = [], 0
    for count in counts:
        out.append(refs[start : start + count])
        start += count
    return out


def each_chunk(columns, body, width=CHUNK):
    for i in range(columns // width):
        body(slice(i * width, i * width + width))


def each_rows(body):
    @pl.loop(0, TOKENS // ROW_STEP)
    def _(i):
        body(pl.ds(pl.multiple_of(i * ROW_STEP, ROW_STEP), ROW_STEP))


SHIFT = 144
HOT = pltpu.VMEM((2, SHIFT + 384, 256), bf16)


def make_hot(offsets, order, chosen):
    for half in range(2):
        line = 2 * order + half
        feature = lax.broadcasted_iota(jnp.int32, (SHIFT + 384, 256), 0) - SHIFT
        chosen[half, :, :] = hot(feature, offsets[line : line + 1, :])


def group_window(here, half, group):
    core = here[1] ^ half
    number = jnp.right_shift(here[0], 4) ^ (2 * half)
    number = number ^ ((group & 1) * (4 + core)) ^ ((group >> 1) * (5 - core))
    first = number * 240
    start = jnp.minimum(jnp.right_shift(first, 7) * 128, D - 384)
    rows = pl.ds(pl.multiple_of(SHIFT + start - first, 16), 384)
    return pl.ds(pl.multiple_of(start, 128), 384), rows


def slot(group):
    return slice(group * 256, group * 256 + 256)


def shuffle(here, chosen, value, own, other):
    for half, target in enumerate((own, other)):
        for group in range(4):
            window, rows = group_window(here, half, group)
            target[:, slot(group)] = dot(value[:, window], chosen[half, rows, :]).astype(bf16)


def unshuffle(here, chosen, value, out):
    out[...] = jnp.zeros(out.shape, f32)
    for number in range(8):
        first = number * 240
        start = min(first // 128 * 128, D - 384)
        apart = jnp.right_shift(here[0], 4) ^ number
        half = jnp.right_shift(apart, 1) & 1
        core = here[1] ^ half
        low = apart & 1
        high = (jnp.right_shift(apart, 2) & 1) ^ low
        group = (high + 2 * low) * (1 - core) + (low + 2 * high) * core
        place = pl.ds(pl.multiple_of((4 * half + group) * 256, 256), 256)
        rows = slice(SHIFT + start - first, SHIFT + start - first + 384)
        out[:, start : start + 384] += cols_dot(value[:, place], chosen[half, rows, :])


def group_rows(order, pieces, half, group, span=slice(None)):
    rows = 64 if order == 1 else ROWS
    parts = []
    for number in range(256 // rows):
        piece, offset = piece_place(order, number)
        start = offset + group * rows
        start = start if isinstance(start, int) else pl.multiple_of(start, ROWS)
        parts.append(pieces[2 * half + piece][pl.ds(start, rows), span])
    return jnp.concatenate(parts, axis=0)


def group_sum(order, own, other, pieces, span):
    total = None
    for half, value in enumerate((own, other)):
        rows = [group_rows(order, pieces, half, group, span) for group in range(4)]
        term = dot(value[...], jnp.concatenate(rows, axis=0))
        total = term if total is None else total + term
    return total


def group_back(order, value, flow, first, wide):
    pieces = []
    for half in range(2):
        pieces += flow(first + 2 * half, first + 2 * half + 1)
        for group in range(4):
            term = cols_dot(value[...], group_rows(order, pieces, half, group))
            wide[:, slot(group + 4 * half)] = term.astype(bf16)
    return pieces


def pieces_of(own, other):
    return [ref[:, cut] for ref in (own, other) for cut in (slice(0, 512), slice(512, 1024))]


def row_move(transposed=False):
    row = lax.broadcasted_iota(jnp.int32, (TOKENS, TOKENS), 1 if transposed else 0)
    token = lax.broadcasted_iota(jnp.int32, (TOKENS, TOKENS), 0 if transposed else 1)
    moved = jnp.right_shift(row, 3) * 4 + (row & 3) + (jnp.right_shift(row, 2) & 1) * 128
    return hot(token, moved)


def moments(value):
    average = jnp.mean(value, axis=-1, keepdims=True)
    centered = value - average
    variance = jnp.mean(centered * centered, axis=-1, keepdims=True)
    return centered, lax.rsqrt(variance + epsilon)


def norm_back(value, grad, gain, base):
    centered, scale = moments(value)
    normed = centered * scale
    scaled = grad * gain
    inner = scaled - jnp.mean(scaled, axis=-1, keepdims=True)
    inner = inner - normed * jnp.mean(scaled * normed, axis=-1, keepdims=True)
    return base + scale * inner, grad * normed


def embed_body(flow, scalars, results, more):
    here, level = scalars
    stream, own, other, packed, vectors = results
    normed, chosen, looked = more
    codes, targets, offsets, shard_column, marks = flow(0, 1, 2, 3, 4)
    make_hot(offsets, 0, chosen)
    row = lax.broadcasted_iota(jnp.int32, (64, TOKENS), 0)
    token = lax.broadcasted_iota(jnp.int32, (64, TOKENS), 1)
    every = hot(row * RATIO, token)
    for line, first, start in ((3, 5, 0), (4, 9, 1024)):
        total = None
        for k in range(4):
            (table,) = flow(first + k)
            spread = hot(codes[...], targets[line : line + 1, 512 * k : 512 * k + 512])
            term = dot(dot(every, spread).astype(bf16), table[...])
            total = term if total is None else total + term
        looked[:, start : start + total.shape[1]] = total.astype(bf16)
    (hidden,) = flow(13)
    heads = flow(14, 15, 16, 17)
    chunk = lax.broadcasted_iota(jnp.int32, (SHARDS, 512), 0)
    row = lax.broadcasted_iota(jnp.int32, (SHARDS, 512), 1)
    lines = None
    for k in range(4):
        term = dot(hot(row + 512 * k, chunk * ROWS + 15), heads[k][...])
        lines = term if lines is None else lines + term
    spread = rows_dot(lines.astype(bf16), hot(shard_column[:, 0:1], marks[0:1, :]))
    within = lax.broadcasted_iota(jnp.int32, (SHARDS, 1), 0)
    group = sum((within >= 15 * r).astype(jnp.int32) for r in range(1, 7))
    spread = jnp.where(within - group * 15 == marks[1:2, :], spread, 0.0).astype(bf16)
    number = lax.broadcasted_iota(jnp.int32, (8, SHARDS), 1)
    first = lax.broadcasted_iota(jnp.int32, (8, SHARDS), 0) * 15
    inside = jnp.where((number >= first) & (number < first + 15), 1.0, 0.0).astype(bf16)
    vectors[...] = dot(inside, spread)
    flow.out(4)
    level_row = jnp.where(level[0] == 0, vectors[4:5, :], vectors[5:6, :])
    token = lax.broadcasted_iota(jnp.int32, (ROW_STEP, 64), 0)
    column = lax.broadcasted_iota(jnp.int32, (ROW_STEP, 64), 1)

    def rows(span):
        four = hot(jnp.right_shift(token + span.start, 2), column)
        value = dot(four, looked[...]) + hidden[span, :].astype(f32) + level_row
        stream[span, :] = value
        centered, scale = moments(value)
        normed[span, :] = (centered * scale * vectors[0:1, :] + vectors[2:3, :]).astype(bf16)

    each_rows(rows)
    flow.out(0)
    normed[...] = dot(row_move(), normed[...]).astype(bf16)
    shuffle(here, chosen, normed, own, other)
    flow.out(1, 2)
    weight = flow(18, 19, 20, 21)
    packed[...] = sum(dot(p, w[:, 0:1440]) for p, w in zip(pieces_of(own, other), weight)).astype(bf16)
    flow.out(3)


def embed(here, level, hidden, codes, targets, offsets, shard_column, marks, tables_a, tables_b, qkv):
    outs = (
        shape(TOKENS, D, f32),
        shape(TOKENS, HALF),
        shape(TOKENS, HALF),
        shape(TOKENS, 1440),
        shape(8, D, f32),
    )
    return flowing(
        embed_body,
        (here, level),
        (codes, targets, offsets, shard_column, marks, *tables_a, *tables_b, hidden, *qkv, *qkv),
        outs,
        [pltpu.VMEM((TOKENS, D), bf16), HOT, pltpu.VMEM((64, D), bf16)],
        8e9,
        {i: (0, 128) for i in (14, 15, 16, 17)},
    )


def probabilities(columns):
    query, key = columns[:, 0:480], columns[:, 480:960]
    row = lax.broadcasted_iota(jnp.int32, (TOKENS, TOKENS), 0)
    other = lax.broadcasted_iota(jnp.int32, (TOKENS, TOKENS), 1)
    mask = ((row & 3) == (other & 3)) & (jnp.right_shift(row, 2) >= jnp.right_shift(other, 2))
    scores = jnp.where(mask, cols_dot(query, key) * HEAD ** (-0.5), -1e30)
    top = jnp.max(scores, axis=-1, keepdims=True)
    total = top + jnp.log(jnp.sum(jnp.exp(scores - top), axis=-1, keepdims=True))
    return jnp.exp(scores - total)


def attend_kernel(columns, mixed):
    mixed[...] = dot(probabilities(columns).astype(bf16), columns[:, 960:1440]).astype(bf16)


def attend(columns):
    out = shape(TOKENS, 480)
    return call(
        attend_kernel, out, grid=(1,), in_specs=[whole(columns)], out_specs=whole(out)
    )(columns)


def attend_back_kernel(columns, d_mixed, d_packed):
    probs = probabilities(columns)
    low = probs.astype(bf16)
    d_probs = cols_dot(d_mixed[...], columns[:, 960:1440])
    d_scores = (probs * (d_probs - jnp.sum(probs * d_probs, axis=-1, keepdims=True))).astype(bf16)
    scale = HEAD ** (-0.5)
    d_packed[:, 0:480] = (dot(d_scores, columns[:, 480:960]) * scale).astype(bf16)
    d_packed[:, 480:960] = (rows_dot(d_scores, columns[:, 0:480]) * scale).astype(bf16)
    d_packed[:, 960:1440] = rows_dot(low, d_mixed[...]).astype(bf16)
    d_packed[:, 1440:1536] = jnp.zeros((TOKENS, 96), bf16)


def attend_back(columns, d_mixed):
    out = shape(TOKENS, 1536)
    return call(
        attend_back_kernel,
        out,
        grid=(1,),
        in_specs=[whole(columns), whole(d_mixed)],
        out_specs=whole(out),
    )(columns, d_mixed)


WORK = pltpu.VMEM((TOKENS, D), f32)
WIDE = pltpu.VMEM((TOKENS, 2 * HALF), bf16)
LOW = pltpu.VMEM((TOKENS, D), bf16)


def ahead_body(flow, scalars, results, more):
    (here,) = scalars
    (d_active,) = results
    wide, chosen = more
    upstream, offsets = flow(0, 1)
    make_hot(offsets, 2, chosen)
    group_back(2, upstream, flow, 2, wide)
    unshuffle(here, chosen, wide, d_active)
    flow.out(0)


def ahead(here, upstream, offsets, reduce):
    return flowing(
        ahead_body, (here,), (upstream, offsets, *reduce), (shape(TOKENS, D, f32),), [WIDE, HOT], 4e9
    )[0]


def middle_body(flow, scalars, results, more):
    (here,) = scalars
    mixed, mid, second_own, second_other, active_own, active_other = results[:6]
    d_upward, d_mid, attn_own, attn_other, d_mixed, sums = results[6:]
    work, wide, low, *chosen = more
    mixed_columns, offsets = flow(0, 1)
    for order in range(3):
        make_hot(offsets, order, chosen[order])
    mixed[:, 480:512] = jnp.zeros((TOKENS, 32), bf16)
    mixed[:, 0:480] = dot(row_move(True), mixed_columns[...]).astype(bf16)
    flow.out(0)
    end = tail_lanes(mixed[:, 0:480])
    rest, attn = flow(2, 3, 4, 5), flow(6, 7, 8, 9)
    for k in range(4):
        total = cols_dot(mixed[:, 0:384], attn[k][...]) + cols_dot(end, rest[k][...])
        wide[:, 512 * k : 512 * k + 512] = total.astype(bf16)
    unshuffle(here, chosen[0], wide, work)
    stream, vectors = flow(10, 11)

    def rows_first(span):
        value = stream[span, :] + work[span, :]
        mid[span, :] = value
        centered, scale = moments(value)
        low[span, :] = (centered * scale * vectors[1:2, :] + vectors[3:4, :]).astype(bf16)

    each_rows(rows_first)
    flow.out(1)
    shuffle(here, chosen[1], low, second_own, second_other)
    flow.out(2, 3)
    expand = flow(12, 13, 14, 15)

    def up(span):
        work[:, span] = group_sum(1, second_own, second_other, expand, span)

    each_chunk(D, up)
    (d_active,) = flow(16)

    def rows_active(span):
        value = work[span, :]
        root = np.float32(np.sqrt(2 / np.pi))
        square = value * value
        bend = jnp.tanh(value * (root + np.float32(root * 0.044715) * square))
        half = 0.5 * value
        low[span, :] = (half + half * bend).astype(bf16)
        inner = root + np.float32(3 * root * 0.044715) * square
        slope = 0.5 + 0.5 * bend + (half * inner) * (1.0 - bend * bend)
        d_upward[span, :] = (slope * d_active[span, :]).astype(bf16)

    each_rows(rows_active)
    flow.out(6)
    shuffle(here, chosen[2], low, active_own, active_other)
    flow.out(4, 5)
    for half in range(2):
        for group in range(4):
            term = cols_dot(d_upward[...], group_rows(1, expand, half, group))
            wide[:, slot(group + 4 * half)] = term.astype(bf16)
    unshuffle(here, chosen[1], wide, work)
    (upstream,) = flow(17)
    sums[...] = jnp.zeros(sums.shape, f32)

    def rows_back(span):
        base = upstream[span, :].astype(f32)
        grad = work[span, :]
        value, gain_part = norm_back(mid[span, :], grad, vectors[1:2, :], base)
        d_mid[span, :] = value
        low[span, :] = value.astype(bf16)
        sums[0:1, :] += jnp.sum(gain_part, axis=0, keepdims=True)
        sums[1:2, :] += jnp.sum(grad, axis=0, keepdims=True)

    each_rows(rows_back)
    flow.out(7, 11)
    shuffle(here, chosen[0], low, attn_own, attn_other)
    flow.out(8, 9)
    parts = pieces_of(attn_own, attn_other)
    back = sum(dot(p, w[...]) for p, w in zip(parts, attn)).astype(bf16)
    d_mixed[:, 0:384] = dot(row_move(), back).astype(bf16)
    back = sum(dot(p, w[...]) for p, w in zip(parts, rest)).astype(bf16)
    back = dot(row_move(), back).astype(bf16)
    source = lax.broadcasted_iota(jnp.int32, (256, 128), 0)
    target = lax.broadcasted_iota(jnp.int32, (256, 128), 1)
    d_mixed[:, 384:480] = dot(back, hot(source - 160, target))[:, 0:96].astype(bf16)
    flow.out(10)


def middle(here, mixed_columns, stream, vectors, offsets, d_active, upstream, qkv, attn, expand):
    half = shape(TOKENS, HALF)
    outs = (
        (shape(TOKENS, 512), shape(TOKENS, D, f32))
        + (half,) * 4
        + (shape(TOKENS, D), shape(TOKENS, D, f32), half, half, shape(TOKENS, 480), shape(8, D, f32))
    )
    return flowing(
        middle_body,
        (here,),
        (mixed_columns, offsets, *qkv, *attn, stream, vectors, *expand, d_active, upstream),
        outs,
        [WORK, WIDE, LOW, HOT, HOT, HOT],
        12e9,
        {i: (1280, 1536) for i in (2, 3, 4, 5)},
    )


def down_body(flow, scalars, results, more):
    (block_out,) = results
    active_own, active_other = flow(0, 1)
    reduce = flow(2, 3, 4, 5)
    (mid,) = flow(6)

    def down(span):
        total = group_sum(2, active_own, active_other, reduce, span)
        block_out[:, span] = (mid[:, span] + total).astype(bf16)

    each_chunk(D, down)
    flow.out(0)


def down(mid, active_own, active_other, reduce):
    return flowing(
        down_body, (), (active_own, active_other, *reduce, mid), (shape(TOKENS, D),), [], 4e9
    )[0]


def last_body(flow, scalars, results, more):
    here, level = scalars
    d_stream, sums_out, small = results
    work, wide, totals, chosen, low = more
    d_packed, offsets = flow(0, 1)
    make_hot(offsets, 0, chosen)
    moved = dot(row_move(True), d_packed[:, 0:1440]).astype(bf16)
    for k in range(4):
        (weight,) = flow(2 + k)
        wide[:, 512 * k : 512 * k + 512] = cols_dot(moved, weight[:, 0:1440]).astype(bf16)
    unshuffle(here, chosen, wide, work)
    totals[...] = jnp.zeros(totals.shape, f32)
    stream, d_mid, vectors, sums, shard_column, marks, codes = flow(6, 7, 8, 9, 10, 11, 12)

    def rows(span):
        grad = work[span, :]
        value, gain_part = norm_back(stream[span, :], grad, vectors[0:1, :], d_mid[span, :])
        d_stream[span, :] = value
        low[span, :] = value.astype(bf16)
        totals[0:1, :] += jnp.sum(gain_part, axis=0, keepdims=True)
        totals[2:3, :] += jnp.sum(grad, axis=0, keepdims=True)
        totals[6:7, :] += jnp.sum(value, axis=0, keepdims=True)

    each_rows(rows)
    flow.out(0)
    row = lax.broadcasted_iota(jnp.int32, (64, TOKENS), 0)
    token = lax.broadcasted_iota(jnp.int32, (64, TOKENS), 1)
    every = hot(row, jnp.right_shift(token, 2))
    sums_out[:, 0:1024] = dot(every, low[:, 0:1024]).astype(bf16)
    sums_out[:, 1152:2048] = dot(every, low[:, 1024:1920]).astype(bf16)
    lane = lax.broadcasted_iota(jnp.int32, (TOKENS, 128), 1)
    code = codes[...]
    code = jnp.where(lane == 0, jnp.right_shift(code, 4), jnp.where(lane == 1, code & 15, 0))
    code = dot(hot(row * RATIO, token), code.astype(f32).astype(bf16)).astype(bf16)
    sums_out[:, 1024:1152] = code
    sums_out[:, 2048:2176] = code
    totals[1:2, :] = sums[0:1, :]
    totals[3:4, :] = sums[1:2, :]
    totals[4:5, :] = jnp.where(level[0] == 0, totals[6:7, :], 0.0)
    totals[5:6, :] = jnp.where(level[0] == 1, totals[6:7, :], 0.0)
    number = lax.broadcasted_iota(jnp.int32, (SHARDS, 8), 0)
    first = lax.broadcasted_iota(jnp.int32, (SHARDS, 8), 1) * 15
    inside = jnp.where((number >= first) & (number < first + 15) & (number < 90), 1.0, 0.0)
    repeated = dot(inside.astype(bf16), totals[...].astype(bf16))
    within = lax.broadcasted_iota(jnp.int32, (SHARDS, 1), 0)
    group = sum((within >= 15 * r).astype(jnp.int32) for r in range(1, 7))
    repeated = jnp.where(within - group * 15 == marks[1:2, :], repeated, 0.0).astype(bf16)
    spread = cols_dot(hot(shard_column[:, 2:3], marks[0:1, :]), repeated).astype(bf16)
    small[...] = spread[0:64]
    sums_out[:, 2176:2304] = spread[64:128]
    flow.out(1, 2)


def last(here, level, d_packed, stream, d_mid, vectors, sums, offsets, shard_column, marks, codes, qkv):
    outs = (shape(TOKENS, D, f32), shape(64, 2304), shape(64, 128))
    return flowing(
        last_body,
        (here, level),
        (d_packed, offsets, *qkv, stream, d_mid, vectors, sums, shard_column, marks, codes),
        outs,
        [WORK, WIDE, pltpu.VMEM((8, D), f32), HOT, LOW],
        60e9,
    )


def finish_kernel(kept0, got0, kept1, got1, kept2, got2, *outs):
    grad_qkv, grad_attn, grad_expand, grad_reduce, table, levels, gains, shifts = outs

    def total(kept, got, start, stop):
        return kept[:, start:stop].astype(f32) + got[:, start:stop].astype(f32)

    grad_attn[...] = total(kept0, got0, 0, 480)[:15]
    grad_qkv[...] = total(kept0, got0, 512, 1952)[:15]
    grad_expand[...] = total(kept1, got1, 0, 1920)[:15]
    table[:, 0:1024] = total(kept1, got1, 1920, 2944)
    grad_reduce[...] = total(kept2, got2, 0, 1920)[:15]
    table[:, 1024:1920] = total(kept2, got2, 1920, 2816)
    line = total(kept2, got2, 2816, 2944)[0:1]
    for target, first in ((gains, 0), (shifts, 2), (levels, 4)):
        for row in range(2):
            start = (first + row) * 15
            target[row : row + 1, :] = line[:, start : start + 15]


def finish(*pairs):
    outs = tuple(
        shape(*s, f32)
        for s in ((15, 1440), (15, 480), (15, D), (15, D), (16, D), (2, 15), (2, 15), (2, 15))
    )
    return call(
        finish_kernel,
        outs,
        grid=(1,),
        in_specs=[whole(v) for v in pairs],
        out_specs=outs_whole(outs),
    )(*pairs)


def body(
    hidden_in,
    cond_codes,
    level_ids,
    qkv_weight,
    attn_out_weight,
    mlp_in_weight,
    mlp_out_weight,
    code_table,
    level_table,
    norm_gain,
    norm_bias,
    grad_out,
):
    yl, co, yh, z, x = (lax.axis_index(name) for name in AXES)
    me = yl * 64 + co * 32 + yh * 16 + z * 4 + x
    here = jnp.stack((me, co))
    *shards, targets, offsets, shard_column, codes = prepare(
        here,
        qkv_weight,
        attn_out_weight.T,
        mlp_in_weight,
        mlp_out_weight,
        code_table,
        norm_gain,
        norm_bias,
        level_table,
        cond_codes,
    )
    feature = np.arange(D, dtype=np.int32)
    marks = jnp.asarray(np.stack((feature // 15, feature % 15)))

    def exchanged(values, step):
        return [exchange(v, order, step) for v, order in zip(values, ORDERS)]

    def singles(lists):
        return [v for (v,) in lists]

    small = singles(join(shards, exchanged(shards, 0)))
    for step in (1, 2):
        small = singles(join(small, exchanged(small, step)))
    cuts = [((0, split), (split, v.shape[1])) for v, split in zip(small, SPLITS)]
    small = join(small, exchanged(small, 3), cuts)
    first, second = [v for v, _ in small], [v for _, v in small]
    first = singles(join(first, exchanged(first, 4)))
    first, second = lax.optimization_barrier((first, second))
    rests = exchanged(first, 5)
    second_got = exchanged(second, 4)
    pieces = [(h, r, swap_cores(h), swap_cores(r)) for h, r in zip(first, rests)]
    second = singles(join(second, second_got))
    pieces, second = lax.optimization_barrier((pieces, second))
    qkv, table_a, table_b = pieces
    rests = exchanged(second, 5)

    stream, first_own, first_other, packed, vectors = embed(
        here, level_ids, hidden_in[0], codes, targets, offsets, shard_column, marks, table_a, table_b, qkv
    )

    def over_blocks(value):
        return lax.all_to_all(value, BLK, split_axis=0, concat_axis=0, tiled=True)

    columns = over_blocks(packed)
    mixed = attend(columns)
    mixed, rests = lax.optimization_barrier((mixed, rests))
    mixed = over_blocks(mixed)
    attn, expand, reduce = [(h, r, swap_cores(h), swap_cores(r)) for h, r in zip(second, rests)]
    upstream = grad_out[0]
    upstream_got = swap_cores(upstream)
    d_active = ahead(here, upstream, offsets, reduce)
    mixed, d_active = lax.optimization_barrier((mixed, d_active))
    (
        mixed,
        mid,
        second_own,
        second_other,
        active_own,
        active_other,
        d_upward,
        d_mid,
        attn_own,
        attn_other,
        d_mixed,
        sums,
    ) = middle(here, mixed, stream, vectors, offsets, d_active, upstream, qkv, attn, expand)
    swapped = [swap_cores(v) for v in (active_other, second_other, d_upward, attn_other, mixed)]
    d_mixed = over_blocks(d_mixed)
    block_out = down(mid, active_own, active_other, reduce)
    d_mixed, block_out = lax.optimization_barrier((d_mixed, block_out))
    d_packed = attend_back(columns, d_mixed)
    d_packed, active_own, second_own, swapped = lax.optimization_barrier(
        (d_packed, active_own, second_own, swapped)
    )
    active_got, second_got, d_upward_got, attn_got, mixed_got = swapped
    d_packed = over_blocks(d_packed)
    reduce_grad = outer(2, active_own, active_got, upstream, upstream_got)
    reduce_got = exchange(reduce_grad[1], ORDERS[2], 5)
    expand_grad = outer(1, second_own, second_got, d_upward, d_upward_got)
    expand_got = exchange(expand_grad[1], ORDERS[1], 5)
    d_packed, reduce_grad, expand_grad = lax.optimization_barrier((d_packed, reduce_grad, expand_grad))
    first_got = swap_cores(first_other)

    qkv_grad = outer_pair(
        (attn_own, attn_got, mixed, mixed_got),
        (first_own, first_got, d_packed, swap_cores(d_packed)),
    )
    qkv_got = exchange(qkv_grad[1], ORDERS[0], 5)
    d_packed, qkv_grad = lax.optimization_barrier((d_packed, qkv_grad))

    d_stream, code_sums, small = last(
        here, level_ids, d_packed, stream, d_mid, vectors, sums, offsets, shard_column, marks, codes, qkv
    )
    outs = (shape(128, 1152), shape(160, 1024), shape(32, 128))
    rows_a, rows_b, small = simple(spread_kernel, outs, code_sums, swap_cores(code_sums), small)
    got_a, got_b = exchange(rows_a, ORDERS[1], 5), exchange(rows_b, ORDERS[2], 5)
    early = add_halves([[(expand_grad[0], expand_got)], [(reduce_grad[0], reduce_got)]])
    early_got = [exchange(sent, order, 4) for (_, sent), order in zip(early, ORDERS[1:])]
    got_a, got_b, early = lax.optimization_barrier((got_a, got_b, early))
    qkv_got, _ = lax.optimization_barrier((qkv_got, (got_a, got_b)))
    (first_sums,) = add_halves([[(qkv_grad[0], qkv_got)]])
    first_got = exchange(first_sums[1], ORDERS[0], 4)
    outs = (shape(256, 1152), shape(272, 1024), shape(16, 128))
    rows_a, rows_b, small = simple(widen_kernel, outs, rows_a, got_a, rows_b, got_b, small)
    got_a, got_b = exchange(rows_a, ORDERS[1], 4), exchange(rows_b, ORDERS[2], 4)
    outs = (shape(256, 1024), shape(256, 1024))
    grad_a, grad_b = simple(
        place_kernel, outs, rows_a, got_a, rows_b, got_b, small, targets, flops=1e9
    )
    sums = add_halves(
        [
            [(first_sums[0], first_got)],
            [(early[0][0], early_got[0]), (grad_a, None)],
            [(early[1][0], early_got[1]), (grad_b, None)],
        ]
    )
    for step in (3, 2, 1):
        got = exchanged([sent for _, sent in sums], step)
        sums = add_halves([[(kept, v)] for (kept, _), v in zip(sums, got)])
    got = exchanged([sent for _, sent in sums], 0)
    pairs = [v for (kept, _), mine in zip(sums, got) for v in (kept, mine)]
    grad_qkv, grad_attn, grad_expand, grad_reduce, grad_table, levels, gains, shifts = finish(*pairs)
    return (
        block_out[None],
        d_stream[None],
        grad_qkv,
        grad_attn.T,
        grad_expand,
        grad_reduce,
        grad_table,
        levels,
        gains,
        shifts,
    )


def solution(mesh):
    fine = Mesh(mesh.devices.reshape(2, 2, 2, 4, 4), AXES)
    return jax.shard_map(
        body,
        mesh=fine,
        in_specs=(
            P(WIN, BLK, None),
            P(WIN, BLK),
            P(WIN),
            P(AXES, None),
            P(None, AXES),
            P(AXES, None),
            P(AXES, None),
            P(AXES, None),
            P(None, AXES),
            P(None, AXES),
            P(None, AXES),
            P(WIN, BLK, None),
        ),
        out_specs=(
            P(WIN, BLK, None),
            P(WIN, BLK, None),
            P(AXES, None),
            P(None, AXES),
            P(AXES, None),
            P(AXES, None),
            P(AXES, None),
            P(None, AXES),
            P(None, AXES),
            P(None, AXES),
        ),
        check_vma=False,
    )
```

```python
import functools

import jax
import jax.numpy as jnp
import numpy as np
from jax import lax
from jax.experimental import pallas as pl
from jax.experimental.pallas import tpu as pltpu
from jax.sharding import Mesh, PartitionSpec as P

HEAD = 480
BLOCK = 128
RATIO = 4
D = 1920
SHARDS = 128
ROWS = 16
HALF = 1024
HALVES = (slice(0, HALF), slice(HALF, 2 * HALF))
SPLITS = (1536, 1024, 896)
TOKENS = 256
CHUNK = 640
MIB = 2**20
ROW_STEP = 128
epsilon = 1e-05
bf16 = jnp.bfloat16
f32 = jnp.float32
AXES = ("yl", "co", "yh", "z", "x")
WIN = ("yl", "co")
BLK = ("yh", "z", "x")
STEP_BITS = {"x": (1, 3), "z": (4, 12), "y": (64, 80)}
CORE_BIT = 32
ORDERS = (("x", "z", "y"), ("z", "y", "x"), ("y", "x", "z"))


def exchange(value, order, step):
    masks = STEP_BITS[order[step // 2]]
    pairs = [(i, i ^ masks[(step % 2) ^ ((i >> 5) & 1)]) for i in range(SHARDS)]
    return lax.ppermute(value, AXES, pairs)


def swap_cores(value):
    return lax.ppermute(value, AXES, [(i, i ^ CORE_BIT) for i in range(SHARDS)])


def call(kernel, out_shape, vmem=16, flops=0, **options):
    params = pltpu.CompilerParams(vmem_limit_bytes=vmem * MIB)

    def run(*args):
        outs = out_shape if isinstance(out_shape, tuple) else (out_shape,)
        size = sum(v.size * v.dtype.itemsize for v in args + outs)
        cost = pl.CostEstimate(flops=int(flops), bytes_accessed=size, transcendentals=0)
        return pl.pallas_call(
            kernel, out_shape=out_shape, compiler_params=params, cost_estimate=cost, **options
        )(*args)

    return run


def whole(v):
    return pl.BlockSpec(
        v.shape, lambda i: (0,) * len(v.shape), pipeline_mode=pl.Buffered(buffer_count=1)
    )


def outs_whole(shapes):
    return tuple(pl.BlockSpec(v.shape, lambda i: (0, 0)) for v in shapes)


def shape(rows, columns, dtype=bf16):
    return jax.ShapeDtypeStruct((rows, columns), dtype)


def dot(left, right):
    return jnp.dot(left, right, preferred_element_type=f32)


def rows_dot(left, right):
    return lax.dot_general(left, right, (((0,), (0,)), ((), ())), preferred_element_type=f32)


def cols_dot(left, right):
    return lax.dot_general(left, right, (((1,), (1,)), ((), ())), preferred_element_type=f32)


def hot(left, right):
    return jnp.where(left == right, 1.0, 0.0).astype(bf16)


def join_kernel(tiles, cuts, *refs):
    count = len(cuts)
    sources, targets = refs[: 2 * count], list(refs[2 * count :])
    step = pl.program_id(0)
    for i, spans in enumerate(cuts):
        mine, targets = targets[: len(spans)], targets[len(spans) :]
        for source, here in ((sources[2 * i], step < tiles), (sources[2 * i + 1], step >= tiles)):

            @pl.when(here)
            def _(source=source, mine=mine, spans=spans):
                for target, (start, stop) in zip(mine, spans):
                    target[...] = source[:, start:stop]


def join(firsts, seconds, cuts=None):
    rows = firsts[0].shape[0]
    cuts = cuts or [((0, v.shape[1]),) for v in firsts]
    tiles = max(rows // 128, 1)
    tile = rows // tiles
    specs, args = [], []
    for first, second in zip(firsts, seconds):
        columns = first.shape[1]
        specs += [
            pl.BlockSpec((tile, columns), lambda i: (jnp.minimum(i, tiles - 1), 0)),
            pl.BlockSpec((tile, columns), lambda i: (jnp.maximum(i - tiles, 0), 0)),
        ]
        args += [first, second]
    widths = [stop - start for spans in cuts for start, stop in spans]
    out = call(
        functools.partial(join_kernel, tiles, cuts),
        tuple(shape(2 * rows, width) for width in widths),
        grid=(2 * tiles,),
        in_specs=specs,
        out_specs=tuple(pl.BlockSpec((tile, width), lambda i: (i, 0)) for width in widths),
    )(*args)
    out = list(out)
    return [[out.pop(0) for _ in spans] for spans in cuts]


def add_kernel(groups, *refs):
    count = sum(4 if added else 2 for group in groups for added in group)
    sources, targets = refs[:count], refs[count:]
    for i, group in enumerate(groups):
        start = 0
        for added in group:
            mine, sources = sources[: 4 if added else 2], sources[4 if added else 2 :]
            span = slice(start, start + mine[0].shape[1])
            for half in range(2):
                value = mine[half][...]
                if added:
                    value = (value.astype(f32) + mine[half + 2][...].astype(f32)).astype(bf16)
                targets[2 * i + half][:, span] = value
            start = span.stop


def add_halves(groups):
    rows = groups[0][0][0].shape[0] // 2
    tiles = max(rows // 128, 1)
    tile = rows // tiles
    specs, args, widths = [], [], []
    for group in groups:
        for kept, got in group:
            columns = kept.shape[1]
            low = pl.BlockSpec((tile, columns), lambda i: (i, 0))
            high = pl.BlockSpec((tile, columns), lambda i: (i + tiles, 0))
            specs += [low, high] * (1 if got is None else 2)
            args += [kept, kept] + ([] if got is None else [got, got])
        widths.append(sum(kept.shape[1] for kept, _ in group))
    out = call(
        functools.partial(add_kernel, [[got is not None for _, got in group] for group in groups]),
        tuple(shape(rows, width) for width in widths for _ in range(2)),
        grid=(tiles,),
        in_specs=specs,
        out_specs=tuple(pl.BlockSpec((tile, width), lambda i: (i, 0)) for width in widths for _ in range(2)),
    )(*args)
    return [(out[2 * i], out[2 * i + 1]) for i in range(len(groups))]


def store_group(order, group, kept, sent, total):
    if order == 0:
        start = 256 * (group & 1)
        (kept, sent)[group >> 1][start : start + 256, :] = total
    for number in range(4 if order == 1 else 16 if order == 2 else 0):
        rows = 64 if order == 1 else ROWS
        half, offset = piece_place(order, number)
        start = offset + group * rows
        (kept, sent)[half][start : start + rows, :] = total[number * rows : number * rows + rows]


def piece_place(order, number):
    if order == 1:
        return number >> 1, 256 * (number & 1)
    return number >> 3, 256 * ((number >> 2) & 1) + 64 * (number & 3)


def outer_kernel(order, left, left_got, right, right_got, kept, sent, turned):
    @pl.when(pl.program_id(0) == 0)
    def _():
        turned[:, 0:256] = left[...].T
        turned[:, 256:512] = left_got[...].T

    for group in range(4):
        rows = slice(256 * group, 256 * group + 256)
        total = dot(turned[rows, 0:256], right[...]) + dot(turned[rows, 256:512], right_got[...])
        store_group(order, group, kept, sent, total.astype(bf16))


def outer(order, left, left_got, right, right_got):
    columns = right.shape[1]
    width = 640 if columns % 640 == 0 else 512
    outs = (shape(HALF // 2, columns), shape(HALF // 2, columns))
    tile = pl.BlockSpec((TOKENS, width), lambda i: (0, i))
    out = pl.BlockSpec((HALF // 2, width), lambda i: (0, i))
    return call(
        functools.partial(outer_kernel, order),
        outs,
        vmem=60 if order else 16,
        flops=2 * 512 * HALF * columns,
        grid=(columns // width,),
        in_specs=[whole(left), whole(left_got), tile, tile],
        out_specs=(out, out),
        scratch_shapes=[pltpu.VMEM((HALF, 512), bf16)],
    )(left, left_got, right, right_got)


def pair_kernel(one, one_got, two, two_got, right, right_got, other, other_got, kept, sent, turned):
    def run(left, left_got, right, right_got):
        turned[:, 0:256] = left[...].T
        turned[:, 256:512] = left_got[...].T
        for cut in range(0, right.shape[1], 512):
            span = slice(cut, cut + 512)
            for half, target in enumerate((kept, sent)):
                rows = slice(512 * half, 512 * half + 512)
                total = dot(turned[rows, 0:256], right[:, span])
                total = total + dot(turned[rows, 256:512], right_got[:, span])
                target[:, span] = total.astype(bf16)

    @pl.when(pl.program_id(0) == 0)
    def _():
        run(one, one_got, other, other_got)

    @pl.when(pl.program_id(0) > 0)
    def _():
        run(two, two_got, right, right_got)


def outer_pair(first, second):
    one, one_got, other, other_got = first
    two, two_got, right, right_got = second
    outs = (shape(HALF // 2, 2048), shape(HALF // 2, 2048))
    tile = pl.BlockSpec((TOKENS, 512), lambda i: (0, jnp.maximum(i - 1, 0)))
    out = pl.BlockSpec((HALF // 2, 512), lambda i: (0, i))
    return call(
        pair_kernel,
        outs,
        vmem=60,
        flops=2 * 512 * HALF * 2048,
        grid=(4,),
        in_specs=[whole(v) for v in (one, one_got, two, two_got)]
        + [tile, tile, whole(other), whole(other_got)],
        out_specs=(out, out),
        scratch_shapes=[pltpu.VMEM((HALF, 512), bf16)],
    )(one, one_got, two, two_got, right, right_got, other, other_got)


def spread_kernel(mine, got, small, rows_a, rows_b, kept):
    for i, source in enumerate((mine, got)):
        rows_a[64 * i : 64 * i + 64, :] = source[:, 0:1152]
        rows_b[64 * i : 64 * i + 64, :] = source[:, 1152:2176]
    total = (small[...].astype(f32) + got[:, 2176:2304].astype(f32)).astype(bf16)
    kept[...] = total[0:32]
    rows_b[128:160, :] = jnp.zeros((32, 1024), bf16)
    rows_b[128:160, 0:128] = total[32:64]


def widen_kernel(mine_a, got_a, mine_b, got_b, small, rows_a, rows_b, kept):
    rows_a[0:128, :] = mine_a[...]
    rows_a[128:256, :] = got_a[...]
    rows_b[0:128, :] = mine_b[0:128, :]
    rows_b[128:256, :] = got_b[0:128, :]
    total = (small[...].astype(f32) + got_b[128:160, 0:128].astype(f32)).astype(bf16)
    kept[...] = total[0:16]
    rows_b[256:272, :] = jnp.zeros((16, 1024), bf16)
    rows_b[256:272, 0:128] = total[16:32]


def place_kernel(mine_a, got_a, mine_b, got_b, small, targets, grad_a, grad_b):
    for line, width, sources, target in (
        (3, 1024, (mine_a, got_a), grad_a),
        (4, 896, (mine_b, got_b), grad_b),
    ):
        total = None
        for source in sources:
            code = source[0:256, width : width + 128].astype(f32).astype(jnp.int32)
            chosen = hot(code[:, 0:1] * 16 + code[:, 1:2], targets[line : line + 1, 0:256])
            term = rows_dot(chosen, source[0:256, 0:width])
            total = term if total is None else total + term
        target[:, 0:width] = total.astype(bf16)
    total = (small[...].astype(f32) + got_b[256:272, 0:128].astype(f32)).astype(bf16)
    row = lax.broadcasted_iota(jnp.int32, (256, 16), 0)
    chunk = lax.broadcasted_iota(jnp.int32, (256, 16), 1)
    grad_b[:, 896:1024] = dot(hot(row, chunk * ROWS), total).astype(bf16)


def simple(kernel, outs, *args, flops=0):
    return call(
        kernel,
        outs,
        flops=flops,
        grid=(1,),
        in_specs=[whole(v) for v in args],
        out_specs=outs_whole(outs),
    )(*args)


def shard_tables():
    table = np.zeros((2, 8, SHARDS), np.int32)
    groups = np.zeros((2, 8, 16), np.int32)
    inside = (("x", "z"), ("z", "x"), ("x", "z"))
    for core in range(2):
        for number, order in enumerate(ORDERS):
            for place in range(SHARDS):
                here = core ^ (place >> 6)
                mask = (place >> 6) * CORE_BIT
                for step in range(6):
                    if (place >> step) & 1:
                        mask ^= STEP_BITS[order[step // 2]][(step % 2) ^ here]
                table[core, number, place] = mask
            for half in range(2):
                for place in range(16):
                    mask = 0
                    for step in range(4):
                        if (place >> step) & 1:
                            mask ^= STEP_BITS[inside[number][step // 2]][(step % 2) ^ core ^ half]
                    groups[core, 2 * number + half, place] = mask
    table[:, 3:5] = table[:, 1:3]
    lines = np.repeat(table, ROWS, axis=2)
    return lines, np.repeat(groups, ROWS, axis=2), table.transpose(0, 2, 1).copy()


def prepare_kernel(qkv, attn, expand, reduce, table, gain, shift, level, *refs):
    codes_line, lines, groups, shards = refs[:4]
    first, second, third, targets, offsets, shard_column, codes = refs[4:]
    for target in (first, second, third):
        target[...] = jnp.zeros(target.shape, bf16)
    first[0:15, 0:1440] = qkv[...]
    first[0:15, 1440:1536] = attn[:, 384:480]
    first[0:15, 1536:1920] = attn[:, 0:384]
    second[:, 0:1024] = table[:, 0:1024]
    second[0:15, 1024:2944] = expand[...]
    third[:, 0:896] = table[:, 1024:1920]
    third[0:15, 896:2816] = reduce[...]
    for number, ref in enumerate((gain, shift, level)):
        for row in range(2):
            start = (2 * number + row) * 15
            first[15:16, start : start + 15] = ref[row : row + 1, :]
    yl, core, yh, z, x = (lax.axis_index(name) for name in AXES)
    me = yl * 64 + core * 32 + yh * 16 + z * 4 + x
    place = jnp.where(core == 0, lines[0], lines[1]) ^ me
    inside = lax.broadcasted_iota(jnp.int32, place.shape, 1) & 15
    targets[...] = place * 16 + inside
    place = jnp.where(core == 0, groups[0], groups[1]) ^ (me & 15)
    inside = lax.broadcasted_iota(jnp.int32, place.shape, 1) & 15
    offsets[...] = jnp.where(inside < 15, place * 15 + inside, -8192)
    shard_column[...] = jnp.where(core == 0, shards[0], shards[1]) ^ me
    row = lax.broadcasted_iota(jnp.int32, (64, 64), 0)
    column = lax.broadcasted_iota(jnp.int32, (64, 64), 1)
    spread = jnp.where(row == column, codes_line[...], 0)
    codes[...] = jnp.sum(spread, axis=1, keepdims=True)


def prepare(*args):
    i32 = jnp.int32
    args += tuple(jnp.asarray(t) for t in shard_tables())
    outs = (
        shape(16, 1920),
        shape(16, 2944),
        shape(16, 2816),
        shape(8, 2048, i32),
        shape(8, 256, i32),
        shape(SHARDS, 8, i32),
        shape(64, 1, i32),
    )
    return call(
        prepare_kernel,
        outs,
        vmem=60,
        grid=(1,),
        in_specs=[whole(v) for v in args],
        out_specs=outs_whole(outs),
    )(*args)


class Flow:
    def __init__(self, sources, buffers, targets, results, sem):
        count = len(sources)
        self.copies = [
            pltpu.make_async_copy(source, buffer, sem.at[i])
            for i, (source, buffer) in enumerate(zip(sources, buffers))
        ]
        self.buffers = buffers
        self.leaving = [
            pltpu.make_async_copy(result, target, sem.at[count + i])
            for i, (result, target) in enumerate(zip(results, targets))
        ]
        for copy in self.copies:
            copy.start()

    def __call__(self, *numbers):
        for number in numbers:
            self.copies[number].wait()
        return [self.buffers[number] for number in numbers]

    def out(self, *numbers):
        for number in numbers:
            self.leaving[number].start()

    def end(self):
        for copy in self.leaving:
            copy.wait()


def tail_lanes(value):
    source = lax.broadcasted_iota(jnp.int32, (480, 256), 0)
    target = lax.broadcasted_iota(jnp.int32, (480, 256), 1)
    return dot(value, hot(source, jnp.where(target >= 160, target + 224, -1))).astype(bf16)


def flowing(body, scalars, args, outs, extra, flops, cuts=None):
    anywhere = pl.BlockSpec(memory_space=pl.ANY)
    cuts = cuts or {}
    shapes = [
        (v.shape[0], cuts[i][1] - cuts[i][0]) if i in cuts else v.shape for i, v in enumerate(args)
    ]

    def kernel(*refs):
        first, sources, targets, buffers, results, (sem,), more = split_refs(
            refs, len(scalars), len(args), len(outs), len(args), len(outs), 1, len(extra)
        )
        sources = [
            ref.at[:, cuts[i][0] : cuts[i][1]] if i in cuts else ref for i, ref in enumerate(sources)
        ]
        flow = Flow(sources, buffers, targets, results, sem)
        body(flow, first, results, more)
        flow.end()

    return call(
        kernel,
        outs,
        vmem=60,
        flops=flops,
        in_specs=[pl.BlockSpec(memory_space=pltpu.SMEM)] * len(scalars) + [anywhere] * len(args),
        out_specs=(anywhere,) * len(outs),
        scratch_shapes=[pltpu.VMEM(dims, v.dtype) for dims, v in zip(shapes, args)]
        + [pltpu.VMEM(v.shape, v.dtype) for v in outs]
        + [pltpu.SemaphoreType.DMA((len(args) + len(outs),))]
        + extra,
    )(*scalars, *args)


def split_refs(refs, *counts):
    out, start = [], 0
    for count in counts:
        out.append(refs[start : start + count])
        start += count
    return out


def each_chunk(columns, body, width=CHUNK):
    for i in range(columns // width):
        body(slice(i * width, i * width + width))


def each_rows(body):
    @pl.loop(0, TOKENS // ROW_STEP)
    def _(i):
        body(pl.ds(pl.multiple_of(i * ROW_STEP, ROW_STEP), ROW_STEP))


SHIFT = 144
HOT = pltpu.VMEM((2, SHIFT + 384, 256), bf16)


def make_hot(offsets, order, chosen):
    for half in range(2):
        line = 2 * order + half
        feature = lax.broadcasted_iota(jnp.int32, (SHIFT + 384, 256), 0) - SHIFT
        chosen[half, :, :] = hot(feature, offsets[line : line + 1, :])


def group_window(here, half, group):
    core = here[1] ^ half
    number = jnp.right_shift(here[0], 4) ^ (2 * half)
    number = number ^ ((group & 1) * (4 + core)) ^ ((group >> 1) * (5 - core))
    first = number * 240
    start = jnp.minimum(jnp.right_shift(first, 7) * 128, D - 384)
    rows = pl.ds(pl.multiple_of(SHIFT + start - first, 16), 384)
    return pl.ds(pl.multiple_of(start, 128), 384), rows


def slot(group):
    return slice(group * 256, group * 256 + 256)


def shuffle(here, chosen, value, own, other):
    for half, target in enumerate((own, other)):
        for group in range(4):
            window, rows = group_window(here, half, group)
            target[:, slot(group)] = dot(value[:, window], chosen[half, rows, :]).astype(bf16)


def unshuffle(here, chosen, value, out):
    out[...] = jnp.zeros(out.shape, f32)
    for number in range(8):
        first = number * 240
        start = min(first // 128 * 128, D - 384)
        apart = jnp.right_shift(here[0], 4) ^ number
        half = jnp.right_shift(apart, 1) & 1
        core = here[1] ^ half
        low = apart & 1
        high = (jnp.right_shift(apart, 2) & 1) ^ low
        group = (high + 2 * low) * (1 - core) + (low + 2 * high) * core
        place = pl.ds(pl.multiple_of((4 * half + group) * 256, 256), 256)
        rows = slice(SHIFT + start - first, SHIFT + start - first + 384)
        out[:, start : start + 384] += cols_dot(value[:, place], chosen[half, rows, :])


def group_rows(order, pieces, half, group, span=slice(None)):
    rows = 64 if order == 1 else ROWS
    parts = []
    for number in range(256 // rows):
        piece, offset = piece_place(order, number)
        start = offset + group * rows
        start = start if isinstance(start, int) else pl.multiple_of(start, ROWS)
        parts.append(pieces[2 * half + piece][pl.ds(start, rows), span])
    return jnp.concatenate(parts, axis=0)


def group_sum(order, own, other, pieces, span):
    total = None
    for half, value in enumerate((own, other)):
        rows = [group_rows(order, pieces, half, group, span) for group in range(4)]
        term = dot(value[...], jnp.concatenate(rows, axis=0))
        total = term if total is None else total + term
    return total


def group_back(order, value, flow, first, wide):
    pieces = []
    for half in range(2):
        pieces += flow(first + 2 * half, first + 2 * half + 1)
        for group in range(4):
            term = cols_dot(value[...], group_rows(order, pieces, half, group))
            wide[:, slot(group + 4 * half)] = term.astype(bf16)
    return pieces


def pieces_of(own, other):
    return [ref[:, cut] for ref in (own, other) for cut in (slice(0, 512), slice(512, 1024))]


def row_move(transposed=False):
    row = lax.broadcasted_iota(jnp.int32, (TOKENS, TOKENS), 1 if transposed else 0)
    token = lax.broadcasted_iota(jnp.int32, (TOKENS, TOKENS), 0 if transposed else 1)
    moved = jnp.right_shift(row, 3) * 4 + (row & 3) + (jnp.right_shift(row, 2) & 1) * 128
    return hot(token, moved)


def moments(value):
    average = jnp.mean(value, axis=-1, keepdims=True)
    centered = value - average
    variance = jnp.mean(centered * centered, axis=-1, keepdims=True)
    return centered, lax.rsqrt(variance + epsilon)


def norm_back(value, grad, gain, base):
    centered, scale = moments(value)
    normed = centered * scale
    scaled = grad * gain
    inner = scaled - jnp.mean(scaled, axis=-1, keepdims=True)
    inner = inner - normed * jnp.mean(scaled * normed, axis=-1, keepdims=True)
    return base + scale * inner, grad * normed


def embed_body(flow, scalars, results, more):
    here, level = scalars
    stream, own, other, packed, vectors = results
    normed, chosen, looked = more
    codes, targets, offsets, shard_column, marks = flow(0, 1, 2, 3, 4)
    make_hot(offsets, 0, chosen)
    for line, first, start in ((3, 5, 0), (4, 9, 1024)):
        total = None
        for k in range(4):
            (table,) = flow(first + k)
            spread = hot(codes[...], targets[line : line + 1, 512 * k : 512 * k + 512])
            term = dot(spread, table[...])
            total = term if total is None else total + term
        looked[:, start : start + total.shape[1]] = total.astype(bf16)
    (hidden,) = flow(13)
    heads = flow(14, 15, 16, 17)
    chunk = lax.broadcasted_iota(jnp.int32, (SHARDS, 512), 0)
    row = lax.broadcasted_iota(jnp.int32, (SHARDS, 512), 1)
    lines = None
    for k in range(4):
        term = dot(hot(row + 512 * k, chunk * ROWS + 15), heads[k][...])
        lines = term if lines is None else lines + term
    spread = rows_dot(lines.astype(bf16), hot(shard_column[:, 0:1], marks[0:1, :]))
    within = lax.broadcasted_iota(jnp.int32, (SHARDS, 1), 0)
    group = sum((within >= 15 * r).astype(jnp.int32) for r in range(1, 7))
    spread = jnp.where(within - group * 15 == marks[1:2, :], spread, 0.0).astype(bf16)
    number = lax.broadcasted_iota(jnp.int32, (8, SHARDS), 1)
    first = lax.broadcasted_iota(jnp.int32, (8, SHARDS), 0) * 15
    inside = jnp.where((number >= first) & (number < first + 15), 1.0, 0.0).astype(bf16)
    vectors[...] = dot(inside, spread)
    flow.out(4)
    level_row = jnp.where(level[0] == 0, vectors[4:5, :], vectors[5:6, :])
    token = lax.broadcasted_iota(jnp.int32, (ROW_STEP, 64), 0)
    column = lax.broadcasted_iota(jnp.int32, (ROW_STEP, 64), 1)

    def rows(span):
        four = hot(jnp.right_shift(token + span.start, 2), column)
        value = dot(four, looked[...]) + hidden[span, :].astype(f32) + level_row
        stream[span, :] = value
        centered, scale = moments(value)
        normed[span, :] = (centered * scale * vectors[0:1, :] + vectors[2:3, :]).astype(bf16)

    each_rows(rows)
    flow.out(0)
    normed[...] = dot(row_move(), normed[...]).astype(bf16)
    shuffle(here, chosen, normed, own, other)
    flow.out(1, 2)
    weight = flow(18, 19, 20, 21)
    packed[...] = sum(dot(p, w[:, 0:1440]) for p, w in zip(pieces_of(own, other), weight)).astype(bf16)
    flow.out(3)


def embed(here, level, hidden, codes, targets, offsets, shard_column, marks, tables_a, tables_b, qkv):
    outs = (
        shape(TOKENS, D, f32),
        shape(TOKENS, HALF),
        shape(TOKENS, HALF),
        shape(TOKENS, 1440),
        shape(8, D, f32),
    )
    return flowing(
        embed_body,
        (here, level),
        (codes, targets, offsets, shard_column, marks, *tables_a, *tables_b, hidden, *qkv, *qkv),
        outs,
        [pltpu.VMEM((TOKENS, D), bf16), HOT, pltpu.VMEM((64, D), bf16)],
        8e9,
        {i: (0, 128) for i in (14, 15, 16, 17)},
    )


def probabilities(columns):
    query, key = columns[:, 0:480], columns[:, 480:960]
    row = lax.broadcasted_iota(jnp.int32, (TOKENS, TOKENS), 0)
    other = lax.broadcasted_iota(jnp.int32, (TOKENS, TOKENS), 1)
    mask = ((row & 3) == (other & 3)) & (jnp.right_shift(row, 2) >= jnp.right_shift(other, 2))
    scores = jnp.where(mask, cols_dot(query, key) * HEAD ** (-0.5), -1e30)
    top = jnp.max(scores, axis=-1, keepdims=True)
    total = top + jnp.log(jnp.sum(jnp.exp(scores - top), axis=-1, keepdims=True))
    return jnp.exp(scores - total)


def attend_kernel(columns, mixed):
    mixed[...] = dot(probabilities(columns).astype(bf16), columns[:, 960:1440]).astype(bf16)


def attend(columns):
    out = shape(TOKENS, 480)
    return call(
        attend_kernel, out, grid=(1,), in_specs=[whole(columns)], out_specs=whole(out)
    )(columns)


def attend_back_kernel(columns, d_mixed, d_packed):
    probs = probabilities(columns)
    low = probs.astype(bf16)
    d_probs = cols_dot(d_mixed[...], columns[:, 960:1440])
    d_scores = (probs * (d_probs - jnp.sum(probs * d_probs, axis=-1, keepdims=True))).astype(bf16)
    scale = HEAD ** (-0.5)
    d_packed[:, 0:480] = (dot(d_scores, columns[:, 480:960]) * scale).astype(bf16)
    d_packed[:, 480:960] = (rows_dot(d_scores, columns[:, 0:480]) * scale).astype(bf16)
    d_packed[:, 960:1440] = rows_dot(low, d_mixed[...]).astype(bf16)
    d_packed[:, 1440:1536] = jnp.zeros((TOKENS, 96), bf16)


def attend_back(columns, d_mixed):
    out = shape(TOKENS, 1536)
    return call(
        attend_back_kernel,
        out,
        grid=(1,),
        in_specs=[whole(columns), whole(d_mixed)],
        out_specs=whole(out),
    )(columns, d_mixed)


WORK = pltpu.VMEM((TOKENS, D), f32)
WIDE = pltpu.VMEM((TOKENS, 2 * HALF), bf16)
LOW = pltpu.VMEM((TOKENS, D), bf16)


def ahead_body(flow, scalars, results, more):
    (here,) = scalars
    (d_active,) = results
    wide, chosen = more
    upstream, offsets = flow(0, 1)
    make_hot(offsets, 2, chosen)
    group_back(2, upstream, flow, 2, wide)
    unshuffle(here, chosen, wide, d_active)
    flow.out(0)


def ahead(here, upstream, offsets, reduce):
    return flowing(
        ahead_body, (here,), (upstream, offsets, *reduce), (shape(TOKENS, D, f32),), [WIDE, HOT], 4e9
    )[0]


def middle_body(flow, scalars, results, more):
    (here,) = scalars
    mixed, mid, second_own, second_other, active_own, active_other = results[:6]
    d_upward, d_mid, attn_own, attn_other, d_mixed, sums = results[6:]
    work, wide, low, *chosen = more
    mixed_columns, offsets = flow(0, 1)
    for order in range(3):
        make_hot(offsets, order, chosen[order])
    mixed[:, 480:512] = jnp.zeros((TOKENS, 32), bf16)
    mixed[:, 0:480] = dot(row_move(True), mixed_columns[...]).astype(bf16)
    flow.out(0)
    end = tail_lanes(mixed[:, 0:480])
    rest, attn = flow(2, 3, 4, 5), flow(6, 7, 8, 9)
    for k in range(4):
        total = cols_dot(mixed[:, 0:384], attn[k][...]) + cols_dot(end, rest[k][...])
        wide[:, 512 * k : 512 * k + 512] = total.astype(bf16)
    unshuffle(here, chosen[0], wide, work)
    stream, vectors = flow(10, 11)

    def rows_first(span):
        value = stream[span, :] + work[span, :]
        mid[span, :] = value
        centered, scale = moments(value)
        low[span, :] = (centered * scale * vectors[1:2, :] + vectors[3:4, :]).astype(bf16)

    each_rows(rows_first)
    flow.out(1)
    shuffle(here, chosen[1], low, second_own, second_other)
    flow.out(2, 3)
    expand = flow(12, 13, 14, 15)

    def up(span):
        work[:, span] = group_sum(1, second_own, second_other, expand, span)

    each_chunk(D, up)
    (d_active,) = flow(16)

    def rows_active(span):
        value = work[span, :]
        root = np.float32(np.sqrt(2 / np.pi))
        square = value * value
        bend = jnp.tanh(value * (root + np.float32(root * 0.044715) * square))
        half = 0.5 * value
        low[span, :] = (half + half * bend).astype(bf16)
        inner = root + np.float32(3 * root * 0.044715) * square
        slope = 0.5 + 0.5 * bend + (half * inner) * (1.0 - bend * bend)
        d_upward[span, :] = (slope * d_active[span, :]).astype(bf16)

    each_rows(rows_active)
    flow.out(6)
    shuffle(here, chosen[2], low, active_own, active_other)
    flow.out(4, 5)
    for half in range(2):
        for group in range(4):
            term = cols_dot(d_upward[...], group_rows(1, expand, half, group))
            wide[:, slot(group + 4 * half)] = term.astype(bf16)
    unshuffle(here, chosen[1], wide, work)
    (upstream,) = flow(17)
    sums[...] = jnp.zeros(sums.shape, f32)

    def rows_back(span):
        base = upstream[span, :].astype(f32)
        grad = work[span, :]
        value, gain_part = norm_back(mid[span, :], grad, vectors[1:2, :], base)
        d_mid[span, :] = value
        low[span, :] = value.astype(bf16)
        sums[0:1, :] += jnp.sum(gain_part, axis=0, keepdims=True)
        sums[1:2, :] += jnp.sum(grad, axis=0, keepdims=True)

    each_rows(rows_back)
    flow.out(7, 11)
    shuffle(here, chosen[0], low, attn_own, attn_other)
    flow.out(8, 9)
    parts = pieces_of(attn_own, attn_other)
    back = sum(dot(p, w[...]) for p, w in zip(parts, attn)).astype(bf16)
    d_mixed[:, 0:384] = dot(row_move(), back).astype(bf16)
    back = sum(dot(p, w[...]) for p, w in zip(parts, rest)).astype(bf16)
    back = dot(row_move(), back).astype(bf16)
    source = lax.broadcasted_iota(jnp.int32, (256, 128), 0)
    target = lax.broadcasted_iota(jnp.int32, (256, 128), 1)
    d_mixed[:, 384:480] = dot(back, hot(source - 160, target))[:, 0:96].astype(bf16)
    flow.out(10)


def middle(here, mixed_columns, stream, vectors, offsets, d_active, upstream, qkv, attn, expand):
    half = shape(TOKENS, HALF)
    outs = (
        (shape(TOKENS, 512), shape(TOKENS, D, f32))
        + (half,) * 4
        + (shape(TOKENS, D), shape(TOKENS, D, f32), half, half, shape(TOKENS, 480), shape(8, D, f32))
    )
    return flowing(
        middle_body,
        (here,),
        (mixed_columns, offsets, *qkv, *attn, stream, vectors, *expand, d_active, upstream),
        outs,
        [WORK, WIDE, LOW, HOT, HOT, HOT],
        12e9,
        {i: (1280, 1536) for i in (2, 3, 4, 5)},
    )


def down_body(flow, scalars, results, more):
    (block_out,) = results
    active_own, active_other = flow(0, 1)
    reduce = flow(2, 3, 4, 5)
    (mid,) = flow(6)

    def down(span):
        total = group_sum(2, active_own, active_other, reduce, span)
        block_out[:, span] = (mid[:, span] + total).astype(bf16)

    each_chunk(D, down)
    flow.out(0)


def down(mid, active_own, active_other, reduce):
    return flowing(
        down_body, (), (active_own, active_other, *reduce, mid), (shape(TOKENS, D),), [], 4e9
    )[0]


def last_body(flow, scalars, results, more):
    here, level = scalars
    d_stream, sums_out, small = results
    work, wide, totals, chosen, low = more
    d_packed, offsets = flow(0, 1)
    make_hot(offsets, 0, chosen)
    moved = dot(row_move(True), d_packed[:, 0:1440]).astype(bf16)
    for k in range(4):
        (weight,) = flow(2 + k)
        wide[:, 512 * k : 512 * k + 512] = cols_dot(moved, weight[:, 0:1440]).astype(bf16)
    unshuffle(here, chosen, wide, work)
    totals[...] = jnp.zeros(totals.shape, f32)
    stream, d_mid, vectors, sums, shard_column, marks, codes = flow(6, 7, 8, 9, 10, 11, 12)

    def rows(span):
        grad = work[span, :]
        value, gain_part = norm_back(stream[span, :], grad, vectors[0:1, :], d_mid[span, :])
        d_stream[span, :] = value
        low[span, :] = value.astype(bf16)
        totals[0:1, :] += jnp.sum(gain_part, axis=0, keepdims=True)
        totals[2:3, :] += jnp.sum(grad, axis=0, keepdims=True)
        totals[6:7, :] += jnp.sum(value, axis=0, keepdims=True)

    each_rows(rows)
    flow.out(0)
    row = lax.broadcasted_iota(jnp.int32, (64, TOKENS), 0)
    token = lax.broadcasted_iota(jnp.int32, (64, TOKENS), 1)
    every = hot(row, jnp.right_shift(token, 2))
    sums_out[:, 0:1024] = dot(every, low[:, 0:1024]).astype(bf16)
    sums_out[:, 1152:2048] = dot(every, low[:, 1024:1920]).astype(bf16)
    lane = lax.broadcasted_iota(jnp.int32, (64, 128), 1)
    code = codes[...]
    code = jnp.where(lane == 0, jnp.right_shift(code, 4), jnp.where(lane == 1, code & 15, 0))
    code = code.astype(f32).astype(bf16)
    sums_out[:, 1024:1152] = code
    sums_out[:, 2048:2176] = code
    totals[1:2, :] = sums[0:1, :]
    totals[3:4, :] = sums[1:2, :]
    totals[4:5, :] = jnp.where(level[0] == 0, totals[6:7, :], 0.0)
    totals[5:6, :] = jnp.where(level[0] == 1, totals[6:7, :], 0.0)
    number = lax.broadcasted_iota(jnp.int32, (SHARDS, 8), 0)
    first = lax.broadcasted_iota(jnp.int32, (SHARDS, 8), 1) * 15
    inside = jnp.where((number >= first) & (number < first + 15) & (number < 90), 1.0, 0.0)
    repeated = dot(inside.astype(bf16), totals[...].astype(bf16))
    within = lax.broadcasted_iota(jnp.int32, (SHARDS, 1), 0)
    group = sum((within >= 15 * r).astype(jnp.int32) for r in range(1, 7))
    repeated = jnp.where(within - group * 15 == marks[1:2, :], repeated, 0.0).astype(bf16)
    spread = cols_dot(hot(shard_column[:, 2:3], marks[0:1, :]), repeated).astype(bf16)
    small[...] = spread[0:64]
    sums_out[:, 2176:2304] = spread[64:128]
    flow.out(1, 2)


def last(here, level, d_packed, stream, d_mid, vectors, sums, offsets, shard_column, marks, codes, qkv):
    outs = (shape(TOKENS, D, f32), shape(64, 2304), shape(64, 128))
    return flowing(
        last_body,
        (here, level),
        (d_packed, offsets, *qkv, stream, d_mid, vectors, sums, shard_column, marks, codes),
        outs,
        [WORK, WIDE, pltpu.VMEM((8, D), f32), HOT, LOW],
        60e9,
    )


def finish_kernel(kept0, got0, kept1, got1, kept2, got2, *outs):
    grad_qkv, grad_attn, grad_expand, grad_reduce, table, levels, gains, shifts = outs

    def total(kept, got, start, stop):
        return kept[:, start:stop].astype(f32) + got[:, start:stop].astype(f32)

    grad_attn[...] = total(kept0, got0, 0, 480)[:15]
    grad_qkv[...] = total(kept0, got0, 512, 1952)[:15]
    grad_expand[...] = total(kept1, got1, 0, 1920)[:15]
    table[:, 0:1024] = total(kept1, got1, 1920, 2944)
    grad_reduce[...] = total(kept2, got2, 0, 1920)[:15]
    table[:, 1024:1920] = total(kept2, got2, 1920, 2816)
    line = total(kept2, got2, 2816, 2944)[0:1]
    for target, first in ((gains, 0), (shifts, 2), (levels, 4)):
        for row in range(2):
            start = (first + row) * 15
            target[row : row + 1, :] = line[:, start : start + 15]


def finish(*pairs):
    outs = tuple(
        shape(*s, f32)
        for s in ((15, 1440), (15, 480), (15, D), (15, D), (16, D), (2, 15), (2, 15), (2, 15))
    )
    return call(
        finish_kernel,
        outs,
        grid=(1,),
        in_specs=[whole(v) for v in pairs],
        out_specs=outs_whole(outs),
    )(*pairs)


def body(
    hidden_in,
    cond_codes,
    level_ids,
    qkv_weight,
    attn_out_weight,
    mlp_in_weight,
    mlp_out_weight,
    code_table,
    level_table,
    norm_gain,
    norm_bias,
    grad_out,
):
    yl, co, yh, z, x = (lax.axis_index(name) for name in AXES)
    me = yl * 64 + co * 32 + yh * 16 + z * 4 + x
    here = jnp.stack((me, co))
    *shards, targets, offsets, shard_column, codes = prepare(
        qkv_weight,
        attn_out_weight.T,
        mlp_in_weight,
        mlp_out_weight,
        code_table,
        norm_gain,
        norm_bias,
        level_table,
        cond_codes,
    )
    feature = np.arange(D, dtype=np.int32)
    marks = jnp.asarray(np.stack((feature // 15, feature % 15)))

    def exchanged(values, step):
        return [exchange(v, order, step) for v, order in zip(values, ORDERS)]

    def singles(lists):
        return [v for (v,) in lists]

    small = singles(join(shards, exchanged(shards, 0)))
    for step in (1, 2):
        small = singles(join(small, exchanged(small, step)))
    cuts = [((0, split), (split, v.shape[1])) for v, split in zip(small, SPLITS)]
    small = join(small, exchanged(small, 3), cuts)
    first, second = [v for v, _ in small], [v for _, v in small]
    first = singles(join(first, exchanged(first, 4)))
    first, second = lax.optimization_barrier((first, second))
    rests = exchanged(first, 5)
    second_got = exchanged(second, 4)
    pieces = [(h, r, swap_cores(h), swap_cores(r)) for h, r in zip(first, rests)]
    second = singles(join(second, second_got))
    pieces, second = lax.optimization_barrier((pieces, second))
    qkv, table_a, table_b = pieces
    rests = exchanged(second, 5)

    stream, first_own, first_other, packed, vectors = embed(
        here, level_ids, hidden_in[0], codes, targets, offsets, shard_column, marks, table_a, table_b, qkv
    )

    def over_blocks(value):
        return lax.all_to_all(value, BLK, split_axis=0, concat_axis=0, tiled=True)

    columns = over_blocks(packed)
    mixed = attend(columns)
    mixed, rests = lax.optimization_barrier((mixed, rests))
    mixed = over_blocks(mixed)
    attn, expand, reduce = [(h, r, swap_cores(h), swap_cores(r)) for h, r in zip(second, rests)]
    upstream = grad_out[0]
    upstream_got = swap_cores(upstream)
    d_active = ahead(here, upstream, offsets, reduce)
    mixed, d_active = lax.optimization_barrier((mixed, d_active))
    (
        mixed,
        mid,
        second_own,
        second_other,
        active_own,
        active_other,
        d_upward,
        d_mid,
        attn_own,
        attn_other,
        d_mixed,
        sums,
    ) = middle(here, mixed, stream, vectors, offsets, d_active, upstream, qkv, attn, expand)
    swapped = [swap_cores(v) for v in (active_other, second_other, d_upward, attn_other, mixed)]
    d_mixed = over_blocks(d_mixed)
    block_out = down(mid, active_own, active_other, reduce)
    d_mixed, block_out = lax.optimization_barrier((d_mixed, block_out))
    d_packed = attend_back(columns, d_mixed)
    d_packed, active_own, second_own, swapped = lax.optimization_barrier(
        (d_packed, active_own, second_own, swapped)
    )
    active_got, second_got, d_upward_got, attn_got, mixed_got = swapped
    d_packed = over_blocks(d_packed)
    reduce_grad = outer(2, active_own, active_got, upstream, upstream_got)
    reduce_got = exchange(reduce_grad[1], ORDERS[2], 5)
    expand_grad = outer(1, second_own, second_got, d_upward, d_upward_got)
    expand_got = exchange(expand_grad[1], ORDERS[1], 5)
    d_packed, reduce_grad, expand_grad = lax.optimization_barrier((d_packed, reduce_grad, expand_grad))
    first_got = swap_cores(first_other)

    qkv_grad = outer_pair(
        (attn_own, attn_got, mixed, mixed_got),
        (first_own, first_got, d_packed, swap_cores(d_packed)),
    )
    qkv_got = exchange(qkv_grad[1], ORDERS[0], 5)
    d_packed, qkv_grad = lax.optimization_barrier((d_packed, qkv_grad))

    d_stream, code_sums, small = last(
        here, level_ids, d_packed, stream, d_mid, vectors, sums, offsets, shard_column, marks, codes, qkv
    )
    outs = (shape(128, 1152), shape(160, 1024), shape(32, 128))
    rows_a, rows_b, small = simple(spread_kernel, outs, code_sums, swap_cores(code_sums), small)
    got_a, got_b = exchange(rows_a, ORDERS[1], 5), exchange(rows_b, ORDERS[2], 5)
    early = add_halves([[(expand_grad[0], expand_got)], [(reduce_grad[0], reduce_got)]])
    early_got = [exchange(sent, order, 4) for (_, sent), order in zip(early, ORDERS[1:])]
    got_a, got_b, early = lax.optimization_barrier((got_a, got_b, early))
    outs = (shape(256, 1152), shape(272, 1024), shape(16, 128))
    rows_a, rows_b, small = simple(widen_kernel, outs, rows_a, got_a, rows_b, got_b, small)
    got_a, got_b = exchange(rows_a, ORDERS[1], 4), exchange(rows_b, ORDERS[2], 4)
    qkv_got, _ = lax.optimization_barrier((qkv_got, (rows_a, rows_b)))
    (first_sums,) = add_halves([[(qkv_grad[0], qkv_got)]])
    first_got = exchange(first_sums[1], ORDERS[0], 4)
    outs = (shape(256, 1024), shape(256, 1024))
    grad_a, grad_b = simple(
        place_kernel, outs, rows_a, got_a, rows_b, got_b, small, targets, flops=1e9
    )
    sums = add_halves(
        [
            [(first_sums[0], first_got)],
            [(early[0][0], early_got[0]), (grad_a, None)],
            [(early[1][0], early_got[1]), (grad_b, None)],
        ]
    )
    for step in (3, 2, 1):
        got = exchanged([sent for _, sent in sums], step)
        sums = add_halves([[(kept, v)] for (kept, _), v in zip(sums, got)])
    got = exchanged([sent for _, sent in sums], 0)
    pairs = [v for (kept, _), mine in zip(sums, got) for v in (kept, mine)]
    grad_qkv, grad_attn, grad_expand, grad_reduce, grad_table, levels, gains, shifts = finish(*pairs)
    return (
        block_out[None],
        d_stream[None],
        grad_qkv,
        grad_attn.T,
        grad_expand,
        grad_reduce,
        grad_table,
        levels,
        gains,
        shifts,
    )


def solution(mesh):
    fine = Mesh(mesh.devices.reshape(2, 2, 2, 4, 4), AXES)
    return jax.shard_map(
        body,
        mesh=fine,
        in_specs=(
            P(WIN, BLK, None),
            P(WIN, BLK),
            P(WIN),
            P(AXES, None),
            P(None, AXES),
            P(AXES, None),
            P(AXES, None),
            P(AXES, None),
            P(None, AXES),
            P(None, AXES),
            P(None, AXES),
            P(WIN, BLK, None),
        ),
        out_specs=(
            P(WIN, BLK, None),
            P(WIN, BLK, None),
            P(AXES, None),
            P(None, AXES),
            P(AXES, None),
            P(AXES, None),
            P(AXES, None),
            P(None, AXES),
            P(None, AXES),
            P(None, AXES),
        ),
        check_vma=False,
    )
```
